256 devices in a mesh: space: 32 (over z, y), chan: 8 (over x, core).
Axes of the slice: x: 4, y: 4, z: 8, core: 2. Of those that a mesh axis runs over, the one named last changes fastest.
Arguments:
- feature_map: bfloat16 [128, 224, 1280], P('space', None, 'chan'), may hold values from -6 to 6
- conv_kernel: bfloat16 [9, 32, 1280], P(None, None, 'chan'), may hold values from -0.375 to 0.375
- weight_in: bfloat16 [1280, 5120], P(None, 'chan'), may hold values from -0.15625 to 0.15625
- weight_out: bfloat16 [5120, 1280], P('chan'), may hold values from -0.078125 to 0.078125
- cotangent: bfloat16 [128, 224, 1280], P('space', None, 'chan'), may hold values from -6 to 6
Outputs:
- block_out: bfloat16 [128, 224, 1280], P('space', None, 'chan')
- grad_features: bfloat16 [128, 224, 1280], P('space', None, 'chan')
- grad_kernel: float32 [9, 32, 1280], P(None, None, 'chan')
- grad_weight_in: float32 [1280, 5120], P(None, 'chan')
- grad_weight_out: float32 [5120, 1280], P('chan')
The draws below stay inside these ranges and needn't reach their ends.
All inputs are finite; a program needn't handle non-finite values.
Results may differ from the reference program's by a relative error of at most 0.019.
Values may be sent and summed in bfloat16 or wider, within the bound.
A program may use at most 192 MiB of HBM per device.

```python
import math
import jax
import jax.numpy as jnp
from jax import lax

C = 1280
FF = 5120
GROUPS = 40
WIDTH = 224
HEIGHT = 128
N_CHAN = 8


def levels(key, shape, cuts, low, largest):
    def one(axis_at, shards_of):
        heights = jax.random.uniform(jax.random.fold_in(jax.random.fold_in(key, 6), axis_at), (shards_of,), jnp.float32, low / len(cuts), largest / len(cuts))
        return jnp.repeat(jnp.exp(heights), shape[axis_at] // shards_of).reshape((-1,) + (1,) * (len(shape) - axis_at - 1))

    level = one(*cuts[0])
    for cut in cuts[1:]:
        level = level * one(*cut)
    return level


def noise(own_key, extent, width, most, cuts=(), kind=jnp.bfloat16):
    level = levels(own_key, extent, cuts, -0.22, 0.18) if cuts else 1.0
    entries = jax.random.normal(own_key, extent, jnp.float32) * width * level
    return jnp.minimum(jnp.maximum(entries, -most), most).astype(kind)


def setup_inputs(seed: int = 0) -> dict:
    keys = jax.random.split(jax.random.key(seed), 6)
    feature_map = noise(keys[0], (HEIGHT, WIDTH, C), 1.0, 6.0, ((0, 32), (2, 8)))
    conv_kernel = noise(keys[1], (9, C // GROUPS, C), (9 * (C // GROUPS)) ** -0.5, 0.375, ((2, 8),))
    weight_in = noise(keys[2], (C, FF), C ** -0.5, 0.15625, ((1, 8),))
    weight_out = noise(keys[3], (FF, C), FF ** -0.5, 0.078125, ((0, 8),))
    cotangent = noise(keys[4], (HEIGHT, WIDTH, C), 1.0, 6.0, ((0, 32), (2, 8)))
    return dict(feature_map=feature_map, conv_kernel=conv_kernel, weight_in=weight_in, weight_out=weight_out, cotangent=cotangent)


def pad_map(field):
    return jnp.pad(field, ((1, 1), (1, 1), (0, 0)))

def group_conv(padded, kernel, row_count, col_count):
    width_group = kernel.shape[1]
    channels = kernel.shape[2]
    group_count = channels // width_group
    summed = jnp.zeros((row_count, col_count, group_count, width_group), jnp.float32)
    for tap_index in range(9):
        shift_row, shift_col = (tap_index // 3, tap_index % 3)
        window = padded[shift_row:shift_row + row_count, shift_col:shift_col + col_count]
        window = window.reshape(row_count, col_count, group_count, width_group).astype(jnp.float32)
        taps = kernel[tap_index].reshape(width_group, group_count, width_group).astype(jnp.float32)
        summed = summed + jnp.einsum('hwgj,jgo->hwgo', window, taps)
    return summed.reshape(row_count, col_count, channels)

def group_conv_t(padded, kernel, row_count, col_count):
    width_group = kernel.shape[1]
    channels = kernel.shape[2]
    group_count = channels // width_group
    summed = jnp.zeros((row_count, col_count, group_count, width_group), jnp.float32)
    for tap_index in range(9):
        shift_row, shift_col = (2 - tap_index // 3, 2 - tap_index % 3)
        window = padded[shift_row:shift_row + row_count, shift_col:shift_col + col_count]
        window = window.reshape(row_count, col_count, group_count, width_group).astype(jnp.float32)
        taps = kernel[tap_index].reshape(width_group, group_count, width_group).astype(jnp.float32)
        summed = summed + jnp.einsum('hwgo,jgo->hwgj', window, taps)
    return summed.reshape(row_count, col_count, channels)

def kernel_grad(padded, upstream, width_group, row_count, col_count):
    channels = upstream.shape[2]
    group_count = channels // width_group
    grads = []
    upper = upstream.reshape(row_count, col_count, group_count, width_group).astype(jnp.float32)
    for tap_index in range(9):
        shift_row, shift_col = (tap_index // 3, tap_index % 3)
        window = padded[shift_row:shift_row + row_count, shift_col:shift_col + col_count]
        window = window.reshape(row_count, col_count, group_count, width_group).astype(jnp.float32)
        grads.append(jnp.einsum('hwgj,hwgo->jgo', window, upper).reshape(width_group, channels))
    return jnp.stack(grads, axis=0)

def gelu_slope(values):
    return 0.5 * (1.0 + lax.erf(values / math.sqrt(2.0))) + values * jnp.exp(-0.5 * values * values) / math.sqrt(2.0 * math.pi)

def rounded(values):
    return lax.optimization_barrier(values.astype(jnp.bfloat16)).astype(jnp.float32)

def reference(feature_map, conv_kernel, weight_in, weight_out, cotangent):
    row_count, col_count, channels = feature_map.shape
    width_group = conv_kernel.shape[1]
    pixels = row_count * col_count
    block_hidden = FF // N_CHAN
    grad_scale = 1.0 / math.sqrt(pixels)
    padded = pad_map(feature_map)
    mixed = (feature_map.astype(jnp.float32) + group_conv(padded, conv_kernel, row_count, col_count)).astype(jnp.bfloat16)
    mixed_rows = mixed.reshape(pixels, channels)
    pre = jnp.dot(mixed_rows, weight_in, preferred_element_type=jnp.float32)
    hidden = jax.nn.gelu(pre, approximate=False).astype(jnp.bfloat16)
    mlp = jnp.zeros((pixels, channels), jnp.float32)
    for panel in range(N_CHAN):
        lower = panel * block_hidden
        mlp = mlp + rounded(jnp.dot(hidden[:, lower:lower + block_hidden], weight_out[lower:lower + block_hidden], preferred_element_type=jnp.float32))
    block_out = (mixed_rows.astype(jnp.float32) + mlp).astype(jnp.bfloat16).reshape(row_count, col_count, channels)
    cot_rows = cotangent.reshape(pixels, channels)
    grad_weight_out = jnp.dot(hidden.T, cot_rows, preferred_element_type=jnp.float32) * grad_scale
    dhidden = jnp.dot(cot_rows, weight_out.T, preferred_element_type=jnp.float32)
    dpre = (dhidden * gelu_slope(pre)).astype(jnp.bfloat16)
    grad_weight_in = jnp.dot(mixed_rows.T, dpre, preferred_element_type=jnp.float32) * grad_scale
    dmix = cot_rows.astype(jnp.float32)
    for panel in range(N_CHAN):
        lower = panel * block_hidden
        dmix = dmix + rounded(jnp.dot(dpre[:, lower:lower + block_hidden], weight_in[:, lower:lower + block_hidden].T, preferred_element_type=jnp.float32))
    dmixed = dmix.astype(jnp.bfloat16).reshape(row_count, col_count, channels)
    grad_features = (dmixed.astype(jnp.float32) + group_conv_t(pad_map(dmixed), conv_kernel, row_count, col_count)).astype(jnp.bfloat16)
    grad_kernel = kernel_grad(padded, dmixed, width_group, row_count, col_count) * grad_scale
    return (block_out, grad_features, grad_kernel, grad_weight_in, grad_weight_out)
```

```python
import math

import jax
import jax.numpy as jnp
from jax import lax
from jax.experimental import pallas as pl
from jax.experimental.pallas import tpu as pltpu
from jax.sharding import PartitionSpec as P

MESH = pl.DeviceIdType.MESH
F32 = jnp.float32
BF16 = jnp.bfloat16

NZ, NY, NX = 8, 4, 4
ROWS, COLS, OWN, GROUP = 4, 224, 160, 32
PIX = ROWS * COLS
CH, HID = 1280, 640
LANES = 256
CHUNKS = ((0, 512), (512, 384))
TILES = ((0, 256), (256, 256), (512, 256), (768, 128))
HALVES = ((0, 256), (256, 256), (512, 128))
STREAMS = 5
SROWS = 512
ZFIRST = (True, False, False, False, False)
GK_ROWS = 9 * GROUP
GK_PAD = 384


def dot(a, b, dims):
    return lax.dot_general(a, b, ((dims[:1], dims[1:]), ((), ())), preferred_element_type=F32)


def gelu_slope(values):
    return 0.5 * (1.0 + lax.erf(values * (1.0 / math.sqrt(2.0)))) + values * jnp.exp(
        -0.5 * values * values
    ) * (1.0 / math.sqrt(2.0 * math.pi))


def kernel(
    scale,
    x_ref, ck_ref, wi_hbm, wo_hbm, cot_ref,
    bo_ref, gf_ref, gk_ref, g_hbm,
    xp, dmp, dcat, dense, mixp, wi, wo, wit, wot, cott, mixt, dht, pret, hidt, dpret,
    pb, po, rdb, rdo, psb, pso, rxb, rxo,
    gp, big_r, mid_s, mid_r, fin_s, gks, gkr_y, gk1, gkr_z, gk2,
    lsem, hs, hr, ags, agr, rss, rsr, ars, arr, gss, gsr,
):
    s = lax.axis_index("space")
    c = lax.axis_index("chan")
    z, y, x, k = s // NY, s % NY, c // 2, c % 2
    partner = {"space": s, "chan": 2 * x + 1 - k}
    above = {"space": (s + 31) % 32, "chan": c}
    below = {"space": (s + 1) % 32, "chan": c}

    def xpeer(d):
        return {"space": s, "chan": 2 * ((x + d) % NX) + k}

    def ypeer(d):
        return {"space": z * NY + (y + d) % NY, "chan": c}

    def zpeer(d):
        return {"space": ((z + d) % NZ) * NY + y, "chan": c}

    def send(src, dst, ssem, rsem, dev):
        copy = pltpu.make_async_remote_copy(
            src_ref=src, dst_ref=dst, send_sem=ssem, recv_sem=rsem, device_id=dev, device_id_type=MESH
        )
        copy.start()

    def await_bytes(ref, sem):
        pltpu.make_async_copy(ref, ref, sem).wait()

    def rows(block):
        return pl.ds(pl.multiple_of(block * OWN, 32), OWN)

    load_wi = pltpu.make_async_copy(wi_hbm, wi, lsem.at[0])
    load_wo = pltpu.make_async_copy(wo_hbm, wo, lsem.at[1])
    load_wi.start()
    load_wo.start()
    barrier = pltpu.get_barrier_semaphore()
    peers = [partner, above, below]
    peers += [xpeer(d) for d in range(1, NX)]
    peers += [ypeer(d) for d in range(1, NY)]
    peers += [zpeer(d) for d in range(1, NZ)]
    for dev in peers:
        pl.semaphore_signal(barrier, inc=1, device_id=dev, device_id_type=MESH)

    for h in range(ROWS):
        xp[COLS * (h + 1) : COLS * (h + 2), OWN:LANES] = jnp.zeros((COLS, LANES - OWN), BF16)
        xp[COLS * (h + 1) : COLS * (h + 2), 0:OWN] = x_ref[h]
    cot_rows = cot_ref[...].reshape(PIX, OWN)
    for p in range(PIX // 128):
        block = cot_rows[128 * p : 128 * p + 128].astype(F32).T
        cott[rows(c), 128 * p : 128 * p + 128] = block.astype(BF16)

    pl.semaphore_wait(barrier, len(peers))

    send(xp.at[pl.ds(COLS * ROWS, COLS)], xp.at[pl.ds(0, COLS)], hs.at[0], hr.at[0], below)
    send(xp.at[pl.ds(COLS, COLS)], xp.at[pl.ds(COLS * (ROWS + 1), COLS)], hs.at[1], hr.at[1], above)

    def gather_send(buf, which, part):
        lanes = pl.ds(CHUNKS[part][0], CHUNKS[part][1])
        own = buf.at[rows(c), lanes]
        for d in (2, 1, 3):
            send(own, own, ags.at[which, part, d - 1], agr.at[which, part, d - 1], xpeer(d))
        send(own, own, ags.at[which, part, 3], agr.at[which, part, 3], partner)

    def gather_forward(buf, which, part):
        lanes = pl.ds(CHUNKS[part][0], CHUNKS[part][1])
        for d in (1, 3, 2):
            got = buf.at[rows(2 * ((x + NX - d) % NX) + k), lanes]
            await_bytes(got, agr.at[which, part, d - 1])
            send(got, got, ags.at[which, part, 3 + d], agr.at[which, part, 3 + d], partner)

    def gather_wait(buf, which, part):
        lanes = pl.ds(CHUNKS[part][0], CHUNKS[part][1])
        for d in (0, 1, 3, 2):
            got = buf.at[rows(2 * ((x + NX - d) % NX) + 1 - k), lanes]
            await_bytes(got, agr.at[which, part, 3 + d])

    def gather_done(buf, which):
        for part in range(2):
            lanes = pl.ds(CHUNKS[part][0], CHUNKS[part][1])
            for i in range(7):
                await_bytes(buf.at[pl.ds(0, OWN), lanes], ags.at[which, part, i])

    gather_send(cott, 0, 0)
    gather_send(cott, 0, 1)

    row_group = lax.broadcasted_iota(jnp.int32, (OWN, OWN), 0) // GROUP
    col_group = lax.broadcasted_iota(jnp.int32, (OWN, OWN), 1) // GROUP
    same = row_group == col_group
    dense[...] = jnp.zeros_like(dense)
    for t in range(9):
        tap = ck_ref[t].astype(F32)
        full = jnp.where(same, jnp.concatenate([tap] * (OWN // GROUP), axis=0), 0.0)
        dense[t // 3, 0:OWN, LANES * (t % 3) : LANES * (t % 3) + OWN] = full.astype(BF16)

    column = lax.broadcasted_iota(jnp.int32, (COLS, LANES), 0)

    def later(v):
        return jnp.where(column == 0, 0.0, pltpu.roll(v, 1, 0))

    def earlier(v):
        return jnp.where(column == COLS - 1, 0.0, pltpu.roll(v, COLS - 1, 0))

    def edges(buf, which):
        await_bytes(buf.at[pl.ds(0, COLS)], hr.at[which])
        await_bytes(buf.at[pl.ds(0, COLS)], hr.at[which + 1])
        top = buf[0:COLS].astype(F32)
        buf[0:COLS] = jnp.where(s > 0, top, 0.0).astype(BF16)
        end = buf[COLS * (ROWS + 1) : COLS * (ROWS + 2)].astype(F32)
        buf[COLS * (ROWS + 1) : COLS * (ROWS + 2)] = jnp.where(s < 31, end, 0.0).astype(BF16)

    edges(xp, 0)

    def conv_row(h, carry):
        base = pl.multiple_of(h * COLS, COLS)
        total = dot(xp[pl.ds(base, COLS)], dense[0], (1, 0))
        total += dot(xp[pl.ds(base + COLS, COLS)], dense[1], (1, 0))
        total += dot(xp[pl.ds(base + 2 * COLS, COLS)], dense[2], (1, 0))
        out = later(total[:, 0:LANES]) + total[:, LANES : 2 * LANES] + earlier(total[:, 2 * LANES :])
        mixp[pl.ds(base, COLS)] = (xp[pl.ds(base + COLS, COLS)].astype(F32) + out).astype(BF16)
        return carry

    lax.fori_loop(0, ROWS, conv_row, 0)
    for p in range(PIX // 128):
        block = mixp[128 * p : 128 * p + 128].astype(F32).T
        mixt[rows(c), 128 * p : 128 * p + 128] = block[0:OWN].astype(BF16)
        if p == 3:
            gather_send(mixt, 1, 0)
    gather_send(mixt, 1, 1)

    load_wi.wait()
    load_wo.wait()

    def turn_in(i, carry):
        r = pl.multiple_of(i * 128, 128)
        wit[:, pl.ds(r, 128)] = wi[pl.ds(r, 128), :].astype(F32).T.astype(BF16)
        return carry

    def turn_out(i, carry):
        r = pl.multiple_of(i * 128, 128)
        wot[:, pl.ds(r, 128)] = wo[pl.ds(r, 128), :].astype(F32).T.astype(BF16)
        return carry

    lax.fori_loop(0, CH // 128, turn_in, 0)
    gather_forward(cott, 0, 0)
    gather_forward(cott, 0, 1)
    lax.fori_loop(0, HID // 128, turn_out, 0)
    gather_wait(cott, 0, 0)
    gather_wait(cott, 0, 1)
    for n, w in TILES:
        dht[:, n : n + w] = dot(wo[...], cott[:, n : n + w], (1, 0))

    gather_forward(mixt, 1, 0)
    gather_forward(mixt, 1, 1)
    for part in range(2):
        gather_wait(mixt, 1, part)
        first, width = CHUNKS[part]
        for n, w in TILES:
            if first <= n < first + width:
                pret[:, n : n + w] = dot(wit[...], mixt[:, n : n + w], (1, 0))

        def unit(i, carry, first=first, width=width):
            r = pl.ds(pl.multiple_of(i * 16, 16), 16)
            pre = pret[r, first : first + width]
            upper = 0.5 * (1.0 + lax.erf(pre * (1.0 / math.sqrt(2.0))))
            bell = jnp.exp(-0.5 * pre * pre) * (1.0 / math.sqrt(2.0 * math.pi))
            hidt[r, first : first + width] = (pre * upper).astype(BF16)
            slope = upper + pre * bell
            dpret[r, first : first + width] = (dht[r, first : first + width] * slope).astype(BF16)
            return carry

        lax.fori_loop(0, HID // 16, unit, 0)

    def pair_send(buf, got, which):
        for d in (1, 2, 3, 0):
            block = 2 * ((x + d) % NX) + 1 - k
            send(buf.at[rows(block)], got.at[d], rss.at[which, d], rsr.at[which, d], partner)

    def pair_sum(buf, got, out, landed, which):
        for d in (2, 1, 3, 0):
            await_bytes(got.at[d], rsr.at[which, d])
            if d:
                block = 2 * ((x + d) % NX) + k
                out[d - 1] = (buf[rows(block)].astype(F32) + got[d].astype(F32)).astype(BF16)
                send(out.at[d - 1], landed.at[d - 1], rss.at[which, 3 + d], rsr.at[which, 3 + d], xpeer(d))

    def chan_wait(landed, which):
        for d in range(1, NX):
            await_bytes(landed.at[d - 1], rsr.at[which, 3 + d])

    def chan_sum(buf, got, landed, lanes):
        total = buf[rows(c), lanes].astype(F32) + got[0, :, lanes].astype(F32)
        for d in range(1, NX):
            total = total + landed[d - 1, :, lanes].astype(F32)
        return total

    def pair_done(got, which):
        for i in range(7):
            await_bytes(got.at[0], rss.at[which, i])

    def start(i):
        base = SROWS * i
        if ZFIRST[i]:
            n, per, peer, me = NZ, SROWS // NZ, zpeer, z
        else:
            n, per, peer, me = NY, SROWS // NY, ypeer, y
        return base, n, per, peer, me

    def stream_rs1(i):
        base, n, per, peer, me = start(i)
        for d in range(1, n):
            there = pl.multiple_of(base + per * ((me + d) % n), 64)
            send(
                gp.at[pl.ds(there, per)], big_r.at[i, pl.ds(per * (d - 1), per)],
                ars.at[i, 0], arr.at[i, 0], peer(d),
            )

    def second(i):
        if ZFIRST[i]:
            return NY, ypeer, y
        return NZ, zpeer, z

    def stream_rs2(i):
        base, n, per, peer, me = start(i)
        await_bytes(big_r.at[i, pl.ds(0, per * (n - 1))], arr.at[i, 0])
        mine = pl.ds(pl.multiple_of(base + per * me, 64), per)
        total = gp[mine].astype(F32)
        for d in range(1, n):
            total = total + big_r[i, per * (d - 1) : per * d].astype(F32)
        mid_s[i, 0:per] = total.astype(BF16)
        n2, peer2, me2 = second(i)
        for d in range(1, n2):
            there = pl.multiple_of(16 * ((me2 + d) % n2), 16)
            send(
                mid_s.at[i, pl.ds(there, 16)], mid_r.at[i, pl.ds(16 * (d - 1), 16)],
                ars.at[i, 1], arr.at[i, 1], peer2(d),
            )

    def stream_ag1(i):
        n2, peer2, me2 = second(i)
        await_bytes(mid_r.at[i, pl.ds(0, 16 * (n2 - 1))], arr.at[i, 1])
        mine = pl.ds(pl.multiple_of(16 * me2, 16), 16)
        total = mid_s[i, mine].astype(F32)
        for d in range(1, n2):
            total = total + mid_r[i, 16 * (d - 1) : 16 * d].astype(F32)
        fin_s[i, mine] = total.astype(BF16)
        for d in range(1, n2):
            send(fin_s.at[i, mine], fin_s.at[i, mine], ars.at[i, 2], arr.at[i, 2], peer2(d))

    def stream_ag2(i):
        base, n, per, peer, me = start(i)
        n2, peer2, me2 = second(i)
        await_bytes(fin_s.at[i, pl.ds(0, 16 * (n2 - 1))], arr.at[i, 2])
        mine = g_hbm.at[pl.ds(pl.multiple_of(base + per * me, 64), per)]
        for d in range(1, n):
            send(fin_s.at[i, pl.ds(0, per)], mine, ars.at[i, 3], arr.at[i, 3], peer(d))
        pltpu.make_async_copy(fin_s.at[i, pl.ds(0, per)], mine, lsem.at[2 + i]).start()

    def stream_end(i):
        base, n, per, peer, me = start(i)
        n2, peer2, me2 = second(i)
        big = big_r.at[i, pl.ds(0, per * (n - 1))]
        small = mid_r.at[i, pl.ds(0, 16 * (n2 - 1))]
        await_bytes(g_hbm.at[pl.ds(base, per * (n - 1))], arr.at[i, 3])
        await_bytes(big, ars.at[i, 0])
        await_bytes(small, ars.at[i, 1])
        await_bytes(small, ars.at[i, 2])
        await_bytes(big, ars.at[i, 3])
        await_bytes(fin_s.at[i, pl.ds(0, per)], lsem.at[2 + i])

    for n, w in TILES:
        pb[:, n : n + w] = dot(wi[...], dpret[:, n : n + w], (1, 0)).astype(BF16)
    pair_send(pb, rdb, 0)
    for half in range(2):
        for n, w in HALVES:
            cot_tile = cott[HID * half + n : HID * half + n + w]
            gp[HID * half : HID * half + HID, n : n + w] = dot(hidt[...], cot_tile, (1, 1)).astype(BF16)
    stream_rs1(0)
    stream_rs1(1)
    pair_sum(pb, rdb, psb, rxb, 0)
    for n, w in TILES:
        po[:, n : n + w] = dot(wot[...], hidt[:, n : n + w], (1, 0)).astype(BF16)
    pair_send(po, rdo, 1)
    for n, w in HALVES:
        gp[CH : 2 * CH, n : n + w] = dot(mixt[...], dpret[n : n + w], (1, 1)).astype(BF16)
    stream_rs1(2)
    stream_rs1(3)
    stream_rs1(4)
    pair_sum(po, rdo, pso, rxo, 1)

    chan_wait(rxb, 0)
    dmp[COLS : COLS * (ROWS + 1), OWN:LANES] = jnp.zeros((PIX, LANES - OWN), BF16)
    for p in range(PIX // 128):
        lanes = slice(128 * p, 128 * p + 128)
        total = cott[rows(c), lanes].astype(F32) + chan_sum(pb, rdb, rxb, lanes)
        dmp[COLS + 128 * p : COLS + 128 * p + 128, 0:OWN] = total.T.astype(BF16)
    send(dmp.at[pl.ds(COLS * ROWS, COLS)], dmp.at[pl.ds(0, COLS)], hs.at[2], hr.at[2], below)
    send(dmp.at[pl.ds(COLS, COLS)], dmp.at[pl.ds(COLS * (ROWS + 1), COLS)], hs.at[3], hr.at[3], above)

    for h in range(ROWS):
        v = dmp[COLS * (h + 1) : COLS * (h + 2)].astype(F32)
        dcat[COLS * h : COLS * (h + 1), 0:LANES] = earlier(v).astype(BF16)
        dcat[COLS * h : COLS * (h + 1), LANES : 2 * LANES] = dmp[COLS * (h + 1) : COLS * (h + 2)]
        dcat[COLS * h : COLS * (h + 1), 2 * LANES :] = later(v).astype(BF16)
    lane_group = lax.broadcasted_iota(jnp.int32, (GROUP, LANES), 1) // GROUP
    gks[GK_ROWS:GK_PAD] = jnp.zeros((GK_PAD - GK_ROWS, LANES), BF16)
    for a in range(3):
        full = dot(xp[COLS * a : COLS * a + PIX], dcat[...], (0, 0))
        for b in range(3):
            part = jnp.zeros((GROUP, LANES), F32)
            for g in range(OWN // GROUP):
                piece = full[GROUP * g : GROUP * (g + 1), LANES * b : LANES * (b + 1)]
                part = part + jnp.where(lane_group == g, piece, 0.0)
            gks[GROUP * (3 * a + b) : GROUP * (3 * a + b + 1)] = part.astype(BF16)
    for d in range(1, NY):
        send(gks, gkr_y.at[d - 1], gss.at[0], gsr.at[0], ypeer(d))

    stream_rs2(0)
    stream_rs2(1)

    edges(dmp, 2)

    def back_row(h, carry):
        base = pl.multiple_of(h * COLS, COLS)
        sums = []
        for b in range(3):
            total = None
            for a in range(3):
                u = dmp[pl.ds(base + (2 - a) * COLS, COLS)]
                term = dot(u, dense[a, :, LANES * b : LANES * (b + 1)], (1, 1))
                total = term if total is None else total + term
            sums.append(total)
        out = earlier(sums[0]) + sums[1] + later(sums[2])
        out = out + dmp[pl.ds(base + COLS, COLS)].astype(F32)
        gf_ref[h] = out[:, 0:OWN].astype(BF16)
        return carry

    lax.fori_loop(0, ROWS, back_row, 0)

    stream_rs2(2)
    stream_rs2(3)
    stream_rs2(4)

    await_bytes(gkr_y, gsr.at[0])
    total = gks[...].astype(F32)
    for d in range(1, NY):
        total = total + gkr_y[d - 1].astype(F32)
    gk1[...] = total.astype(BF16)
    per = GK_PAD // NZ
    for d in range(1, NZ):
        there = pl.multiple_of(per * ((z + d) % NZ), 16)
        send(gk1.at[pl.ds(there, per)], gkr_z.at[pl.ds(per * (d - 1), per)], gss.at[1], gsr.at[1], zpeer(d))

    chan_wait(rxo, 1)
    for p in range(PIX // 128):
        lanes = slice(128 * p, 128 * p + 128)
        total = chan_sum(po, rdo, rxo, lanes).T
        total = total + mixp[128 * p : 128 * p + 128, 0:OWN].astype(F32)
        mixp[128 * p : 128 * p + 128, 0:OWN] = total.astype(BF16)
    for h in range(ROWS):
        bo_ref[h] = mixp[COLS * h : COLS * (h + 1), 0:OWN]

    for i in range(STREAMS):
        stream_ag1(i)
        if i == 1:
            await_bytes(gkr_z, gsr.at[1])
            mine = pl.ds(pl.multiple_of(per * z, 16), per)
            total = gk1[mine].astype(F32)
            for d in range(1, NZ):
                total = total + gkr_z[per * (d - 1) : per * d].astype(F32)
            gk2[mine] = total.astype(BF16)
            for d in range(1, NZ):
                send(gk2.at[mine], gk2.at[mine], gss.at[2], gsr.at[2], zpeer(d))
    for i in range(STREAMS):
        stream_ag2(i)

    await_bytes(gk2.at[pl.ds(0, per * (NZ - 1))], gsr.at[2])
    for t in range(9):
        gk_ref[t] = gk2[GROUP * t : GROUP * (t + 1), 0:OWN].astype(F32) * scale

    for i in range(STREAMS):
        stream_end(i)
    gather_done(cott, 0)
    gather_done(mixt, 1)
    pair_done(rdb, 0)
    pair_done(rdo, 1)
    for i in range(4):
        await_bytes(xp.at[pl.ds(0, COLS)], hs.at[i])
    await_bytes(gkr_y, gss.at[0])
    await_bytes(gkr_z, gss.at[1])
    await_bytes(gkr_z, gss.at[2])


def body(feature_map, conv_kernel, weight_in, weight_out, cotangent):
    scale = 1.0 / math.sqrt(ROWS * NZ * NY * COLS)
    vmem = pl.BlockSpec(memory_space=pltpu.VMEM)
    hbm = pl.BlockSpec(memory_space=pl.ANY)

    def run(*refs):
        kernel(scale, *refs)

    per = GK_PAD // NZ
    block_out, grad_features, grad_conv, grads = pl.pallas_call(
        run,
        out_shape=[
            jax.ShapeDtypeStruct((ROWS, COLS, OWN), BF16),
            jax.ShapeDtypeStruct((ROWS, COLS, OWN), BF16),
            jax.ShapeDtypeStruct((9, GROUP, OWN), F32),
            jax.ShapeDtypeStruct((2 * CH, HID), BF16),
        ],
        in_specs=[vmem, vmem, hbm, hbm, vmem],
        out_specs=[vmem, vmem, vmem, hbm],
        scratch_shapes=[
            pltpu.VMEM((COLS * (ROWS + 2), LANES), BF16),
            pltpu.VMEM((COLS * (ROWS + 2), LANES), BF16),
            pltpu.VMEM((PIX, 3 * LANES), BF16),
            pltpu.VMEM((3, LANES, 3 * LANES), BF16),
            pltpu.VMEM((PIX, LANES), BF16),
            pltpu.VMEM((CH, HID), BF16),
            pltpu.VMEM((HID, CH), BF16),
            pltpu.VMEM((HID, CH), BF16),
            pltpu.VMEM((CH, HID), BF16),
            pltpu.VMEM((CH, PIX), BF16),
            pltpu.VMEM((CH, PIX), BF16),
            pltpu.VMEM((HID, PIX), F32),
            pltpu.VMEM((HID, PIX), F32),
            pltpu.VMEM((HID, PIX), BF16),
            pltpu.VMEM((HID, PIX), BF16),
            pltpu.VMEM((CH, PIX), BF16),
            pltpu.VMEM((CH, PIX), BF16),
            pltpu.VMEM((NX, OWN, PIX), BF16),
            pltpu.VMEM((NX, OWN, PIX), BF16),
            pltpu.VMEM((NX - 1, OWN, PIX), BF16),
            pltpu.VMEM((NX - 1, OWN, PIX), BF16),
            pltpu.VMEM((NX - 1, OWN, PIX), BF16),
            pltpu.VMEM((NX - 1, OWN, PIX), BF16),
            pltpu.VMEM((2 * CH, HID), BF16),
            pltpu.VMEM((STREAMS, 448, HID), BF16),
            pltpu.VMEM((STREAMS, 128, HID), BF16),
            pltpu.VMEM((STREAMS, 112, HID), BF16),
            pltpu.VMEM((STREAMS, 128, HID), BF16),
            pltpu.VMEM((GK_PAD, LANES), BF16),
            pltpu.VMEM((NY - 1, GK_PAD, LANES), BF16),
            pltpu.VMEM((GK_PAD, LANES), BF16),
            pltpu.VMEM((per * (NZ - 1), LANES), BF16),
            pltpu.VMEM((GK_PAD, LANES), BF16),
            pltpu.SemaphoreType.DMA((2 + STREAMS,)),
            pltpu.SemaphoreType.DMA((4,)),
            pltpu.SemaphoreType.DMA((4,)),
            pltpu.SemaphoreType.DMA((2, 2, 7)),
            pltpu.SemaphoreType.DMA((2, 2, 7)),
            pltpu.SemaphoreType.DMA((2, 7)),
            pltpu.SemaphoreType.DMA((2, 7)),
            pltpu.SemaphoreType.DMA((STREAMS, 4)),
            pltpu.SemaphoreType.DMA((STREAMS, 4)),
            pltpu.SemaphoreType.DMA((3,)),
            pltpu.SemaphoreType.DMA((3,)),
        ],
        compiler_params=pltpu.CompilerParams(
            collective_id=0, has_side_effects=True, vmem_limit_bytes=60 << 20
        ),
    )(feature_map, conv_kernel, weight_in, weight_out, cotangent)
    grad_in = grads[CH:].astype(F32) * scale
    grad_out = jnp.concatenate([grads[:HID], grads[HID:CH]], axis=1).astype(F32) * scale
    return block_out, grad_features, grad_conv, grad_in, grad_out


def solution(mesh):
    return jax.shard_map(
        body,
        mesh=mesh,
        in_specs=(
            P("space", None, "chan"),
            P(None, None, "chan"),
            P(None, "chan"),
            P("chan", None),
            P("space", None, "chan"),
        ),
        out_specs=(
            P("space", None, "chan"),
            P("space", None, "chan"),
            P(None, None, "chan"),
            P(None, "chan"),
            P("chan", None),
        ),
        check_vma=False,
    )
```

```python
import math

import jax
import jax.numpy as jnp
from jax import lax
from jax.experimental import pallas as pl
from jax.experimental.pallas import tpu as pltpu
from jax.sharding import PartitionSpec as P

MESH = pl.DeviceIdType.MESH
F32 = jnp.float32
BF16 = jnp.bfloat16

NZ, NY, NX = 8, 4, 4
ROWS, COLS, OWN, GROUP = 4, 224, 160, 32
PIX = ROWS * COLS
CH, HID = 1280, 640
LANES = 256
CHUNKS = ((0, 512), (512, 384))
TILES = ((0, 256), (256, 256), (512, 256), (768, 128))
HALVES = ((0, 256), (256, 256), (512, 128))
STREAMS = 5
SROWS = 512
ZFIRST = (True, False, False, False, False)
GK_ROWS = 9 * GROUP
GK_PAD = 384


def dot(a, b, dims):
    return lax.dot_general(a, b, ((dims[:1], dims[1:]), ((), ())), preferred_element_type=F32)


def gelu_slope(values):
    return 0.5 * (1.0 + lax.erf(values * (1.0 / math.sqrt(2.0)))) + values * jnp.exp(
        -0.5 * values * values
    ) * (1.0 / math.sqrt(2.0 * math.pi))


def kernel(
    scale,
    x_ref, ck_ref, wi_hbm, wo_hbm, cot_ref,
    bo_ref, gf_ref, gk_ref, g_hbm,
    xp, hx, dmp, dcat, dense, mixp, wi, wo, wit, wot, cott, mixt, dht, pret, hidt, dpret,
    pb, po, rdb, rdo, psb, pso, rxb, rxo,
    gp, big_r, mid_s, mid_r, fin_s, gks, gkr_y, gk1, gkr_z, gk2,
    lsem, hs, hr, ags, agr, rss, rsr, ars, arr, gss, gsr,
):
    s = lax.axis_index("space")
    c = lax.axis_index("chan")
    z, y, x, k = s // NY, s % NY, c // 2, c % 2
    partner = {"space": s, "chan": 2 * x + 1 - k}
    above = {"space": (s + 31) % 32, "chan": c}
    below = {"space": (s + 1) % 32, "chan": c}

    def xpeer(d):
        return {"space": s, "chan": 2 * ((x + d) % NX) + k}

    def ypeer(d):
        return {"space": z * NY + (y + d) % NY, "chan": c}

    def zpeer(d):
        return {"space": ((z + d) % NZ) * NY + y, "chan": c}

    def send(src, dst, ssem, rsem, dev):
        copy = pltpu.make_async_remote_copy(
            src_ref=src, dst_ref=dst, send_sem=ssem, recv_sem=rsem, device_id=dev, device_id_type=MESH
        )
        copy.start()

    def await_bytes(ref, sem):
        pltpu.make_async_copy(ref, ref, sem).wait()

    def rows(block):
        return pl.ds(pl.multiple_of(block * OWN, 32), OWN)

    load_wi = pltpu.make_async_copy(wi_hbm, wi, lsem.at[0])
    load_wo = pltpu.make_async_copy(wo_hbm, wo, lsem.at[1])
    load_wi.start()
    load_wo.start()
    barrier = pltpu.get_barrier_semaphore()
    peers = [partner, above, below]
    peers += [xpeer(d) for d in range(1, NX)]
    peers += [ypeer(d) for d in range(1, NY)]
    peers += [zpeer(d) for d in range(1, NZ)]
    for dev in peers:
        pl.semaphore_signal(barrier, inc=1, device_id=dev, device_id_type=MESH)

    own_cot = jnp.concatenate([cot_ref[h].astype(F32) for h in range(ROWS)], axis=1)
    cott[rows(c), :] = own_cot.astype(BF16)
    pl.semaphore_wait(barrier, len(peers))

    send(x_ref.at[ROWS - 1], hx.at[0], hs.at[0], hr.at[0], below)
    send(x_ref.at[0], hx.at[1], hs.at[1], hr.at[1], above)

    def gather_send(buf, which, part):
        lanes = pl.ds(CHUNKS[part][0], CHUNKS[part][1])
        own = buf.at[rows(c), lanes]
        for d in (2, 1, 3):
            send(own, own, ags.at[which, part, d - 1], agr.at[which, part, d - 1], xpeer(d))
        send(own, own, ags.at[which, part, 3], agr.at[which, part, 3], partner)

    def gather_forward(buf, which, part):
        lanes = pl.ds(CHUNKS[part][0], CHUNKS[part][1])
        for d in (1, 3, 2):
            got = buf.at[rows(2 * ((x + NX - d) % NX) + k), lanes]
            await_bytes(got, agr.at[which, part, d - 1])
            send(got, got, ags.at[which, part, 3 + d], agr.at[which, part, 3 + d], partner)

    def gather_wait(buf, which, part):
        lanes = pl.ds(CHUNKS[part][0], CHUNKS[part][1])
        for d in (0, 1, 3, 2):
            got = buf.at[rows(2 * ((x + NX - d) % NX) + 1 - k), lanes]
            await_bytes(got, agr.at[which, part, 3 + d])

    def gather_done(buf, which):
        for part in range(2):
            lanes = pl.ds(CHUNKS[part][0], CHUNKS[part][1])
            for i in range(7):
                await_bytes(buf.at[pl.ds(0, OWN), lanes], ags.at[which, part, i])

    gather_send(cott, 0, 0)
    gather_send(cott, 0, 1)

    xp[:, OWN:LANES] = jnp.zeros((COLS * (ROWS + 2), LANES - OWN), BF16)
    for h in range(ROWS):
        xp[COLS * (h + 1) : COLS * (h + 2), 0:OWN] = x_ref[h].astype(F32).T.astype(BF16)

    row_group = lax.broadcasted_iota(jnp.int32, (OWN, OWN), 0) // GROUP
    col_group = lax.broadcasted_iota(jnp.int32, (OWN, OWN), 1) // GROUP
    same = row_group == col_group
    dense[...] = jnp.zeros_like(dense)
    for t in range(9):
        tap = ck_ref[t].astype(F32)
        full = jnp.where(same, jnp.concatenate([tap] * (OWN // GROUP), axis=0), 0.0)
        dense[t // 3, 0:OWN, LANES * (t % 3) : LANES * (t % 3) + OWN] = full.astype(BF16)

    column = lax.broadcasted_iota(jnp.int32, (COLS, LANES), 0)

    def later(v):
        return jnp.where(column == 0, 0.0, pltpu.roll(v, 1, 0))

    def earlier(v):
        return jnp.where(column == COLS - 1, 0.0, pltpu.roll(v, COLS - 1, 0))

    last = NZ * NY - 1
    await_bytes(hx.at[0], hr.at[0])
    xp[0:COLS, 0:OWN] = jnp.where(s > 0, hx[0].astype(F32).T, 0.0).astype(BF16)
    await_bytes(hx.at[1], hr.at[1])
    below_row = jnp.where(s < last, hx[1].astype(F32).T, 0.0)
    xp[COLS * (ROWS + 1) : COLS * (ROWS + 2), 0:OWN] = below_row.astype(BF16)

    def conv_row(h, carry):
        base = pl.multiple_of(h * COLS, COLS)
        total = dot(xp[pl.ds(base, COLS)], dense[0], (1, 0))
        total += dot(xp[pl.ds(base + COLS, COLS)], dense[1], (1, 0))
        total += dot(xp[pl.ds(base + 2 * COLS, COLS)], dense[2], (1, 0))
        out = later(total[:, 0:LANES]) + total[:, LANES : 2 * LANES] + earlier(total[:, 2 * LANES :])
        mixp[pl.ds(base, COLS)] = (xp[pl.ds(base + COLS, COLS)].astype(F32) + out).astype(BF16)
        return carry

    lax.fori_loop(0, ROWS, conv_row, 0)
    for p in range(PIX // 128):
        block = mixp[128 * p : 128 * p + 128].astype(F32).T
        mixt[rows(c), 128 * p : 128 * p + 128] = block[0:OWN].astype(BF16)
        if p == 3:
            gather_send(mixt, 1, 0)
    gather_send(mixt, 1, 1)

    load_wi.wait()
    load_wo.wait()

    def turn_in(i, carry):
        r = pl.multiple_of(i * 128, 128)
        wit[:, pl.ds(r, 128)] = wi[pl.ds(r, 128), :].astype(F32).T.astype(BF16)
        return carry

    def turn_out(i, carry):
        r = pl.multiple_of(i * 128, 128)
        wot[:, pl.ds(r, 128)] = wo[pl.ds(r, 128), :].astype(F32).T.astype(BF16)
        return carry

    lax.fori_loop(0, CH // 128, turn_in, 0)
    gather_forward(cott, 0, 0)
    gather_forward(cott, 0, 1)
    lax.fori_loop(0, HID // 128, turn_out, 0)
    gather_wait(cott, 0, 0)
    gather_wait(cott, 0, 1)
    for n, w in TILES:
        dht[:, n : n + w] = dot(wo[...], cott[:, n : n + w], (1, 0))

    gather_forward(mixt, 1, 0)
    gather_forward(mixt, 1, 1)
    for part in range(2):
        gather_wait(mixt, 1, part)
        first, width = CHUNKS[part]
        for n, w in TILES:
            if first <= n < first + width:
                pret[:, n : n + w] = dot(wit[...], mixt[:, n : n + w], (1, 0))

        def unit(i, carry, first=first, width=width):
            r = pl.ds(pl.multiple_of(i * 16, 16), 16)
            pre = pret[r, first : first + width]
            upper = 0.5 * (1.0 + lax.erf(pre * (1.0 / math.sqrt(2.0))))
            bell = jnp.exp(-0.5 * pre * pre) * (1.0 / math.sqrt(2.0 * math.pi))
            hidt[r, first : first + width] = (pre * upper).astype(BF16)
            slope = upper + pre * bell
            dpret[r, first : first + width] = (dht[r, first : first + width] * slope).astype(BF16)
            return carry

        lax.fori_loop(0, HID // 16, unit, 0)

    def pair_send(buf, got, which):
        for d in (1, 2, 3, 0):
            block = 2 * ((x + d) % NX) + 1 - k
            send(buf.at[rows(block)], got.at[d], rss.at[which, d], rsr.at[which, d], partner)

    def pair_sum(buf, got, out, landed, which):
        for d in (2, 1, 3, 0):
            await_bytes(got.at[d], rsr.at[which, d])
            if d:
                block = 2 * ((x + d) % NX) + k
                out[d - 1] = (buf[rows(block)].astype(F32) + got[d].astype(F32)).astype(BF16)
                send(out.at[d - 1], landed.at[d - 1], rss.at[which, 3 + d], rsr.at[which, 3 + d], xpeer(d))

    def chan_wait(landed, which):
        for d in range(1, NX):
            await_bytes(landed.at[d - 1], rsr.at[which, 3 + d])

    def chan_sum(buf, got, landed, lanes):
        total = buf[rows(c), lanes].astype(F32) + got[0, :, lanes].astype(F32)
        for d in range(1, NX):
            total = total + landed[d - 1, :, lanes].astype(F32)
        return total

    def pair_done(got, which):
        for i in range(7):
            await_bytes(got.at[0], rss.at[which, i])

    def start(i):
        base = SROWS * i
        if ZFIRST[i]:
            n, per, peer, me = NZ, SROWS // NZ, zpeer, z
        else:
            n, per, peer, me = NY, SROWS // NY, ypeer, y
        return base, n, per, peer, me

    def stream_rs1(i):
        base, n, per, peer, me = start(i)
        for d in range(1, n):
            there = pl.multiple_of(base + per * ((me + d) % n), 64)
            send(
                gp.at[pl.ds(there, per)], big_r.at[i, pl.ds(per * (d - 1), per)],
                ars.at[i, 0], arr.at[i, 0], peer(d),
            )

    def second(i):
        if ZFIRST[i]:
            return NY, ypeer, y
        return NZ, zpeer, z

    def stream_rs2(i):
        base, n, per, peer, me = start(i)
        await_bytes(big_r.at[i, pl.ds(0, per * (n - 1))], arr.at[i, 0])
        mine = pl.ds(pl.multiple_of(base + per * me, 64), per)
        total = gp[mine].astype(F32)
        for d in range(1, n):
            total = total + big_r[i, per * (d - 1) : per * d].astype(F32)
        mid_s[i, 0:per] = total.astype(BF16)
        n2, peer2, me2 = second(i)
        for d in range(1, n2):
            there = pl.multiple_of(16 * ((me2 + d) % n2), 16)
            send(
                mid_s.at[i, pl.ds(there, 16)], mid_r.at[i, pl.ds(16 * (d - 1), 16)],
                ars.at[i, 1], arr.at[i, 1], peer2(d),
            )

    def stream_ag1(i):
        n2, peer2, me2 = second(i)
        await_bytes(mid_r.at[i, pl.ds(0, 16 * (n2 - 1))], arr.at[i, 1])
        mine = pl.ds(pl.multiple_of(16 * me2, 16), 16)
        total = mid_s[i, mine].astype(F32)
        for d in range(1, n2):
            total = total + mid_r[i, 16 * (d - 1) : 16 * d].astype(F32)
        fin_s[i, mine] = total.astype(BF16)
        for d in range(1, n2):
            send(fin_s.at[i, mine], fin_s.at[i, mine], ars.at[i, 2], arr.at[i, 2], peer2(d))

    def stream_ag2(i):
        base, n, per, peer, me = start(i)
        n2, peer2, me2 = second(i)
        await_bytes(fin_s.at[i, pl.ds(0, 16 * (n2 - 1))], arr.at[i, 2])
        mine = g_hbm.at[pl.ds(pl.multiple_of(base + per * me, 64), per)]
        for d in range(1, n):
            send(fin_s.at[i, pl.ds(0, per)], mine, ars.at[i, 3], arr.at[i, 3], peer(d))
        pltpu.make_async_copy(fin_s.at[i, pl.ds(0, per)], mine, lsem.at[2 + i]).start()

    def stream_end(i):
        base, n, per, peer, me = start(i)
        n2, peer2, me2 = second(i)
        big = big_r.at[i, pl.ds(0, per * (n - 1))]
        small = mid_r.at[i, pl.ds(0, 16 * (n2 - 1))]
        await_bytes(g_hbm.at[pl.ds(base, per * (n - 1))], arr.at[i, 3])
        await_bytes(big, ars.at[i, 0])
        await_bytes(small, ars.at[i, 1])
        await_bytes(small, ars.at[i, 2])
        await_bytes(big, ars.at[i, 3])
        await_bytes(fin_s.at[i, pl.ds(0, per)], lsem.at[2 + i])

    for half in range(2):
        for n, w in HALVES:
            cot_tile = cott[HID * half + n : HID * half + n + w]
            gp[HID * half : HID * half + HID, n : n + w] = dot(hidt[...], cot_tile, (1, 1)).astype(BF16)
    stream_rs1(1)
    stream_rs1(0)
    for n, w in TILES:
        pb[:, n : n + w] = dot(wi[...], dpret[:, n : n + w], (1, 0)).astype(BF16)
    pair_send(pb, rdb, 0)
    for n, w in HALVES:
        gp[CH : 2 * CH, n : n + w] = dot(mixt[...], dpret[n : n + w], (1, 1)).astype(BF16)
    stream_rs1(2)
    for n, w in TILES:
        po[:, n : n + w] = dot(wot[...], hidt[:, n : n + w], (1, 0)).astype(BF16)
    pair_send(po, rdo, 1)
    pair_sum(pb, rdb, psb, rxb, 0)
    pair_sum(po, rdo, pso, rxo, 1)
    stream_rs2(1)
    stream_rs1(3)
    stream_rs2(0)
    stream_ag1(1)
    stream_rs2(2)
    stream_rs1(4)

    chan_wait(rxb, 0)
    dmp[COLS : COLS * (ROWS + 1), OWN:LANES] = jnp.zeros((PIX, LANES - OWN), BF16)
    for p in range(PIX // 128):
        lanes = slice(128 * p, 128 * p + 128)
        total = cott[rows(c), lanes].astype(F32) + chan_sum(pb, rdb, rxb, lanes)
        dmp[COLS + 128 * p : COLS + 128 * p + 128, 0:OWN] = total.T.astype(BF16)
    send(dmp.at[pl.ds(COLS * ROWS, COLS)], dmp.at[pl.ds(0, COLS)], hs.at[2], hr.at[2], below)
    send(dmp.at[pl.ds(COLS, COLS)], dmp.at[pl.ds(COLS * (ROWS + 1), COLS)], hs.at[3], hr.at[3], above)

    for h in range(ROWS):
        v = dmp[COLS * (h + 1) : COLS * (h + 2)].astype(F32)
        dcat[COLS * h : COLS * (h + 1), 0:LANES] = earlier(v).astype(BF16)
        dcat[COLS * h : COLS * (h + 1), LANES : 2 * LANES] = dmp[COLS * (h + 1) : COLS * (h + 2)]
        dcat[COLS * h : COLS * (h + 1), 2 * LANES :] = later(v).astype(BF16)
    lane_group = lax.broadcasted_iota(jnp.int32, (GROUP, LANES), 1) // GROUP
    gks[GK_ROWS:GK_PAD] = jnp.zeros((GK_PAD - GK_ROWS, LANES), BF16)
    for a in range(3):
        full = dot(xp[COLS * a : COLS * a + PIX], dcat[...], (0, 0))
        for b in range(3):
            part = jnp.zeros((GROUP, LANES), F32)
            for g in range(OWN // GROUP):
                piece = full[GROUP * g : GROUP * (g + 1), LANES * b : LANES * (b + 1)]
                part = part + jnp.where(lane_group == g, piece, 0.0)
            gks[GROUP * (3 * a + b) : GROUP * (3 * a + b + 1)] = part.astype(BF16)
    for d in range(1, NY):
        send(gks, gkr_y.at[d - 1], gss.at[0], gsr.at[0], ypeer(d))

    stream_ag1(0)
    stream_ag2(1)
    stream_ag1(2)
    stream_rs2(3)

    await_bytes(dmp.at[pl.ds(0, COLS)], hr.at[2])
    await_bytes(dmp.at[pl.ds(0, COLS)], hr.at[3])
    top = dmp[0:COLS].astype(F32)
    dmp[0:COLS] = jnp.where(s > 0, top, 0.0).astype(BF16)
    end = dmp[COLS * (ROWS + 1) : COLS * (ROWS + 2)].astype(F32)
    dmp[COLS * (ROWS + 1) : COLS * (ROWS + 2)] = jnp.where(s < last, end, 0.0).astype(BF16)

    def back_row(h, carry):
        base = pl.multiple_of(h * COLS, COLS)
        sums = []
        for b in range(3):
            total = None
            for a in range(3):
                u = dmp[pl.ds(base + (2 - a) * COLS, COLS)]
                term = dot(u, dense[a, :, LANES * b : LANES * (b + 1)], (1, 1))
                total = term if total is None else total + term
            sums.append(total)
        out = earlier(sums[0]) + sums[1] + later(sums[2])
        out = out + dmp[pl.ds(base + COLS, COLS)].astype(F32)
        gf_ref[h] = out.T[0:OWN].astype(BF16)
        return carry

    lax.fori_loop(0, ROWS, back_row, 0)

    stream_ag2(0)
    stream_ag2(2)
    stream_ag1(3)
    stream_rs2(4)

    await_bytes(gkr_y, gsr.at[0])
    total = gks[...].astype(F32)
    for d in range(1, NY):
        total = total + gkr_y[d - 1].astype(F32)
    gk1[...] = total.astype(BF16)
    per = GK_PAD // NZ
    for d in range(1, NZ):
        there = pl.multiple_of(per * ((z + d) % NZ), 16)
        send(gk1.at[pl.ds(there, per)], gkr_z.at[pl.ds(per * (d - 1), per)], gss.at[1], gsr.at[1], zpeer(d))

    stream_ag2(3)
    stream_ag1(4)
    await_bytes(gkr_z, gsr.at[1])
    mine = pl.ds(pl.multiple_of(per * z, 16), per)
    total = gk1[mine].astype(F32)
    for d in range(1, NZ):
        total = total + gkr_z[per * (d - 1) : per * d].astype(F32)
    gk2[mine] = total.astype(BF16)
    for d in range(1, NZ):
        send(gk2.at[mine], gk2.at[mine], gss.at[2], gsr.at[2], zpeer(d))
    stream_ag2(4)

    chan_wait(rxo, 1)
    total = chan_sum(po, rdo, rxo, slice(0, PIX)) + mixt[rows(c), :].astype(F32)
    for h in range(ROWS):
        bo_ref[h] = total[:, COLS * h : COLS * (h + 1)].astype(BF16)

    await_bytes(gk2.at[pl.ds(0, per * (NZ - 1))], gsr.at[2])
    for t in range(9):
        gk_ref[t] = gk2[GROUP * t : GROUP * (t + 1), 0:OWN].astype(F32) * scale

    for i in range(STREAMS):
        stream_end(i)
    gather_done(cott, 0)
    gather_done(mixt, 1)
    pair_done(rdb, 0)
    pair_done(rdo, 1)
    for i in range(2):
        await_bytes(hx.at[i], hs.at[i])
        await_bytes(dmp.at[pl.ds(0, COLS)], hs.at[2 + i])
    await_bytes(gkr_y, gss.at[0])
    await_bytes(gkr_z, gss.at[1])
    await_bytes(gkr_z, gss.at[2])


def finish(
    scale, in_ref, left_ref, right_ref, bo_ref, gf_ref, gk_ref,
    grad_in_ref, grad_out_ref, block_out_ref, features_ref, taps_ref,
):
    block_out_ref[...] = bo_ref[...]
    features_ref[...] = gf_ref[...]
    taps_ref[...] = gk_ref[...]
    grad_in_ref[...] = in_ref[...].astype(F32) * scale
    grad_out_ref[:, 0:HID] = left_ref[...].astype(F32) * scale
    grad_out_ref[:, HID:CH] = right_ref[...].astype(F32) * scale


def turned(cells):
    return jnp.transpose(cells, (0, 2, 1))


def body(feature_map, conv_kernel, weight_in, weight_out, cotangent):
    scale = 1.0 / math.sqrt(ROWS * NZ * NY * COLS)
    vmem = pl.BlockSpec(memory_space=pltpu.VMEM)
    hbm = pl.BlockSpec(memory_space=pl.ANY)

    def run(*refs):
        kernel(scale, *refs)

    per = GK_PAD // NZ
    block_out, grad_features, grad_conv, grads = pl.pallas_call(
        run,
        out_shape=[
            jax.ShapeDtypeStruct((ROWS, OWN, COLS), BF16),
            jax.ShapeDtypeStruct((ROWS, OWN, COLS), BF16),
            jax.ShapeDtypeStruct((9, GROUP, OWN), F32),
            jax.ShapeDtypeStruct((2 * CH, HID), BF16),
        ],
        in_specs=[vmem, vmem, hbm, hbm, vmem],
        out_specs=[vmem, vmem, vmem, hbm],
        scratch_shapes=[
            pltpu.VMEM((COLS * (ROWS + 2), LANES), BF16),
            pltpu.VMEM((2, OWN, COLS), BF16),
            pltpu.VMEM((COLS * (ROWS + 2), LANES), BF16),
            pltpu.VMEM((PIX, 3 * LANES), BF16),
            pltpu.VMEM((3, LANES, 3 * LANES), BF16),
            pltpu.VMEM((PIX, LANES), BF16),
            pltpu.VMEM((CH, HID), BF16),
            pltpu.VMEM((HID, CH), BF16),
            pltpu.VMEM((HID, CH), BF16),
            pltpu.VMEM((CH, HID), BF16),
            pltpu.VMEM((CH, PIX), BF16),
            pltpu.VMEM((CH, PIX), BF16),
            pltpu.VMEM((HID, PIX), F32),
            pltpu.VMEM((HID, PIX), F32),
            pltpu.VMEM((HID, PIX), BF16),
            pltpu.VMEM((HID, PIX), BF16),
            pltpu.VMEM((CH, PIX), BF16),
            pltpu.VMEM((CH, PIX), BF16),
            pltpu.VMEM((NX, OWN, PIX), BF16),
            pltpu.VMEM((NX, OWN, PIX), BF16),
            pltpu.VMEM((NX - 1, OWN, PIX), BF16),
            pltpu.VMEM((NX - 1, OWN, PIX), BF16),
            pltpu.VMEM((NX - 1, OWN, PIX), BF16),
            pltpu.VMEM((NX - 1, OWN, PIX), BF16),
            pltpu.VMEM((2 * CH, HID), BF16),
            pltpu.VMEM((STREAMS, 448, HID), BF16),
            pltpu.VMEM((STREAMS, 128, HID), BF16),
            pltpu.VMEM((STREAMS, 112, HID), BF16),
            pltpu.VMEM((STREAMS, 128, HID), BF16),
            pltpu.VMEM((GK_PAD, LANES), BF16),
            pltpu.VMEM((NY - 1, GK_PAD, LANES), BF16),
            pltpu.VMEM((GK_PAD, LANES), BF16),
            pltpu.VMEM((per * (NZ - 1), LANES), BF16),
            pltpu.VMEM((GK_PAD, LANES), BF16),
            pltpu.SemaphoreType.DMA((2 + STREAMS,)),
            pltpu.SemaphoreType.DMA((4,)),
            pltpu.SemaphoreType.DMA((4,)),
            pltpu.SemaphoreType.DMA((2, 2, 7)),
            pltpu.SemaphoreType.DMA((2, 2, 7)),
            pltpu.SemaphoreType.DMA((2, 7)),
            pltpu.SemaphoreType.DMA((2, 7)),
            pltpu.SemaphoreType.DMA((STREAMS, 4)),
            pltpu.SemaphoreType.DMA((STREAMS, 4)),
            pltpu.SemaphoreType.DMA((3,)),
            pltpu.SemaphoreType.DMA((3,)),
        ],
        compiler_params=pltpu.CompilerParams(
            collective_id=0, has_side_effects=True, vmem_limit_bytes=60 << 20
        ),
    )(turned(feature_map), conv_kernel, weight_in, weight_out, turned(cotangent))
    steps = ROWS
    halves = pl.BlockSpec((HID // steps, HID), lambda i: (i, 0))
    row = pl.BlockSpec((1, OWN, COLS), lambda i: (i, 0, 0))
    taps = pl.BlockSpec((9, GROUP, OWN), lambda i: (0, 0, 0))
    grad_in, grad_out, block_out, grad_features, grad_conv = pl.pallas_call(
        lambda *refs: finish(scale, *refs),
        grid=(steps,),
        out_shape=[
            jax.ShapeDtypeStruct((CH, HID), F32),
            jax.ShapeDtypeStruct((HID, CH), F32),
            jax.ShapeDtypeStruct((ROWS, OWN, COLS), BF16),
            jax.ShapeDtypeStruct((ROWS, OWN, COLS), BF16),
            jax.ShapeDtypeStruct((9, GROUP, OWN), F32),
        ],
        in_specs=[
            pl.BlockSpec((CH // steps, HID), lambda i: (steps + i, 0)),
            halves,
            pl.BlockSpec((HID // steps, HID), lambda i: (steps + i, 0)),
            row, row, taps,
        ],
        out_specs=[
            pl.BlockSpec((CH // steps, HID), lambda i: (i, 0)),
            pl.BlockSpec((HID // steps, CH), lambda i: (i, 0)),
            row, row, taps,
        ],
        compiler_params=pltpu.CompilerParams(vmem_limit_bytes=32 << 20),
    )(grads, grads, grads, block_out, grad_features, grad_conv)
    return turned(block_out), turned(grad_features), grad_conv, grad_in, grad_out


def solution(mesh):
    return jax.shard_map(
        body,
        mesh=mesh,
        in_specs=(
            P("space", None, "chan"),
            P(None, None, "chan"),
            P(None, "chan"),
            P("chan", None),
            P("space", None, "chan"),
        ),
        out_specs=(
            P("space", None, "chan"),
            P("space", None, "chan"),
            P(None, None, "chan"),
            P(None, "chan"),
            P("chan", None),
        ),
        check_vma=False,
    )
```

```python
import math

import jax
import jax.numpy as jnp
from jax import lax
from jax.experimental import pallas as pl
from jax.experimental.pallas import tpu as pltpu
from jax.sharding import PartitionSpec as P

MESH = pl.DeviceIdType.MESH
F32 = jnp.float32
BF16 = jnp.bfloat16

NZ, NY, NX = 8, 4, 4
ROWS, COLS, OWN, GROUP = 4, 224, 160, 32
PIX = ROWS * COLS
CH, HID = 1280, 640
LANES = 256
CHUNKS = ((0, 512), (512, 384))
TILES = ((0, 256), (256, 256), (512, 256), (768, 128))
HALVES = ((0, 256), (256, 256), (512, 128))
STREAMS = 5
SROWS = 512
ZFIRST = (True, False, False, False, False)
GK_ROWS = 9 * GROUP
GK_PAD = 384


def dot(a, b, dims):
    return lax.dot_general(a, b, ((dims[:1], dims[1:]), ((), ())), preferred_element_type=F32)


def gelu_slope(values):
    return 0.5 * (1.0 + lax.erf(values * (1.0 / math.sqrt(2.0)))) + values * jnp.exp(
        -0.5 * values * values
    ) * (1.0 / math.sqrt(2.0 * math.pi))


def kernel(
    scale,
    x_ref, ck_ref, wi_hbm, wo_hbm, cot_ref,
    bo_ref, gf_ref, gk_ref, g_hbm,
    xp, hx, dmp, dcat, dense, mixp, wi, wo, wit, wot, cott, mixt, dht, pret, hidt, dpret,
    pb, po, rdb, rdo, psb, pso, rxb, rxo,
    gp, big_r, mid_s, mid_r, fin_s, gks, gkr_y, gk1, gkr_z, gk2,
    lsem, hs, hr, ags, agr, rss, rsr, ars, arr, gss, gsr,
):
    s = lax.axis_index("space")
    c = lax.axis_index("chan")
    z, y, x, k = s // NY, s % NY, c // 2, c % 2
    partner = {"space": s, "chan": 2 * x + 1 - k}
    above = {"space": (s + 31) % 32, "chan": c}
    below = {"space": (s + 1) % 32, "chan": c}

    def xpeer(d):
        return {"space": s, "chan": 2 * ((x + d) % NX) + k}

    def ypeer(d):
        return {"space": z * NY + (y + d) % NY, "chan": c}

    def zpeer(d):
        return {"space": ((z + d) % NZ) * NY + y, "chan": c}

    def send(src, dst, ssem, rsem, dev):
        copy = pltpu.make_async_remote_copy(
            src_ref=src, dst_ref=dst, send_sem=ssem, recv_sem=rsem, device_id=dev, device_id_type=MESH
        )
        copy.start()

    def await_bytes(ref, sem):
        pltpu.make_async_copy(ref, ref, sem).wait()

    def rows(block):
        return pl.ds(pl.multiple_of(block * OWN, 32), OWN)

    load_wi = pltpu.make_async_copy(wi_hbm, wi, lsem.at[0])
    load_wo = pltpu.make_async_copy(wo_hbm, wo, lsem.at[1])
    load_wi.start()
    load_wo.start()
    barrier = pltpu.get_barrier_semaphore()
    peers = [partner, above, below]
    peers += [xpeer(d) for d in range(1, NX)]
    peers += [ypeer(d) for d in range(1, NY)]
    peers += [zpeer(d) for d in range(1, NZ)]
    for dev in peers:
        pl.semaphore_signal(barrier, inc=1, device_id=dev, device_id_type=MESH)

    own_cot = jnp.concatenate([cot_ref[h].astype(F32) for h in range(ROWS)], axis=1)
    cott[rows(c), :] = own_cot.astype(BF16)
    pl.semaphore_wait(barrier, len(peers))

    send(x_ref.at[ROWS - 1], hx.at[0], hs.at[0], hr.at[0], below)
    send(x_ref.at[0], hx.at[1], hs.at[1], hr.at[1], above)

    def gather_send(buf, which, part):
        lanes = pl.ds(CHUNKS[part][0], CHUNKS[part][1])
        own = buf.at[rows(c), lanes]
        for d in (2, 1, 3):
            send(own, own, ags.at[which, part, d - 1], agr.at[which, part, d - 1], xpeer(d))
        send(own, own, ags.at[which, part, 3], agr.at[which, part, 3], partner)

    def gather_forward(buf, which, part):
        lanes = pl.ds(CHUNKS[part][0], CHUNKS[part][1])
        for d in (1, 3, 2):
            got = buf.at[rows(2 * ((x + NX - d) % NX) + k), lanes]
            await_bytes(got, agr.at[which, part, d - 1])
            send(got, got, ags.at[which, part, 3 + d], agr.at[which, part, 3 + d], partner)

    def gather_wait(buf, which, part):
        lanes = pl.ds(CHUNKS[part][0], CHUNKS[part][1])
        for d in (0, 1, 3, 2):
            got = buf.at[rows(2 * ((x + NX - d) % NX) + 1 - k), lanes]
            await_bytes(got, agr.at[which, part, 3 + d])

    def gather_done(buf, which):
        for part in range(2):
            lanes = pl.ds(CHUNKS[part][0], CHUNKS[part][1])
            for i in range(7):
                await_bytes(buf.at[pl.ds(0, OWN), lanes], ags.at[which, part, i])

    gather_send(cott, 0, 0)
    gather_send(cott, 0, 1)

    xp[:, OWN:LANES] = jnp.zeros((COLS * (ROWS + 2), LANES - OWN), BF16)
    for h in range(ROWS):
        xp[COLS * (h + 1) : COLS * (h + 2), 0:OWN] = x_ref[h].astype(F32).T.astype(BF16)

    row_group = lax.broadcasted_iota(jnp.int32, (OWN, OWN), 0) // GROUP
    col_group = lax.broadcasted_iota(jnp.int32, (OWN, OWN), 1) // GROUP
    same = row_group == col_group
    dense[...] = jnp.zeros_like(dense)
    for t in range(9):
        tap = ck_ref[t].astype(F32)
        full = jnp.where(same, jnp.concatenate([tap] * (OWN // GROUP), axis=0), 0.0)
        dense[t // 3, 0:OWN, LANES * (t % 3) : LANES * (t % 3) + OWN] = full.astype(BF16)

    column = lax.broadcasted_iota(jnp.int32, (COLS, LANES), 0)

    def later(v):
        return jnp.where(column == 0, 0.0, pltpu.roll(v, 1, 0))

    def earlier(v):
        return jnp.where(column == COLS - 1, 0.0, pltpu.roll(v, COLS - 1, 0))

    last = NZ * NY - 1
    await_bytes(hx.at[0], hr.at[0])
    xp[0:COLS, 0:OWN] = jnp.where(s > 0, hx[0].astype(F32).T, 0.0).astype(BF16)
    await_bytes(hx.at[1], hr.at[1])
    below_row = jnp.where(s < last, hx[1].astype(F32).T, 0.0)
    xp[COLS * (ROWS + 1) : COLS * (ROWS + 2), 0:OWN] = below_row.astype(BF16)

    def conv_row(h, carry):
        base = pl.multiple_of(h * COLS, COLS)
        total = dot(xp[pl.ds(base, COLS)], dense[0], (1, 0))
        total += dot(xp[pl.ds(base + COLS, COLS)], dense[1], (1, 0))
        total += dot(xp[pl.ds(base + 2 * COLS, COLS)], dense[2], (1, 0))
        out = later(total[:, 0:LANES]) + total[:, LANES : 2 * LANES] + earlier(total[:, 2 * LANES :])
        mixp[pl.ds(base, COLS)] = (xp[pl.ds(base + COLS, COLS)].astype(F32) + out).astype(BF16)
        return carry

    lax.fori_loop(0, ROWS, conv_row, 0)
    for p in range(PIX // 128):
        block = mixp[128 * p : 128 * p + 128].astype(F32).T
        mixt[rows(c), 128 * p : 128 * p + 128] = block[0:OWN].astype(BF16)
        if p == 3:
            gather_send(mixt, 1, 0)
    gather_send(mixt, 1, 1)

    load_wi.wait()
    load_wo.wait()

    def turn_in(i, carry):
        r = pl.multiple_of(i * 128, 128)
        wit[:, pl.ds(r, 128)] = wi[pl.ds(r, 128), :].astype(F32).T.astype(BF16)
        return carry

    def turn_out(i, carry):
        r = pl.multiple_of(i * 128, 128)
        wot[:, pl.ds(r, 128)] = wo[pl.ds(r, 128), :].astype(F32).T.astype(BF16)
        return carry

    lax.fori_loop(0, CH // 128, turn_in, 0)
    gather_forward(cott, 0, 0)
    gather_forward(cott, 0, 1)
    lax.fori_loop(0, HID // 128, turn_out, 0)
    gather_wait(cott, 0, 0)
    gather_wait(cott, 0, 1)
    for n, w in TILES:
        dht[:, n : n + w] = dot(wo[...], cott[:, n : n + w], (1, 0))

    gather_forward(mixt, 1, 0)
    gather_forward(mixt, 1, 1)
    for part in range(2):
        gather_wait(mixt, 1, part)
        first, width = CHUNKS[part]
        for n, w in TILES:
            if first <= n < first + width:
                pret[:, n : n + w] = dot(wit[...], mixt[:, n : n + w], (1, 0))

        def unit(i, carry, first=first, width=width):
            r = pl.ds(pl.multiple_of(i * 16, 16), 16)
            pre = pret[r, first : first + width]
            upper = 0.5 * (1.0 + lax.erf(pre * (1.0 / math.sqrt(2.0))))
            bell = jnp.exp(-0.5 * pre * pre) * (1.0 / math.sqrt(2.0 * math.pi))
            hidt[r, first : first + width] = (pre * upper).astype(BF16)
            slope = upper + pre * bell
            dpret[r, first : first + width] = (dht[r, first : first + width] * slope).astype(BF16)
            return carry

        lax.fori_loop(0, HID // 16, unit, 0)

    def pair_send(buf, got, which):
        for d in (1, 2, 3, 0):
            block = 2 * ((x + d) % NX) + 1 - k
            send(buf.at[rows(block)], got.at[d], rss.at[which, d], rsr.at[which, d], partner)

    def pair_sum(buf, got, out, landed, which):
        for d in (2, 1, 3, 0):
            await_bytes(got.at[d], rsr.at[which, d])
            if d:
                block = 2 * ((x + d) % NX) + k
                out[d - 1] = (buf[rows(block)].astype(F32) + got[d].astype(F32)).astype(BF16)
                send(out.at[d - 1], landed.at[d - 1], rss.at[which, 3 + d], rsr.at[which, 3 + d], xpeer(d))

    def chan_wait(landed, which):
        for d in range(1, NX):
            await_bytes(landed.at[d - 1], rsr.at[which, 3 + d])

    def chan_sum(buf, got, landed, lanes):
        total = buf[rows(c), lanes].astype(F32) + got[0, :, lanes].astype(F32)
        for d in range(1, NX):
            total = total + landed[d - 1, :, lanes].astype(F32)
        return total

    def pair_done(got, which):
        for i in range(7):
            await_bytes(got.at[0], rss.at[which, i])

    def start(i):
        base = SROWS * i
        if ZFIRST[i]:
            n, per, peer, me = NZ, SROWS // NZ, zpeer, z
        else:
            n, per, peer, me = NY, SROWS // NY, ypeer, y
        return base, n, per, peer, me

    def stream_rs1(i):
        base, n, per, peer, me = start(i)
        for d in range(1, n):
            there = pl.multiple_of(base + per * ((me + d) % n), 64)
            send(
                gp.at[pl.ds(there, per)], big_r.at[i, pl.ds(per * (d - 1), per)],
                ars.at[i, 0], arr.at[i, 0], peer(d),
            )

    def second(i):
        if ZFIRST[i]:
            return NY, ypeer, y
        return NZ, zpeer, z

    def stream_rs2(i):
        base, n, per, peer, me = start(i)
        await_bytes(big_r.at[i, pl.ds(0, per * (n - 1))], arr.at[i, 0])
        mine = pl.ds(pl.multiple_of(base + per * me, 64), per)
        total = gp[mine].astype(F32)
        for d in range(1, n):
            total = total + big_r[i, per * (d - 1) : per * d].astype(F32)
        mid_s[i, 0:per] = total.astype(BF16)
        n2, peer2, me2 = second(i)
        for d in range(1, n2):
            there = pl.multiple_of(16 * ((me2 + d) % n2), 16)
            send(
                mid_s.at[i, pl.ds(there, 16)], mid_r.at[i, pl.ds(16 * (d - 1), 16)],
                ars.at[i, 1], arr.at[i, 1], peer2(d),
            )

    def stream_ag1(i):
        n2, peer2, me2 = second(i)
        await_bytes(mid_r.at[i, pl.ds(0, 16 * (n2 - 1))], arr.at[i, 1])
        mine = pl.ds(pl.multiple_of(16 * me2, 16), 16)
        total = mid_s[i, mine].astype(F32)
        for d in range(1, n2):
            total = total + mid_r[i, 16 * (d - 1) : 16 * d].astype(F32)
        fin_s[i, mine] = total.astype(BF16)
        for d in range(1, n2):
            send(fin_s.at[i, mine], fin_s.at[i, mine], ars.at[i, 2], arr.at[i, 2], peer2(d))

    def stream_ag2(i):
        base, n, per, peer, me = start(i)
        n2, peer2, me2 = second(i)
        await_bytes(fin_s.at[i, pl.ds(0, 16 * (n2 - 1))], arr.at[i, 2])
        mine = g_hbm.at[pl.ds(pl.multiple_of(base + per * me, 64), per)]
        for d in range(1, n):
            send(fin_s.at[i, pl.ds(0, per)], mine, ars.at[i, 3], arr.at[i, 3], peer(d))
        pltpu.make_async_copy(fin_s.at[i, pl.ds(0, per)], mine, lsem.at[2 + i]).start()

    def stream_end(i):
        base, n, per, peer, me = start(i)
        n2, peer2, me2 = second(i)
        big = big_r.at[i, pl.ds(0, per * (n - 1))]
        small = mid_r.at[i, pl.ds(0, 16 * (n2 - 1))]
        await_bytes(g_hbm.at[pl.ds(base, per * (n - 1))], arr.at[i, 3])
        await_bytes(big, ars.at[i, 0])
        await_bytes(small, ars.at[i, 1])
        await_bytes(small, ars.at[i, 2])
        await_bytes(big, ars.at[i, 3])
        await_bytes(fin_s.at[i, pl.ds(0, per)], lsem.at[2 + i])

    for half in range(2):
        for n, w in HALVES:
            cot_tile = cott[HID * half + n : HID * half + n + w]
            gp[HID * half : HID * half + HID, n : n + w] = dot(hidt[...], cot_tile, (1, 1)).astype(BF16)
    stream_rs1(1)
    stream_rs1(0)
    for n, w in TILES:
        pb[:, n : n + w] = dot(wi[...], dpret[:, n : n + w], (1, 0)).astype(BF16)
    pair_send(pb, rdb, 0)
    for n, w in HALVES:
        gp[CH : 2 * CH, n : n + w] = dot(mixt[...], dpret[n : n + w], (1, 1)).astype(BF16)
    stream_rs1(2)
    for n, w in TILES:
        po[:, n : n + w] = dot(wot[...], hidt[:, n : n + w], (1, 0)).astype(BF16)
    pair_send(po, rdo, 1)
    pair_sum(pb, rdb, psb, rxb, 0)
    stream_rs2(1)
    stream_rs1(3)
    stream_rs2(2)
    stream_rs1(4)
    pair_sum(po, rdo, pso, rxo, 1)
    stream_rs2(0)
    stream_ag1(1)

    chan_wait(rxb, 0)
    dmp[COLS : COLS * (ROWS + 1), OWN:LANES] = jnp.zeros((PIX, LANES - OWN), BF16)
    for p in range(PIX // 128):
        lanes = slice(128 * p, 128 * p + 128)
        total = cott[rows(c), lanes].astype(F32) + chan_sum(pb, rdb, rxb, lanes)
        dmp[COLS + 128 * p : COLS + 128 * p + 128, 0:OWN] = total.T.astype(BF16)
    send(dmp.at[pl.ds(COLS * ROWS, COLS)], dmp.at[pl.ds(0, COLS)], hs.at[2], hr.at[2], below)
    send(dmp.at[pl.ds(COLS, COLS)], dmp.at[pl.ds(COLS * (ROWS + 1), COLS)], hs.at[3], hr.at[3], above)

    for h in range(ROWS):
        v = dmp[COLS * (h + 1) : COLS * (h + 2)].astype(F32)
        dcat[COLS * h : COLS * (h + 1), 0:LANES] = earlier(v).astype(BF16)
        dcat[COLS * h : COLS * (h + 1), LANES : 2 * LANES] = dmp[COLS * (h + 1) : COLS * (h + 2)]
        dcat[COLS * h : COLS * (h + 1), 2 * LANES :] = later(v).astype(BF16)
    lane_group = lax.broadcasted_iota(jnp.int32, (GROUP, LANES), 1) // GROUP
    gks[GK_ROWS:GK_PAD] = jnp.zeros((GK_PAD - GK_ROWS, LANES), BF16)
    for a in range(3):
        full = dot(xp[COLS * a : COLS * a + PIX], dcat[...], (0, 0))
        for b in range(3):
            part = jnp.zeros((GROUP, LANES), F32)
            for g in range(OWN // GROUP):
                piece = full[GROUP * g : GROUP * (g + 1), LANES * b : LANES * (b + 1)]
                part = part + jnp.where(lane_group == g, piece, 0.0)
            gks[GROUP * (3 * a + b) : GROUP * (3 * a + b + 1)] = part.astype(BF16)
    for d in range(1, NY):
        send(gks, gkr_y.at[d - 1], gss.at[0], gsr.at[0], ypeer(d))

    stream_ag1(2)
    stream_ag2(1)
    stream_rs2(3)
    stream_ag1(0)
    stream_ag2(2)

    await_bytes(dmp.at[pl.ds(0, COLS)], hr.at[2])
    await_bytes(dmp.at[pl.ds(0, COLS)], hr.at[3])
    top = dmp[0:COLS].astype(F32)
    dmp[0:COLS] = jnp.where(s > 0, top, 0.0).astype(BF16)
    end = dmp[COLS * (ROWS + 1) : COLS * (ROWS + 2)].astype(F32)
    dmp[COLS * (ROWS + 1) : COLS * (ROWS + 2)] = jnp.where(s < last, end, 0.0).astype(BF16)

    def back_row(h, carry):
        base = pl.multiple_of(h * COLS, COLS)
        sums = []
        for b in range(3):
            total = None
            for a in range(3):
                u = dmp[pl.ds(base + (2 - a) * COLS, COLS)]
                term = dot(u, dense[a, :, LANES * b : LANES * (b + 1)], (1, 1))
                total = term if total is None else total + term
            sums.append(total)
        out = earlier(sums[0]) + sums[1] + later(sums[2])
        out = out + dmp[pl.ds(base + COLS, COLS)].astype(F32)
        gf_ref[h] = out.T[0:OWN].astype(BF16)
        return carry

    lax.fori_loop(0, ROWS, back_row, 0)

    stream_rs2(4)
    stream_ag2(0)
    stream_ag1(3)

    await_bytes(gkr_y, gsr.at[0])
    total = gks[...].astype(F32)
    for d in range(1, NY):
        total = total + gkr_y[d - 1].astype(F32)
    gk1[...] = total.astype(BF16)
    per = GK_PAD // NZ
    for d in range(1, NZ):
        there = pl.multiple_of(per * ((z + d) % NZ), 16)
        send(gk1.at[pl.ds(there, per)], gkr_z.at[pl.ds(per * (d - 1), per)], gss.at[1], gsr.at[1], zpeer(d))

    stream_ag2(3)
    stream_ag1(4)

    chan_wait(rxo, 1)
    total = chan_sum(po, rdo, rxo, slice(0, PIX)) + mixt[rows(c), :].astype(F32)
    for h in range(ROWS):
        bo_ref[h] = total[:, COLS * h : COLS * (h + 1)].astype(BF16)

    await_bytes(gkr_z, gsr.at[1])
    mine = pl.ds(pl.multiple_of(per * z, 16), per)
    total = gk1[mine].astype(F32)
    for d in range(1, NZ):
        total = total + gkr_z[per * (d - 1) : per * d].astype(F32)
    gk2[mine] = total.astype(BF16)
    for d in range(1, NZ):
        send(gk2.at[mine], gk2.at[mine], gss.at[2], gsr.at[2], zpeer(d))
    stream_ag2(4)

    await_bytes(gk2.at[pl.ds(0, per * (NZ - 1))], gsr.at[2])
    for t in range(9):
        gk_ref[t] = gk2[GROUP * t : GROUP * (t + 1), 0:OWN].astype(F32) * scale

    for i in range(STREAMS):
        stream_end(i)
    gather_done(cott, 0)
    gather_done(mixt, 1)
    pair_done(rdb, 0)
    pair_done(rdo, 1)
    for i in range(2):
        await_bytes(hx.at[i], hs.at[i])
        await_bytes(dmp.at[pl.ds(0, COLS)], hs.at[2 + i])
    await_bytes(gkr_y, gss.at[0])
    await_bytes(gkr_z, gss.at[1])
    await_bytes(gkr_z, gss.at[2])


def finish(
    scale, in_ref, left_ref, right_ref, bo_ref, gf_ref, gk_ref,
    grad_in_ref, grad_out_ref, block_out_ref, features_ref, taps_ref,
):
    block_out_ref[...] = bo_ref[...]
    features_ref[...] = gf_ref[...]
    taps_ref[...] = gk_ref[...]
    grad_in_ref[...] = in_ref[...].astype(F32) * scale
    grad_out_ref[:, 0:HID] = left_ref[...].astype(F32) * scale
    grad_out_ref[:, HID:CH] = right_ref[...].astype(F32) * scale


def turned(cells):
    return jnp.transpose(cells, (0, 2, 1))


def body(feature_map, conv_kernel, weight_in, weight_out, cotangent):
    scale = 1.0 / math.sqrt(ROWS * NZ * NY * COLS)
    vmem = pl.BlockSpec(memory_space=pltpu.VMEM)
    hbm = pl.BlockSpec(memory_space=pl.ANY)

    def run(*refs):
        kernel(scale, *refs)

    per = GK_PAD // NZ
    block_out, grad_features, grad_conv, grads = pl.pallas_call(
        run,
        out_shape=[
            jax.ShapeDtypeStruct((ROWS, OWN, COLS), BF16),
            jax.ShapeDtypeStruct((ROWS, OWN, COLS), BF16),
            jax.ShapeDtypeStruct((9, GROUP, OWN), F32),
            jax.ShapeDtypeStruct((2 * CH, HID), BF16),
        ],
        in_specs=[vmem, vmem, hbm, hbm, vmem],
        out_specs=[vmem, vmem, vmem, hbm],
        scratch_shapes=[
            pltpu.VMEM((COLS * (ROWS + 2), LANES), BF16),
            pltpu.VMEM((2, OWN, COLS), BF16),
            pltpu.VMEM((COLS * (ROWS + 2), LANES), BF16),
            pltpu.VMEM((PIX, 3 * LANES), BF16),
            pltpu.VMEM((3, LANES, 3 * LANES), BF16),
            pltpu.VMEM((PIX, LANES), BF16),
            pltpu.VMEM((CH, HID), BF16),
            pltpu.VMEM((HID, CH), BF16),
            pltpu.VMEM((HID, CH), BF16),
            pltpu.VMEM((CH, HID), BF16),
            pltpu.VMEM((CH, PIX), BF16),
            pltpu.VMEM((CH, PIX), BF16),
            pltpu.VMEM((HID, PIX), F32),
            pltpu.VMEM((HID, PIX), F32),
            pltpu.VMEM((HID, PIX), BF16),
            pltpu.VMEM((HID, PIX), BF16),
            pltpu.VMEM((CH, PIX), BF16),
            pltpu.VMEM((CH, PIX), BF16),
            pltpu.VMEM((NX, OWN, PIX), BF16),
            pltpu.VMEM((NX, OWN, PIX), BF16),
            pltpu.VMEM((NX - 1, OWN, PIX), BF16),
            pltpu.VMEM((NX - 1, OWN, PIX), BF16),
            pltpu.VMEM((NX - 1, OWN, PIX), BF16),
            pltpu.VMEM((NX - 1, OWN, PIX), BF16),
            pltpu.VMEM((2 * CH, HID), BF16),
            pltpu.VMEM((STREAMS, 448, HID), BF16),
            pltpu.VMEM((STREAMS, 128, HID), BF16),
            pltpu.VMEM((STREAMS, 112, HID), BF16),
            pltpu.VMEM((STREAMS, 128, HID), BF16),
            pltpu.VMEM((GK_PAD, LANES), BF16),
            pltpu.VMEM((NY - 1, GK_PAD, LANES), BF16),
            pltpu.VMEM((GK_PAD, LANES), BF16),
            pltpu.VMEM((per * (NZ - 1), LANES), BF16),
            pltpu.VMEM((GK_PAD, LANES), BF16),
            pltpu.SemaphoreType.DMA((2 + STREAMS,)),
            pltpu.SemaphoreType.DMA((4,)),
            pltpu.SemaphoreType.DMA((4,)),
            pltpu.SemaphoreType.DMA((2, 2, 7)),
            pltpu.SemaphoreType.DMA((2, 2, 7)),
            pltpu.SemaphoreType.DMA((2, 7)),
            pltpu.SemaphoreType.DMA((2, 7)),
            pltpu.SemaphoreType.DMA((STREAMS, 4)),
            pltpu.SemaphoreType.DMA((STREAMS, 4)),
            pltpu.SemaphoreType.DMA((3,)),
            pltpu.SemaphoreType.DMA((3,)),
        ],
        compiler_params=pltpu.CompilerParams(
            collective_id=0, has_side_effects=True, vmem_limit_bytes=60 << 20
        ),
    )(turned(feature_map), conv_kernel, weight_in, weight_out, turned(cotangent))
    steps = ROWS
    halves = pl.BlockSpec((HID // steps, HID), lambda i: (i, 0))
    row = pl.BlockSpec((1, OWN, COLS), lambda i: (i, 0, 0))
    taps = pl.BlockSpec((9, GROUP, OWN), lambda i: (0, 0, 0))
    grad_in, grad_out, block_out, grad_features, grad_conv = pl.pallas_call(
        lambda *refs: finish(scale, *refs),
        grid=(steps,),
        out_shape=[
            jax.ShapeDtypeStruct((CH, HID), F32),
            jax.ShapeDtypeStruct((HID, CH), F32),
            jax.ShapeDtypeStruct((ROWS, OWN, COLS), BF16),
            jax.ShapeDtypeStruct((ROWS, OWN, COLS), BF16),
            jax.ShapeDtypeStruct((9, GROUP, OWN), F32),
        ],
        in_specs=[
            pl.BlockSpec((CH // steps, HID), lambda i: (steps + i, 0)),
            halves,
            pl.BlockSpec((HID // steps, HID), lambda i: (steps + i, 0)),
            row, row, taps,
        ],
        out_specs=[
            pl.BlockSpec((CH // steps, HID), lambda i: (i, 0)),
            pl.BlockSpec((HID // steps, CH), lambda i: (i, 0)),
            row, row, taps,
        ],
        compiler_params=pltpu.CompilerParams(vmem_limit_bytes=60 << 20),
    )(grads, grads, grads, block_out, grad_features, grad_conv)
    return turned(block_out), turned(grad_features), grad_conv, grad_in, grad_out


def solution(mesh):
    return jax.shard_map(
        body,
        mesh=mesh,
        in_specs=(
            P("space", None, "chan"),
            P(None, None, "chan"),
            P(None, "chan"),
            P("chan", None),
            P("space", None, "chan"),
        ),
        out_specs=(
            P("space", None, "chan"),
            P("space", None, "chan"),
            P(None, None, "chan"),
            P(None, "chan"),
            P("chan", None),
        ),
        check_vma=False,
    )
```

```python
import math

import jax
import jax.numpy as jnp
from jax import lax
from jax.experimental import pallas as pl
from jax.experimental.pallas import tpu as pltpu
from jax.sharding import PartitionSpec as P

MESH = pl.DeviceIdType.MESH
F32 = jnp.float32
BF16 = jnp.bfloat16

NZ, NY, NX = 8, 4, 4
ROWS, COLS, OWN, GROUP = 4, 224, 160, 32
PIX = ROWS * COLS
CH, HID = 1280, 640
LANES = 256
CHUNKS = ((0, 512), (512, 384))
TILES = ((0, 256), (256, 256), (512, 256), (768, 128))
HALVES = ((0, 256), (256, 256), (512, 128))
STREAMS = 5
SROWS = 512
ZFIRST = (True, False, False, False, False)
GK_ROWS = 9 * GROUP
GK_PAD = 384


def dot(a, b, dims):
    return lax.dot_general(a, b, ((dims[:1], dims[1:]), ((), ())), preferred_element_type=F32)


def gelu_slope(values):
    return 0.5 * (1.0 + lax.erf(values * (1.0 / math.sqrt(2.0)))) + values * jnp.exp(
        -0.5 * values * values
    ) * (1.0 / math.sqrt(2.0 * math.pi))


def kernel(
    scale,
    x_ref, ck_ref, wi_hbm, wo_hbm, cot_ref,
    bo_ref, gf_ref, gk_ref, g_hbm,
    xp, hx, dmp, dcat, dense, mixp, wi, wo, wit, wot, cott, mixt, dht, pret, hidt, dpret,
    pb, po, rdb, rdo, psb, pso, rxb, rxo,
    gp, far_r, relay_s, big_r, mid_s, mid_r, fin_s, gks, gkr_y, gk1, gkr_z, gk2,
    lsem, hs, hr, ags, agr, rss, rsr, ars, arr, gss, gsr,
):
    s = lax.axis_index("space")
    c = lax.axis_index("chan")
    z, y, x, k = s // NY, s % NY, c // 2, c % 2
    partner = {"space": s, "chan": 2 * x + 1 - k}
    above = {"space": (s + 31) % 32, "chan": c}
    below = {"space": (s + 1) % 32, "chan": c}

    def xpeer(d):
        return {"space": s, "chan": 2 * ((x + d) % NX) + k}

    def ypeer(d):
        return {"space": z * NY + (y + d) % NY, "chan": c}

    def zpeer(d):
        return {"space": ((z + d) % NZ) * NY + y, "chan": c}

    def send(src, dst, ssem, rsem, dev):
        copy = pltpu.make_async_remote_copy(
            src_ref=src, dst_ref=dst, send_sem=ssem, recv_sem=rsem, device_id=dev, device_id_type=MESH
        )
        copy.start()

    def await_bytes(ref, sem):
        pltpu.make_async_copy(ref, ref, sem).wait()

    def rows(block):
        return pl.ds(pl.multiple_of(block * OWN, 32), OWN)

    load_wi = pltpu.make_async_copy(wi_hbm, wi, lsem.at[0])
    load_wo = pltpu.make_async_copy(wo_hbm, wo, lsem.at[1])
    load_wi.start()
    load_wo.start()
    barrier = pltpu.get_barrier_semaphore()
    peers = [partner, above, below]
    peers += [xpeer(d) for d in range(1, NX)]
    peers += [ypeer(d) for d in range(1, NY)]
    peers += [zpeer(d) for d in range(1, NZ)]
    for dev in peers:
        pl.semaphore_signal(barrier, inc=1, device_id=dev, device_id_type=MESH)

    own_cot = jnp.concatenate([cot_ref[h].astype(F32) for h in range(ROWS)], axis=1)
    cott[rows(c), :] = own_cot.astype(BF16)
    pl.semaphore_wait(barrier, len(peers))

    send(x_ref.at[ROWS - 1], hx.at[0], hs.at[0], hr.at[0], below)
    send(x_ref.at[0], hx.at[1], hs.at[1], hr.at[1], above)

    def gather_send(buf, which, part):
        lanes = pl.ds(CHUNKS[part][0], CHUNKS[part][1])
        own = buf.at[rows(c), lanes]
        for d in (2, 1, 3):
            send(own, own, ags.at[which, part, d - 1], agr.at[which, part, d - 1], xpeer(d))
        send(own, own, ags.at[which, part, 3], agr.at[which, part, 3], partner)

    def gather_forward(buf, which, part):
        lanes = pl.ds(CHUNKS[part][0], CHUNKS[part][1])
        for d in (1, 3, 2):
            got = buf.at[rows(2 * ((x + NX - d) % NX) + k), lanes]
            await_bytes(got, agr.at[which, part, d - 1])
            send(got, got, ags.at[which, part, 3 + d], agr.at[which, part, 3 + d], partner)

    def gather_wait(buf, which, part):
        lanes = pl.ds(CHUNKS[part][0], CHUNKS[part][1])
        for d in (0, 1, 3, 2):
            got = buf.at[rows(2 * ((x + NX - d) % NX) + 1 - k), lanes]
            await_bytes(got, agr.at[which, part, 3 + d])

    def gather_done(buf, which):
        for part in range(2):
            lanes = pl.ds(CHUNKS[part][0], CHUNKS[part][1])
            for i in range(7):
                await_bytes(buf.at[pl.ds(0, OWN), lanes], ags.at[which, part, i])

    gather_send(cott, 0, 0)
    gather_send(cott, 0, 1)

    xp[:, OWN:LANES] = jnp.zeros((COLS * (ROWS + 2), LANES - OWN), BF16)
    for h in range(ROWS):
        xp[COLS * (h + 1) : COLS * (h + 2), 0:OWN] = x_ref[h].astype(F32).T.astype(BF16)

    row_group = lax.broadcasted_iota(jnp.int32, (OWN, OWN), 0) // GROUP
    col_group = lax.broadcasted_iota(jnp.int32, (OWN, OWN), 1) // GROUP
    same = row_group == col_group
    dense[...] = jnp.zeros_like(dense)
    for t in range(9):
        tap = ck_ref[t].astype(F32)
        full = jnp.where(same, jnp.concatenate([tap] * (OWN // GROUP), axis=0), 0.0)
        dense[t // 3, 0:OWN, LANES * (t % 3) : LANES * (t % 3) + OWN] = full.astype(BF16)

    column = lax.broadcasted_iota(jnp.int32, (COLS, LANES), 0)

    def later(v):
        return jnp.where(column == 0, 0.0, pltpu.roll(v, 1, 0))

    def earlier(v):
        return jnp.where(column == COLS - 1, 0.0, pltpu.roll(v, COLS - 1, 0))

    last = NZ * NY - 1
    await_bytes(hx.at[0], hr.at[0])
    xp[0:COLS, 0:OWN] = jnp.where(s > 0, hx[0].astype(F32).T, 0.0).astype(BF16)
    await_bytes(hx.at[1], hr.at[1])
    below_row = jnp.where(s < last, hx[1].astype(F32).T, 0.0)
    xp[COLS * (ROWS + 1) : COLS * (ROWS + 2), 0:OWN] = below_row.astype(BF16)

    def conv_row(h, carry):
        base = pl.multiple_of(h * COLS, COLS)
        total = dot(xp[pl.ds(base, COLS)], dense[0], (1, 0))
        total += dot(xp[pl.ds(base + COLS, COLS)], dense[1], (1, 0))
        total += dot(xp[pl.ds(base + 2 * COLS, COLS)], dense[2], (1, 0))
        out = later(total[:, 0:LANES]) + total[:, LANES : 2 * LANES] + earlier(total[:, 2 * LANES :])
        mixp[pl.ds(base, COLS)] = (xp[pl.ds(base + COLS, COLS)].astype(F32) + out).astype(BF16)
        return carry

    lax.fori_loop(0, ROWS, conv_row, 0)
    for p in range(PIX // 128):
        block = mixp[128 * p : 128 * p + 128].astype(F32).T
        mixt[rows(c), 128 * p : 128 * p + 128] = block[0:OWN].astype(BF16)
        if p == 3:
            gather_send(mixt, 1, 0)
    gather_send(mixt, 1, 1)

    load_wi.wait()
    load_wo.wait()

    def turn_in(i, carry):
        r = pl.multiple_of(i * 128, 128)
        wit[:, pl.ds(r, 128)] = wi[pl.ds(r, 128), :].astype(F32).T.astype(BF16)
        return carry

    def turn_out(i, carry):
        r = pl.multiple_of(i * 128, 128)
        wot[:, pl.ds(r, 128)] = wo[pl.ds(r, 128), :].astype(F32).T.astype(BF16)
        return carry

    lax.fori_loop(0, CH // 128, turn_in, 0)
    gather_forward(cott, 0, 0)
    gather_forward(cott, 0, 1)
    lax.fori_loop(0, HID // 128, turn_out, 0)
    gather_wait(cott, 0, 0)
    gather_wait(cott, 0, 1)
    for n, w in TILES:
        dht[:, n : n + w] = dot(wo[...], cott[:, n : n + w], (1, 0))

    gather_forward(mixt, 1, 0)
    gather_forward(mixt, 1, 1)
    for part in range(2):
        gather_wait(mixt, 1, part)
        first, width = CHUNKS[part]
        for n, w in TILES:
            if first <= n < first + width:
                pret[:, n : n + w] = dot(wit[...], mixt[:, n : n + w], (1, 0))

        def unit(i, carry, first=first, width=width):
            r = pl.ds(pl.multiple_of(i * 16, 16), 16)
            pre = pret[r, first : first + width]
            upper = 0.5 * (1.0 + lax.erf(pre * (1.0 / math.sqrt(2.0))))
            bell = jnp.exp(-0.5 * pre * pre) * (1.0 / math.sqrt(2.0 * math.pi))
            hidt[r, first : first + width] = (pre * upper).astype(BF16)
            slope = upper + pre * bell
            dpret[r, first : first + width] = (dht[r, first : first + width] * slope).astype(BF16)
            return carry

        lax.fori_loop(0, HID // 16, unit, 0)

    def pair_send(buf, got, which):
        for d in (1, 2, 3, 0):
            block = 2 * ((x + d) % NX) + 1 - k
            send(buf.at[rows(block)], got.at[d], rss.at[which, d], rsr.at[which, d], partner)

    def pair_sum(buf, got, out, landed, which):
        for d in (2, 1, 3, 0):
            await_bytes(got.at[d], rsr.at[which, d])
            if d:
                block = 2 * ((x + d) % NX) + k
                out[d - 1] = (buf[rows(block)].astype(F32) + got[d].astype(F32)).astype(BF16)
                send(out.at[d - 1], landed.at[d - 1], rss.at[which, 3 + d], rsr.at[which, 3 + d], xpeer(d))

    def chan_wait(landed, which):
        for d in range(1, NX):
            await_bytes(landed.at[d - 1], rsr.at[which, 3 + d])

    def chan_sum(buf, got, landed, lanes):
        total = buf[rows(c), lanes].astype(F32) + got[0, :, lanes].astype(F32)
        for d in range(1, NX):
            total = total + landed[d - 1, :, lanes].astype(F32)
        return total

    def pair_done(got, which):
        for i in range(7):
            await_bytes(got.at[0], rss.at[which, i])

    def start(i):
        base = SROWS * i
        if ZFIRST[i]:
            n, per, peer, me = NZ, SROWS // NZ, zpeer, z
        else:
            n, per, peer, me = NY, SROWS // NY, ypeer, y
        return base, n, per, peer, me

    def span(i, q, off=0, size=None):
        base, n, per, peer, me = start(i)
        place = base + per * ((me + q + n) % n) + off
        return pl.ds(pl.multiple_of(place, 32), per if size is None else size)

    def hop_table(i):
        if ZFIRST[i]:
            half = SROWS // NZ // 2
            full = 2 * half
            far = [(-3, 0, full, -1), (-4, 0, half, -2), (3, 0, full, 1), (4, half, half, 2)]
            near = [(-1, 0, full, -1, 0), (1, 0, full, 1, full)]
            relay = [(-2, 0, full, -2, 2 * full), (2, 0, full, 2, 3 * full)]
            return full, half, far, near, relay
        half = SROWS // NY // 2
        full = 2 * half
        far = [(2, 0, half, 1), (2, half, half, -1)]
        near = [(1, half, half, 1, half), (-1, 0, half, -1, full)]
        relay = [(1, 0, half, 1, 0), (-1, half, half, -1, full + half)]
        return full, half, far, near, relay

    def stream_rs1(i):
        base, n, per, peer, me = start(i)
        full, half, far, near, relay = hop_table(i)
        at = 0
        for q, off, size, to in far:
            send(gp.at[span(i, q, off, size)], far_r.at[i, pl.ds(at, size)], ars.at[i, 0], arr.at[i, 0], peer(to % n))
            at += size
        for q, off, size, to, place in near:
            send(
                gp.at[span(i, q, off, size)], big_r.at[i, pl.ds(place, size)],
                ars.at[i, 4], arr.at[i, 4], peer(to % n),
            )

    def far_rows(i):
        return far_r.at[i, pl.ds(0, 192 if ZFIRST[i] else 128)]

    def big_rows(i):
        return big_r.at[i, pl.ds(0, 256)]

    def stream_rs1b(i):
        base, n, per, peer, me = start(i)
        full, half, far, near, relay = hop_table(i)
        await_bytes(far_rows(i), arr.at[i, 0])
        if ZFIRST[i]:
            low = gp[span(i, -2)].astype(F32) + far_r[i, 0:full].astype(F32)
            relay_s[i, 0:half] = (low[0:half] + far_r[i, full : full + half].astype(F32)).astype(BF16)
            relay_s[i, half:full] = low[half:].astype(BF16)
            high = gp[span(i, 2)].astype(F32) + far_r[i, full + half : 2 * full + half].astype(F32)
            relay_s[i, full : full + half] = high[0:half].astype(BF16)
            relay_s[i, full + half : 2 * full] = (
                high[half:] + far_r[i, 2 * full + half : 3 * full].astype(F32)
            ).astype(BF16)
        else:
            up = gp[span(i, 1, 0, half)].astype(F32) + far_r[i, 0:half].astype(F32)
            relay_s[i, 0:half] = up.astype(BF16)
            down = gp[span(i, -1, half, half)].astype(F32) + far_r[i, half:full].astype(F32)
            relay_s[i, half:full] = down.astype(BF16)
        at = 0
        for q, off, size, to, place in relay:
            send(
                relay_s.at[i, pl.ds(at, size)], big_r.at[i, pl.ds(place, size)],
                ars.at[i, 5], arr.at[i, 4], peer(to % n),
            )
            at += size

    def second(i):
        if ZFIRST[i]:
            return NY, ypeer, y
        return NZ, zpeer, z

    def stream_rs2(i):
        base, n, per, peer, me = start(i)
        await_bytes(big_rows(i), arr.at[i, 4])
        total = gp[span(i, 0)].astype(F32)
        for d in range(256 // per):
            total = total + big_r[i, per * d : per * (d + 1)].astype(F32)
        mid_s[i, 0:per] = total.astype(BF16)
        n2, peer2, me2 = second(i)
        for d in range(1, n2):
            there = pl.multiple_of(16 * ((me2 + d) % n2), 16)
            send(
                mid_s.at[i, pl.ds(there, 16)], mid_r.at[i, pl.ds(16 * (d - 1), 16)],
                ars.at[i, 1], arr.at[i, 1], peer2(d),
            )

    def stream_ag1(i):
        n2, peer2, me2 = second(i)
        await_bytes(mid_r.at[i, pl.ds(0, 16 * (n2 - 1))], arr.at[i, 1])
        mine = pl.ds(pl.multiple_of(16 * me2, 16), 16)
        total = mid_s[i, mine].astype(F32)
        for d in range(1, n2):
            total = total + mid_r[i, 16 * (d - 1) : 16 * d].astype(F32)
        fin_s[i, mine] = total.astype(BF16)
        for d in range(1, n2):
            send(fin_s.at[i, mine], fin_s.at[i, mine], ars.at[i, 2], arr.at[i, 2], peer2(d))

    def stream_ag2(i):
        base, n, per, peer, me = start(i)
        n2, peer2, me2 = second(i)
        await_bytes(fin_s.at[i, pl.ds(0, 16 * (n2 - 1))], arr.at[i, 2])
        half = per // 2
        for off, to in spread(i):
            send(
                fin_s.at[i, pl.ds(off, half)], g_hbm.at[span(i, 0, off, half)],
                ars.at[i, 3], arr.at[i, 3] if relayed(i, off, to) else arr.at[i, 5], peer(to % n),
            )
        pltpu.make_async_copy(fin_s.at[i, pl.ds(0, per)], g_hbm.at[span(i, 0)], lsem.at[2 + i]).start()

    def spread(i):
        half = SROWS // NZ // 2 if ZFIRST[i] else SROWS // NY // 2
        if ZFIRST[i]:
            return [(off, to) for to in (2, -2, 1, -1) for off in (0, half)]
        return [(0, 1), (half, -1), (half, 1), (0, -1)]

    def relayed(i, off, to):
        return abs(to) == 2 if ZFIRST[i] else (off == 0) == (to == 1)

    def stream_ag2b(i):
        base, n, per, peer, me = start(i)
        half = per // 2
        await_bytes(fin_s.at[i, pl.ds(0, 128)], arr.at[i, 3])
        if ZFIRST[i]:
            onward = [(-2, 0, per, 1), (2, 0, per, -1), (-2, 0, half, 2), (2, half, half, -2)]
        else:
            onward = [(-1, 0, half, 1), (1, half, half, -1)]
        for q, off, size, to in onward:
            block = g_hbm.at[span(i, q, off, size)]
            send(block, block, ars.at[i, 6], arr.at[i, 6], peer(to % n))

    def stream_end(i):
        base, n, per, peer, me = start(i)
        n2, peer2, me2 = second(i)
        small = mid_r.at[i, pl.ds(0, 16 * (n2 - 1))]
        onward = far_rows(i)
        await_bytes(g_hbm.at[pl.ds(base, 128)], arr.at[i, 5])
        await_bytes(g_hbm.at[pl.ds(base, 192 if ZFIRST[i] else 128)], arr.at[i, 6])
        await_bytes(onward, ars.at[i, 0])
        await_bytes(relay_s.at[i, pl.ds(0, 128)], ars.at[i, 4])
        await_bytes(relay_s.at[i, pl.ds(0, 128)], ars.at[i, 5])
        await_bytes(small, ars.at[i, 1])
        await_bytes(small, ars.at[i, 2])
        await_bytes(big_rows(i), ars.at[i, 3])
        await_bytes(onward, ars.at[i, 6])
        await_bytes(fin_s.at[i, pl.ds(0, per)], lsem.at[2 + i])

    for half in range(2):
        for n, w in HALVES:
            cot_tile = cott[HID * half + n : HID * half + n + w]
            gp[HID * half : HID * half + HID, n : n + w] = dot(hidt[...], cot_tile, (1, 1)).astype(BF16)
    stream_rs1(1)
    stream_rs1(0)
    for n, w in TILES:
        pb[:, n : n + w] = dot(wi[...], dpret[:, n : n + w], (1, 0)).astype(BF16)
    pair_send(pb, rdb, 0)
    for n, w in HALVES:
        gp[CH : 2 * CH, n : n + w] = dot(mixt[...], dpret[n : n + w], (1, 1)).astype(BF16)
    stream_rs1(2)
    for n, w in TILES:
        po[:, n : n + w] = dot(wot[...], hidt[:, n : n + w], (1, 0)).astype(BF16)
    pair_send(po, rdo, 1)
    pair_sum(pb, rdb, psb, rxb, 0)
    stream_rs1(3)
    stream_rs1b(1)
    stream_rs1b(0)
    stream_rs1b(2)
    stream_rs2(1)
    stream_rs1(4)
    stream_rs1b(3)
    stream_rs2(2)
    pair_sum(po, rdo, pso, rxo, 1)
    stream_rs2(0)
    stream_ag1(1)
    stream_rs1b(4)
    stream_rs2(3)
    stream_ag1(2)
    stream_ag2(1)

    chan_wait(rxb, 0)
    dmp[COLS : COLS * (ROWS + 1), OWN:LANES] = jnp.zeros((PIX, LANES - OWN), BF16)
    for p in range(PIX // 128):
        lanes = slice(128 * p, 128 * p + 128)
        total = cott[rows(c), lanes].astype(F32) + chan_sum(pb, rdb, rxb, lanes)
        dmp[COLS + 128 * p : COLS + 128 * p + 128, 0:OWN] = total.T.astype(BF16)
    send(dmp.at[pl.ds(COLS * ROWS, COLS)], dmp.at[pl.ds(0, COLS)], hs.at[2], hr.at[2], below)
    send(dmp.at[pl.ds(COLS, COLS)], dmp.at[pl.ds(COLS * (ROWS + 1), COLS)], hs.at[3], hr.at[3], above)

    for h in range(ROWS):
        v = dmp[COLS * (h + 1) : COLS * (h + 2)].astype(F32)
        dcat[COLS * h : COLS * (h + 1), 0:LANES] = earlier(v).astype(BF16)
        dcat[COLS * h : COLS * (h + 1), LANES : 2 * LANES] = dmp[COLS * (h + 1) : COLS * (h + 2)]
        dcat[COLS * h : COLS * (h + 1), 2 * LANES :] = later(v).astype(BF16)
    lane_group = lax.broadcasted_iota(jnp.int32, (GROUP, LANES), 1) // GROUP
    gks[GK_ROWS:GK_PAD] = jnp.zeros((GK_PAD - GK_ROWS, LANES), BF16)
    for a in range(3):
        full = dot(xp[COLS * a : COLS * a + PIX], dcat[...], (0, 0))
        for b in range(3):
            part = jnp.zeros((GROUP, LANES), F32)
            for g in range(OWN // GROUP):
                piece = full[GROUP * g : GROUP * (g + 1), LANES * b : LANES * (b + 1)]
                part = part + jnp.where(lane_group == g, piece, 0.0)
            gks[GROUP * (3 * a + b) : GROUP * (3 * a + b + 1)] = part.astype(BF16)
    for d in range(1, NY):
        send(gks, gkr_y.at[d - 1], gss.at[0], gsr.at[0], ypeer(d))

    stream_ag1(0)
    stream_rs2(4)
    stream_ag2(2)
    stream_ag2b(1)
    stream_ag1(3)

    await_bytes(dmp.at[pl.ds(0, COLS)], hr.at[2])
    await_bytes(dmp.at[pl.ds(0, COLS)], hr.at[3])
    top = dmp[0:COLS].astype(F32)
    dmp[0:COLS] = jnp.where(s > 0, top, 0.0).astype(BF16)
    end = dmp[COLS * (ROWS + 1) : COLS * (ROWS + 2)].astype(F32)
    dmp[COLS * (ROWS + 1) : COLS * (ROWS + 2)] = jnp.where(s < last, end, 0.0).astype(BF16)

    def back_row(h, carry):
        base = pl.multiple_of(h * COLS, COLS)
        sums = []
        for b in range(3):
            total = None
            for a in range(3):
                u = dmp[pl.ds(base + (2 - a) * COLS, COLS)]
                term = dot(u, dense[a, :, LANES * b : LANES * (b + 1)], (1, 1))
                total = term if total is None else total + term
            sums.append(total)
        out = earlier(sums[0]) + sums[1] + later(sums[2])
        out = out + dmp[pl.ds(base + COLS, COLS)].astype(F32)
        gf_ref[h] = out.T[0:OWN].astype(BF16)
        return carry

    lax.fori_loop(0, ROWS, back_row, 0)

    stream_ag2(0)
    stream_ag2(3)
    stream_ag1(4)
    stream_ag2b(2)

    await_bytes(gkr_y, gsr.at[0])
    total = gks[...].astype(F32)
    for d in range(1, NY):
        total = total + gkr_y[d - 1].astype(F32)
    gk1[...] = total.astype(BF16)
    per = GK_PAD // NZ
    for d in range(1, NZ):
        there = pl.multiple_of(per * ((z + d) % NZ), 16)
        send(gk1.at[pl.ds(there, per)], gkr_z.at[pl.ds(per * (d - 1), per)], gss.at[1], gsr.at[1], zpeer(d))

    stream_ag2b(0)
    stream_ag2b(3)
    stream_ag2(4)

    chan_wait(rxo, 1)
    total = chan_sum(po, rdo, rxo, slice(0, PIX)) + mixt[rows(c), :].astype(F32)
    for h in range(ROWS):
        bo_ref[h] = total[:, COLS * h : COLS * (h + 1)].astype(BF16)

    await_bytes(gkr_z, gsr.at[1])
    mine = pl.ds(pl.multiple_of(per * z, 16), per)
    total = gk1[mine].astype(F32)
    for d in range(1, NZ):
        total = total + gkr_z[per * (d - 1) : per * d].astype(F32)
    gk2[mine] = total.astype(BF16)
    for d in range(1, NZ):
        send(gk2.at[mine], gk2.at[mine], gss.at[2], gsr.at[2], zpeer(d))
    stream_ag2b(4)

    await_bytes(gk2.at[pl.ds(0, per * (NZ - 1))], gsr.at[2])
    for t in range(9):
        gk_ref[t] = gk2[GROUP * t : GROUP * (t + 1), 0:OWN].astype(F32) * scale

    for i in range(STREAMS):
        stream_end(i)
    gather_done(cott, 0)
    gather_done(mixt, 1)
    pair_done(rdb, 0)
    pair_done(rdo, 1)
    for i in range(2):
        await_bytes(hx.at[i], hs.at[i])
        await_bytes(dmp.at[pl.ds(0, COLS)], hs.at[2 + i])
    await_bytes(gkr_y, gss.at[0])
    await_bytes(gkr_z, gss.at[1])
    await_bytes(gkr_z, gss.at[2])


def finish(
    scale, in_ref, left_ref, right_ref, bo_ref, gf_ref, gk_ref,
    grad_in_ref, grad_out_ref, block_out_ref, features_ref, taps_ref,
):
    block_out_ref[...] = bo_ref[...]
    features_ref[...] = gf_ref[...]
    taps_ref[...] = gk_ref[...]
    grad_in_ref[...] = in_ref[...].astype(F32) * scale
    grad_out_ref[:, 0:HID] = left_ref[...].astype(F32) * scale
    grad_out_ref[:, HID:CH] = right_ref[...].astype(F32) * scale


def turned(cells):
    return jnp.transpose(cells, (0, 2, 1))


def body(feature_map, conv_kernel, weight_in, weight_out, cotangent):
    scale = 1.0 / math.sqrt(ROWS * NZ * NY * COLS)
    vmem = pl.BlockSpec(memory_space=pltpu.VMEM)
    hbm = pl.BlockSpec(memory_space=pl.ANY)

    def run(*refs):
        kernel(scale, *refs)

    per = GK_PAD // NZ
    block_out, grad_features, grad_conv, grads = pl.pallas_call(
        run,
        out_shape=[
            jax.ShapeDtypeStruct((ROWS, OWN, COLS), BF16),
            jax.ShapeDtypeStruct((ROWS, OWN, COLS), BF16),
            jax.ShapeDtypeStruct((9, GROUP, OWN), F32),
            jax.ShapeDtypeStruct((2 * CH, HID), BF16),
        ],
        in_specs=[vmem, vmem, hbm, hbm, vmem],
        out_specs=[vmem, vmem, vmem, hbm],
        scratch_shapes=[
            pltpu.VMEM((COLS * (ROWS + 2), LANES), BF16),
            pltpu.VMEM((2, OWN, COLS), BF16),
            pltpu.VMEM((COLS * (ROWS + 2), LANES), BF16),
            pltpu.VMEM((PIX, 3 * LANES), BF16),
            pltpu.VMEM((3, LANES, 3 * LANES), BF16),
            pltpu.VMEM((PIX, LANES), BF16),
            pltpu.VMEM((CH, HID), BF16),
            pltpu.VMEM((HID, CH), BF16),
            pltpu.VMEM((HID, CH), BF16),
            pltpu.VMEM((CH, HID), BF16),
            pltpu.VMEM((CH, PIX), BF16),
            pltpu.VMEM((CH, PIX), BF16),
            pltpu.VMEM((HID, PIX), F32),
            pltpu.VMEM((HID, PIX), F32),
            pltpu.VMEM((HID, PIX), BF16),
            pltpu.VMEM((HID, PIX), BF16),
            pltpu.VMEM((CH, PIX), BF16),
            pltpu.VMEM((CH, PIX), BF16),
            pltpu.VMEM((NX, OWN, PIX), BF16),
            pltpu.VMEM((NX, OWN, PIX), BF16),
            pltpu.VMEM((NX - 1, OWN, PIX), BF16),
            pltpu.VMEM((NX - 1, OWN, PIX), BF16),
            pltpu.VMEM((NX - 1, OWN, PIX), BF16),
            pltpu.VMEM((NX - 1, OWN, PIX), BF16),
            pltpu.VMEM((2 * CH, HID), BF16),
            pltpu.VMEM((STREAMS, 192, HID), BF16),
            pltpu.VMEM((STREAMS, 128, HID), BF16),
            pltpu.VMEM((STREAMS, 256, HID), BF16),
            pltpu.VMEM((STREAMS, 128, HID), BF16),
            pltpu.VMEM((STREAMS, 112, HID), BF16),
            pltpu.VMEM((STREAMS, 128, HID), BF16),
            pltpu.VMEM((GK_PAD, LANES), BF16),
            pltpu.VMEM((NY - 1, GK_PAD, LANES), BF16),
            pltpu.VMEM((GK_PAD, LANES), BF16),
            pltpu.VMEM((per * (NZ - 1), LANES), BF16),
            pltpu.VMEM((GK_PAD, LANES), BF16),
            pltpu.SemaphoreType.DMA((2 + STREAMS,)),
            pltpu.SemaphoreType.DMA((4,)),
            pltpu.SemaphoreType.DMA((4,)),
            pltpu.SemaphoreType.DMA((2, 2, 7)),
            pltpu.SemaphoreType.DMA((2, 2, 7)),
            pltpu.SemaphoreType.DMA((2, 7)),
            pltpu.SemaphoreType.DMA((2, 7)),
            pltpu.SemaphoreType.DMA((STREAMS, 7)),
            pltpu.SemaphoreType.DMA((STREAMS, 7)),
            pltpu.SemaphoreType.DMA((3,)),
            pltpu.SemaphoreType.DMA((3,)),
        ],
        compiler_params=pltpu.CompilerParams(
            collective_id=0, has_side_effects=True, vmem_limit_bytes=60 << 20
        ),
    )(turned(feature_map), conv_kernel, weight_in, weight_out, turned(cotangent))
    steps = ROWS
    halves = pl.BlockSpec((HID // steps, HID), lambda i: (i, 0))
    row = pl.BlockSpec((1, OWN, COLS), lambda i: (i, 0, 0))
    taps = pl.BlockSpec((9, GROUP, OWN), lambda i: (0, 0, 0))
    grad_in, grad_out, block_out, grad_features, grad_conv = pl.pallas_call(
        lambda *refs: finish(scale, *refs),
        grid=(steps,),
        out_shape=[
            jax.ShapeDtypeStruct((CH, HID), F32),
            jax.ShapeDtypeStruct((HID, CH), F32),
            jax.ShapeDtypeStruct((ROWS, OWN, COLS), BF16),
            jax.ShapeDtypeStruct((ROWS, OWN, COLS), BF16),
            jax.ShapeDtypeStruct((9, GROUP, OWN), F32),
        ],
        in_specs=[
            pl.BlockSpec((CH // steps, HID), lambda i: (steps + i, 0)),
            halves,
            pl.BlockSpec((HID // steps, HID), lambda i: (steps + i, 0)),
            row, row, taps,
        ],
        out_specs=[
            pl.BlockSpec((CH // steps, HID), lambda i: (i, 0)),
            pl.BlockSpec((HID // steps, CH), lambda i: (i, 0)),
            row, row, taps,
        ],
        compiler_params=pltpu.CompilerParams(vmem_limit_bytes=60 << 20),
    )(grads, grads, grads, block_out, grad_features, grad_conv)
    return turned(block_out), turned(grad_features), grad_conv, grad_in, grad_out


def solution(mesh):
    return jax.shard_map(
        body,
        mesh=mesh,
        in_specs=(
            P("space", None, "chan"),
            P(None, None, "chan"),
            P(None, "chan"),
            P("chan", None),
            P("space", None, "chan"),
        ),
        out_specs=(
            P("space", None, "chan"),
            P("space", None, "chan"),
            P(None, None, "chan"),
            P(None, "chan"),
            P("chan", None),
        ),
        check_vma=False,
    )
```

```python
import math

import jax
import jax.numpy as jnp
from jax import lax
from jax.experimental import pallas as pl
from jax.experimental.pallas import tpu as pltpu
from jax.sharding import PartitionSpec as P

MESH = pl.DeviceIdType.MESH
F32 = jnp.float32
BF16 = jnp.bfloat16

NZ, NY, NX = 8, 4, 4
ROWS, COLS, OWN, GROUP = 4, 224, 160, 32
PIX = ROWS * COLS
CH, HID = 1280, 640
LANES = 256
CHUNKS = ((0, 512), (512, 384))
TILES = ((0, 256), (256, 256), (512, 256), (768, 128))
HALVES = ((0, 256), (256, 256), (512, 128))
STREAMS = 5
SROWS = 512
ZFIRST = (True, False, False, False, False)
GK_ROWS = 9 * GROUP
GK_PAD = 384


def dot(a, b, dims):
    return lax.dot_general(a, b, ((dims[:1], dims[1:]), ((), ())), preferred_element_type=F32)


def gelu_slope(values):
    return 0.5 * (1.0 + lax.erf(values * (1.0 / math.sqrt(2.0)))) + values * jnp.exp(
        -0.5 * values * values
    ) * (1.0 / math.sqrt(2.0 * math.pi))


def kernel(
    scale,
    x_ref, ck_ref, wi_hbm, wo_hbm, cot_ref,
    bo_ref, gf_ref, gk_ref, g_hbm,
    xp, hx, dmp, dcat, dense, mixp, wi, wo, wit, wot, cott, mixt, dht, pret, hidt, dpret,
    pb, po, rdb, rdo, psb, pso, rxb, rxo,
    gp, far_r, relay_s, big_r, mid_s, mid_r, fin_s, gks, gkr_y, gk1, gkr_z, gk2,
    lsem, hs, hr, ags, agr, rss, rsr, ars, arr, gss, gsr,
):
    s = lax.axis_index("space")
    c = lax.axis_index("chan")
    z, y, x, k = s // NY, s % NY, c // 2, c % 2
    partner = {"space": s, "chan": 2 * x + 1 - k}
    above = {"space": (s + 31) % 32, "chan": c}
    below = {"space": (s + 1) % 32, "chan": c}

    def xpeer(d):
        return {"space": s, "chan": 2 * ((x + d) % NX) + k}

    def ypeer(d):
        return {"space": z * NY + (y + d) % NY, "chan": c}

    def zpeer(d):
        return {"space": ((z + d) % NZ) * NY + y, "chan": c}

    def send(src, dst, ssem, rsem, dev):
        copy = pltpu.make_async_remote_copy(
            src_ref=src, dst_ref=dst, send_sem=ssem, recv_sem=rsem, device_id=dev, device_id_type=MESH
        )
        copy.start()

    def await_bytes(ref, sem):
        pltpu.make_async_copy(ref, ref, sem).wait()

    def rows(block):
        return pl.ds(pl.multiple_of(block * OWN, 32), OWN)

    load_wi = pltpu.make_async_copy(wi_hbm, wi, lsem.at[0])
    load_wo = pltpu.make_async_copy(wo_hbm, wo, lsem.at[1])
    load_wi.start()
    load_wo.start()
    barrier = pltpu.get_barrier_semaphore()
    peers = [partner, above, below]
    peers += [xpeer(d) for d in range(1, NX)]
    peers += [ypeer(d) for d in range(1, NY)]
    peers += [zpeer(d) for d in range(1, NZ)]
    for dev in peers:
        pl.semaphore_signal(barrier, inc=1, device_id=dev, device_id_type=MESH)

    own_cot = jnp.concatenate([cot_ref[h].astype(F32) for h in range(ROWS)], axis=1)
    cott[rows(c), :] = own_cot.astype(BF16)
    pl.semaphore_wait(barrier, len(peers))

    send(x_ref.at[ROWS - 1], hx.at[0], hs.at[0], hr.at[0], below)
    send(x_ref.at[0], hx.at[1], hs.at[1], hr.at[1], above)

    def gather_send(buf, which, part):
        lanes = pl.ds(CHUNKS[part][0], CHUNKS[part][1])
        own = buf.at[rows(c), lanes]
        for d in (1, 3) if part == 0 else (3, 1):
            send(own, own, ags.at[which, part, d - 1], agr.at[which, part, d - 1], xpeer(d))
        send(own, own, ags.at[which, part, 3], agr.at[which, part, 3], partner)

    def gather_block(buf, which, part, d):
        lanes = pl.ds(CHUNKS[part][0], CHUNKS[part][1])
        got = buf.at[rows(2 * ((x + NX - d) % NX) + k), lanes]
        await_bytes(got, agr.at[which, part, d - 1])
        return got

    def gather_relay(buf, which):
        for part, d in ((0, 1), (1, 3)):
            got = gather_block(buf, which, part, d)
            send(got, got, ags.at[which, part, 1], agr.at[which, part, 1], xpeer(d))
            send(got, got, ags.at[which, part, 3 + d], agr.at[which, part, 3 + d], partner)

    def gather_forward(buf, which, pairs):
        for part, d in pairs:
            got = gather_block(buf, which, part, d)
            send(got, got, ags.at[which, part, 3 + d], agr.at[which, part, 3 + d], partner)

    def gather_wait(buf, which, part):
        lanes = pl.ds(CHUNKS[part][0], CHUNKS[part][1])
        for d in (0, 1, 3, 2):
            got = buf.at[rows(2 * ((x + NX - d) % NX) + 1 - k), lanes]
            await_bytes(got, agr.at[which, part, 3 + d])

    def gather_done(buf, which):
        for part in range(2):
            lanes = pl.ds(CHUNKS[part][0], CHUNKS[part][1])
            for i in range(7):
                await_bytes(buf.at[pl.ds(0, OWN), lanes], ags.at[which, part, i])

    gather_send(cott, 0, 0)
    gather_send(cott, 0, 1)

    xp[:, OWN:LANES] = jnp.zeros((COLS * (ROWS + 2), LANES - OWN), BF16)
    for h in range(ROWS):
        xp[COLS * (h + 1) : COLS * (h + 2), 0:OWN] = x_ref[h].astype(F32).T.astype(BF16)

    row_group = lax.broadcasted_iota(jnp.int32, (OWN, OWN), 0) // GROUP
    col_group = lax.broadcasted_iota(jnp.int32, (OWN, OWN), 1) // GROUP
    same = row_group == col_group
    dense[...] = jnp.zeros_like(dense)
    for t in range(9):
        tap = ck_ref[t].astype(F32)
        full = jnp.where(same, jnp.concatenate([tap] * (OWN // GROUP), axis=0), 0.0)
        dense[t // 3, 0:OWN, LANES * (t % 3) : LANES * (t % 3) + OWN] = full.astype(BF16)

    column = lax.broadcasted_iota(jnp.int32, (COLS, LANES), 0)

    def later(v):
        return jnp.where(column == 0, 0.0, pltpu.roll(v, 1, 0))

    def earlier(v):
        return jnp.where(column == COLS - 1, 0.0, pltpu.roll(v, COLS - 1, 0))

    last = NZ * NY - 1
    await_bytes(hx.at[0], hr.at[0])
    xp[0:COLS, 0:OWN] = jnp.where(s > 0, hx[0].astype(F32).T, 0.0).astype(BF16)
    await_bytes(hx.at[1], hr.at[1])
    below_row = jnp.where(s < last, hx[1].astype(F32).T, 0.0)
    xp[COLS * (ROWS + 1) : COLS * (ROWS + 2), 0:OWN] = below_row.astype(BF16)

    gather_relay(cott, 0)

    def conv_row(h, carry):
        base = pl.multiple_of(h * COLS, COLS)
        total = dot(xp[pl.ds(base, COLS)], dense[0], (1, 0))
        total += dot(xp[pl.ds(base + COLS, COLS)], dense[1], (1, 0))
        total += dot(xp[pl.ds(base + 2 * COLS, COLS)], dense[2], (1, 0))
        out = later(total[:, 0:LANES]) + total[:, LANES : 2 * LANES] + earlier(total[:, 2 * LANES :])
        mixp[pl.ds(base, COLS)] = (xp[pl.ds(base + COLS, COLS)].astype(F32) + out).astype(BF16)
        return carry

    lax.fori_loop(0, ROWS, conv_row, 0)
    for p in range(PIX // 128):
        block = mixp[128 * p : 128 * p + 128].astype(F32).T
        mixt[rows(c), 128 * p : 128 * p + 128] = block[0:OWN].astype(BF16)
        if p == 3:
            gather_send(mixt, 1, 0)
    gather_send(mixt, 1, 1)

    load_wi.wait()
    load_wo.wait()

    def turn_in(i, carry):
        r = pl.multiple_of(i * 128, 128)
        wit[:, pl.ds(r, 128)] = wi[pl.ds(r, 128), :].astype(F32).T.astype(BF16)
        return carry

    def turn_out(i, carry):
        r = pl.multiple_of(i * 128, 128)
        wot[:, pl.ds(r, 128)] = wo[pl.ds(r, 128), :].astype(F32).T.astype(BF16)
        return carry

    lax.fori_loop(0, CH // 128, turn_in, 0)
    gather_forward(cott, 0, ((0, 3), (1, 1)))
    lax.fori_loop(0, HID // 128, turn_out, 0)
    gather_forward(cott, 0, ((0, 2), (1, 2)))
    gather_relay(mixt, 1)
    gather_wait(cott, 0, 0)
    gather_wait(cott, 0, 1)
    for n, w in TILES:
        dht[:, n : n + w] = dot(wo[...], cott[:, n : n + w], (1, 0))

    gather_forward(mixt, 1, ((0, 3), (1, 1), (0, 2)))
    for part in range(2):
        if part == 1:
            gather_forward(mixt, 1, ((1, 2),))
        gather_wait(mixt, 1, part)
        first, width = CHUNKS[part]
        for n, w in TILES:
            if first <= n < first + width:
                pret[:, n : n + w] = dot(wit[...], mixt[:, n : n + w], (1, 0))

        def unit(i, carry, first=first, width=width):
            r = pl.ds(pl.multiple_of(i * 16, 16), 16)
            pre = pret[r, first : first + width]
            upper = 0.5 * (1.0 + lax.erf(pre * (1.0 / math.sqrt(2.0))))
            bell = jnp.exp(-0.5 * pre * pre) * (1.0 / math.sqrt(2.0 * math.pi))
            hidt[r, first : first + width] = (pre * upper).astype(BF16)
            slope = upper + pre * bell
            dpret[r, first : first + width] = (dht[r, first : first + width] * slope).astype(BF16)
            return carry

        lax.fori_loop(0, HID // 16, unit, 0)

    def pair_send(buf, got, which):
        for d in (1, 2, 3, 0):
            block = 2 * ((x + d) % NX) + 1 - k
            send(buf.at[rows(block)], got.at[d], rss.at[which, d], rsr.at[which, d], partner)

    def pair_sum(buf, got, out, landed, which):
        for d in (2, 1, 3, 0):
            await_bytes(got.at[d], rsr.at[which, d])
            if d:
                block = 2 * ((x + d) % NX) + k
                out[d - 1] = (buf[rows(block)].astype(F32) + got[d].astype(F32)).astype(BF16)
                send(out.at[d - 1], landed.at[d - 1], rss.at[which, 3 + d], rsr.at[which, 3 + d], xpeer(d))

    def chan_wait(landed, which):
        for d in range(1, NX):
            await_bytes(landed.at[d - 1], rsr.at[which, 3 + d])

    def chan_sum(buf, got, landed, lanes):
        total = buf[rows(c), lanes].astype(F32) + got[0, :, lanes].astype(F32)
        for d in range(1, NX):
            total = total + landed[d - 1, :, lanes].astype(F32)
        return total

    def pair_done(got, which):
        for i in range(7):
            await_bytes(got.at[0], rss.at[which, i])

    def start(i):
        base = SROWS * i
        if ZFIRST[i]:
            n, per, peer, me = NZ, SROWS // NZ, zpeer, z
        else:
            n, per, peer, me = NY, SROWS // NY, ypeer, y
        return base, n, per, peer, me

    def span(i, q, off=0, size=None):
        base, n, per, peer, me = start(i)
        place = base + per * ((me + q + n) % n) + off
        return pl.ds(pl.multiple_of(place, 32), per if size is None else size)

    def hop_table(i):
        if ZFIRST[i]:
            half = SROWS // NZ // 2
            full = 2 * half
            far = [(-3, 0, full, -1), (-4, 0, half, -2), (3, 0, full, 1), (4, half, half, 2)]
            near = [(-1, 0, full, -1, 0), (1, 0, full, 1, full)]
            relay = [(-2, 0, full, -2, 2 * full), (2, 0, full, 2, 3 * full)]
            return full, half, far, near, relay
        half = SROWS // NY // 2
        full = 2 * half
        far = [(2, 0, half, 1), (2, half, half, -1)]
        near = [(1, half, half, 1, half), (-1, 0, half, -1, full)]
        relay = [(1, 0, half, 1, 0), (-1, half, half, -1, full + half)]
        return full, half, far, near, relay

    def stream_rs1(i):
        base, n, per, peer, me = start(i)
        full, half, far, near, relay = hop_table(i)
        at = 0
        for q, off, size, to in far:
            send(gp.at[span(i, q, off, size)], far_r.at[i, pl.ds(at, size)], ars.at[i, 0], arr.at[i, 0], peer(to % n))
            at += size
        for q, off, size, to, place in near:
            send(
                gp.at[span(i, q, off, size)], big_r.at[i, pl.ds(place, size)],
                ars.at[i, 4], arr.at[i, 4], peer(to % n),
            )

    def far_rows(i):
        return far_r.at[i, pl.ds(0, 192 if ZFIRST[i] else 128)]

    def big_rows(i):
        return big_r.at[i, pl.ds(0, 256)]

    def stream_rs1b(i):
        base, n, per, peer, me = start(i)
        full, half, far, near, relay = hop_table(i)
        await_bytes(far_rows(i), arr.at[i, 0])
        if ZFIRST[i]:
            low = gp[span(i, -2)].astype(F32) + far_r[i, 0:full].astype(F32)
            relay_s[i, 0:half] = (low[0:half] + far_r[i, full : full + half].astype(F32)).astype(BF16)
            relay_s[i, half:full] = low[half:].astype(BF16)
            high = gp[span(i, 2)].astype(F32) + far_r[i, full + half : 2 * full + half].astype(F32)
            relay_s[i, full : full + half] = high[0:half].astype(BF16)
            relay_s[i, full + half : 2 * full] = (
                high[half:] + far_r[i, 2 * full + half : 3 * full].astype(F32)
            ).astype(BF16)
        else:
            up = gp[span(i, 1, 0, half)].astype(F32) + far_r[i, 0:half].astype(F32)
            relay_s[i, 0:half] = up.astype(BF16)
            down = gp[span(i, -1, half, half)].astype(F32) + far_r[i, half:full].astype(F32)
            relay_s[i, half:full] = down.astype(BF16)
        at = 0
        for q, off, size, to, place in relay:
            send(
                relay_s.at[i, pl.ds(at, size)], big_r.at[i, pl.ds(place, size)],
                ars.at[i, 5], arr.at[i, 4], peer(to % n),
            )
            at += size

    def second(i):
        if ZFIRST[i]:
            return NY, ypeer, y
        return NZ, zpeer, z

    def stream_rs2(i):
        base, n, per, peer, me = start(i)
        await_bytes(big_rows(i), arr.at[i, 4])
        total = gp[span(i, 0)].astype(F32)
        for d in range(256 // per):
            total = total + big_r[i, per * d : per * (d + 1)].astype(F32)
        mid_s[i, 0:per] = total.astype(BF16)
        n2, peer2, me2 = second(i)
        for d in range(1, n2):
            there = pl.multiple_of(16 * ((me2 + d) % n2), 16)
            send(
                mid_s.at[i, pl.ds(there, 16)], mid_r.at[i, pl.ds(16 * (d - 1), 16)],
                ars.at[i, 1], arr.at[i, 1], peer2(d),
            )

    def stream_ag1(i):
        n2, peer2, me2 = second(i)
        await_bytes(mid_r.at[i, pl.ds(0, 16 * (n2 - 1))], arr.at[i, 1])
        mine = pl.ds(pl.multiple_of(16 * me2, 16), 16)
        total = mid_s[i, mine].astype(F32)
        for d in range(1, n2):
            total = total + mid_r[i, 16 * (d - 1) : 16 * d].astype(F32)
        fin_s[i, mine] = total.astype(BF16)
        for d in range(1, n2):
            send(fin_s.at[i, mine], fin_s.at[i, mine], ars.at[i, 2], arr.at[i, 2], peer2(d))

    def stream_ag2(i):
        base, n, per, peer, me = start(i)
        n2, peer2, me2 = second(i)
        await_bytes(fin_s.at[i, pl.ds(0, 16 * (n2 - 1))], arr.at[i, 2])
        half = per // 2
        for off, to in spread(i):
            send(
                fin_s.at[i, pl.ds(off, half)], g_hbm.at[span(i, 0, off, half)],
                ars.at[i, 3], arr.at[i, 3] if relayed(i, off, to) else arr.at[i, 5], peer(to % n),
            )
        pltpu.make_async_copy(fin_s.at[i, pl.ds(0, per)], g_hbm.at[span(i, 0)], lsem.at[2 + i]).start()

    def spread(i):
        half = SROWS // NZ // 2 if ZFIRST[i] else SROWS // NY // 2
        if ZFIRST[i]:
            return [(off, to) for to in (2, -2, 1, -1) for off in (0, half)]
        return [(0, 1), (half, -1), (half, 1), (0, -1)]

    def relayed(i, off, to):
        return abs(to) == 2 if ZFIRST[i] else (off == 0) == (to == 1)

    def stream_ag2b(i):
        base, n, per, peer, me = start(i)
        half = per // 2
        await_bytes(fin_s.at[i, pl.ds(0, 128)], arr.at[i, 3])
        if ZFIRST[i]:
            onward = [(-2, 0, per, 1), (2, 0, per, -1), (-2, 0, half, 2), (2, half, half, -2)]
        else:
            onward = [(-1, 0, half, 1), (1, half, half, -1)]
        for q, off, size, to in onward:
            block = g_hbm.at[span(i, q, off, size)]
            send(block, block, ars.at[i, 6], arr.at[i, 6], peer(to % n))

    def stream_end(i):
        base, n, per, peer, me = start(i)
        n2, peer2, me2 = second(i)
        small = mid_r.at[i, pl.ds(0, 16 * (n2 - 1))]
        onward = far_rows(i)
        await_bytes(g_hbm.at[pl.ds(base, 128)], arr.at[i, 5])
        await_bytes(g_hbm.at[pl.ds(base, 192 if ZFIRST[i] else 128)], arr.at[i, 6])
        await_bytes(onward, ars.at[i, 0])
        await_bytes(relay_s.at[i, pl.ds(0, 128)], ars.at[i, 4])
        await_bytes(relay_s.at[i, pl.ds(0, 128)], ars.at[i, 5])
        await_bytes(small, ars.at[i, 1])
        await_bytes(small, ars.at[i, 2])
        await_bytes(big_rows(i), ars.at[i, 3])
        await_bytes(onward, ars.at[i, 6])
        await_bytes(fin_s.at[i, pl.ds(0, per)], lsem.at[2 + i])

    for half in range(2):
        for n, w in HALVES:
            cot_tile = cott[HID * half + n : HID * half + n + w]
            gp[HID * half : HID * half + HID, n : n + w] = dot(hidt[...], cot_tile, (1, 1)).astype(BF16)
    stream_rs1(1)
    stream_rs1(0)
    for n, w in TILES:
        pb[:, n : n + w] = dot(wi[...], dpret[:, n : n + w], (1, 0)).astype(BF16)
    pair_send(pb, rdb, 0)
    for n, w in HALVES:
        gp[CH : 2 * CH, n : n + w] = dot(mixt[...], dpret[n : n + w], (1, 1)).astype(BF16)
    stream_rs1(2)
    stream_rs1b(1)
    for n, w in TILES:
        po[:, n : n + w] = dot(wot[...], hidt[:, n : n + w], (1, 0)).astype(BF16)
    pair_send(po, rdo, 1)
    pair_sum(pb, rdb, psb, rxb, 0)
    stream_rs1(3)
    stream_rs1b(2)
    stream_rs1b(0)
    stream_rs2(1)
    stream_rs1(4)
    stream_rs1b(3)
    stream_rs2(2)
    pair_sum(po, rdo, pso, rxo, 1)
    stream_rs2(0)
    stream_ag1(1)
    stream_rs1b(4)
    stream_rs2(3)
    stream_ag1(2)
    stream_ag2(1)

    chan_wait(rxb, 0)
    dmp[COLS : COLS * (ROWS + 1), OWN:LANES] = jnp.zeros((PIX, LANES - OWN), BF16)
    for p in range(PIX // 128):
        lanes = slice(128 * p, 128 * p + 128)
        total = cott[rows(c), lanes].astype(F32) + chan_sum(pb, rdb, rxb, lanes)
        dmp[COLS + 128 * p : COLS + 128 * p + 128, 0:OWN] = total.T.astype(BF16)
    send(dmp.at[pl.ds(COLS * ROWS, COLS)], dmp.at[pl.ds(0, COLS)], hs.at[2], hr.at[2], below)
    send(dmp.at[pl.ds(COLS, COLS)], dmp.at[pl.ds(COLS * (ROWS + 1), COLS)], hs.at[3], hr.at[3], above)

    for h in range(ROWS):
        v = dmp[COLS * (h + 1) : COLS * (h + 2)].astype(F32)
        dcat[COLS * h : COLS * (h + 1), 0:LANES] = earlier(v).astype(BF16)
        dcat[COLS * h : COLS * (h + 1), LANES : 2 * LANES] = dmp[COLS * (h + 1) : COLS * (h + 2)]
        dcat[COLS * h : COLS * (h + 1), 2 * LANES :] = later(v).astype(BF16)
    lane_group = lax.broadcasted_iota(jnp.int32, (GROUP, LANES), 1) // GROUP
    gks[GK_ROWS:GK_PAD] = jnp.zeros((GK_PAD - GK_ROWS, LANES), BF16)
    for a in range(3):
        full = dot(xp[COLS * a : COLS * a + PIX], dcat[...], (0, 0))
        for b in range(3):
            part = jnp.zeros((GROUP, LANES), F32)
            for g in range(OWN // GROUP):
                piece = full[GROUP * g : GROUP * (g + 1), LANES * b : LANES * (b + 1)]
                part = part + jnp.where(lane_group == g, piece, 0.0)
            gks[GROUP * (3 * a + b) : GROUP * (3 * a + b + 1)] = part.astype(BF16)
    for d in range(1, NY):
        send(gks, gkr_y.at[d - 1], gss.at[0], gsr.at[0], ypeer(d))

    stream_rs2(4)
    stream_ag1(3)
    stream_ag1(0)
    stream_ag2(2)
    stream_ag2b(1)

    await_bytes(dmp.at[pl.ds(0, COLS)], hr.at[2])
    await_bytes(dmp.at[pl.ds(0, COLS)], hr.at[3])
    top = dmp[0:COLS].astype(F32)
    dmp[0:COLS] = jnp.where(s > 0, top, 0.0).astype(BF16)
    end = dmp[COLS * (ROWS + 1) : COLS * (ROWS + 2)].astype(F32)
    dmp[COLS * (ROWS + 1) : COLS * (ROWS + 2)] = jnp.where(s < last, end, 0.0).astype(BF16)

    def back_row(h, carry):
        base = pl.multiple_of(h * COLS, COLS)
        sums = []
        for b in range(3):
            total = None
            for a in range(3):
                u = dmp[pl.ds(base + (2 - a) * COLS, COLS)]
                term = dot(u, dense[a, :, LANES * b : LANES * (b + 1)], (1, 1))
                total = term if total is None else total + term
            sums.append(total)
        out = earlier(sums[0]) + sums[1] + later(sums[2])
        out = out + dmp[pl.ds(base + COLS, COLS)].astype(F32)
        gf_ref[h] = out.T[0:OWN].astype(BF16)
        return carry

    lax.fori_loop(0, ROWS, back_row, 0)

    stream_ag1(4)
    stream_ag2(3)
    stream_ag2(0)
    stream_ag2b(2)

    await_bytes(gkr_y, gsr.at[0])
    total = gks[...].astype(F32)
    for d in range(1, NY):
        total = total + gkr_y[d - 1].astype(F32)
    gk1[...] = total.astype(BF16)
    per = GK_PAD // NZ
    for d in range(1, NZ):
        there = pl.multiple_of(per * ((z + d) % NZ), 16)
        send(gk1.at[pl.ds(there, per)], gkr_z.at[pl.ds(per * (d - 1), per)], gss.at[1], gsr.at[1], zpeer(d))

    stream_ag2(4)
    stream_ag2b(3)
    stream_ag2b(0)

    chan_wait(rxo, 1)
    total = chan_sum(po, rdo, rxo, slice(0, PIX)) + mixt[rows(c), :].astype(F32)
    for h in range(ROWS):
        bo_ref[h] = total[:, COLS * h : COLS * (h + 1)].astype(BF16)

    await_bytes(gkr_z, gsr.at[1])
    mine = pl.ds(pl.multiple_of(per * z, 16), per)
    total = gk1[mine].astype(F32)
    for d in range(1, NZ):
        total = total + gkr_z[per * (d - 1) : per * d].astype(F32)
    gk2[mine] = total.astype(BF16)
    for d in range(1, NZ):
        send(gk2.at[mine], gk2.at[mine], gss.at[2], gsr.at[2], zpeer(d))
    stream_ag2b(4)

    await_bytes(gk2.at[pl.ds(0, per * (NZ - 1))], gsr.at[2])
    for t in range(9):
        gk_ref[t] = gk2[GROUP * t : GROUP * (t + 1), 0:OWN].astype(F32) * scale

    for i in range(STREAMS):
        stream_end(i)
    gather_done(cott, 0)
    gather_done(mixt, 1)
    pair_done(rdb, 0)
    pair_done(rdo, 1)
    for i in range(2):
        await_bytes(hx.at[i], hs.at[i])
        await_bytes(dmp.at[pl.ds(0, COLS)], hs.at[2 + i])
    await_bytes(gkr_y, gss.at[0])
    await_bytes(gkr_z, gss.at[1])
    await_bytes(gkr_z, gss.at[2])


def finish(
    scale, in_ref, left_ref, right_ref, bo_ref, gf_ref, gk_ref,
    grad_in_ref, grad_out_ref, block_out_ref, features_ref, taps_ref,
):
    block_out_ref[...] = bo_ref[...]
    features_ref[...] = gf_ref[...]
    taps_ref[...] = gk_ref[...]
    grad_in_ref[...] = in_ref[...].astype(F32) * scale
    grad_out_ref[:, 0:HID] = left_ref[...].astype(F32) * scale
    grad_out_ref[:, HID:CH] = right_ref[...].astype(F32) * scale


def turned(cells):
    return jnp.transpose(cells, (0, 2, 1))


def body(feature_map, conv_kernel, weight_in, weight_out, cotangent):
    scale = 1.0 / math.sqrt(ROWS * NZ * NY * COLS)
    vmem = pl.BlockSpec(memory_space=pltpu.VMEM)
    hbm = pl.BlockSpec(memory_space=pl.ANY)

    def run(*refs):
        kernel(scale, *refs)

    per = GK_PAD // NZ
    block_out, grad_features, grad_conv, grads = pl.pallas_call(
        run,
        out_shape=[
            jax.ShapeDtypeStruct((ROWS, OWN, COLS), BF16),
            jax.ShapeDtypeStruct((ROWS, OWN, COLS), BF16),
            jax.ShapeDtypeStruct((9, GROUP, OWN), F32),
            jax.ShapeDtypeStruct((2 * CH, HID), BF16),
        ],
        in_specs=[vmem, vmem, hbm, hbm, vmem],
        out_specs=[vmem, vmem, vmem, hbm],
        scratch_shapes=[
            pltpu.VMEM((COLS * (ROWS + 2), LANES), BF16),
            pltpu.VMEM((2, OWN, COLS), BF16),
            pltpu.VMEM((COLS * (ROWS + 2), LANES), BF16),
            pltpu.VMEM((PIX, 3 * LANES), BF16),
            pltpu.VMEM((3, LANES, 3 * LANES), BF16),
            pltpu.VMEM((PIX, LANES), BF16),
            pltpu.VMEM((CH, HID), BF16),
            pltpu.VMEM((HID, CH), BF16),
            pltpu.VMEM((HID, CH), BF16),
            pltpu.VMEM((CH, HID), BF16),
            pltpu.VMEM((CH, PIX), BF16),
            pltpu.VMEM((CH, PIX), BF16),
            pltpu.VMEM((HID, PIX), F32),
            pltpu.VMEM((HID, PIX), F32),
            pltpu.VMEM((HID, PIX), BF16),
            pltpu.VMEM((HID, PIX), BF16),
            pltpu.VMEM((CH, PIX), BF16),
            pltpu.VMEM((CH, PIX), BF16),
            pltpu.VMEM((NX, OWN, PIX), BF16),
            pltpu.VMEM((NX, OWN, PIX), BF16),
            pltpu.VMEM((NX - 1, OWN, PIX), BF16),
            pltpu.VMEM((NX - 1, OWN, PIX), BF16),
            pltpu.VMEM((NX - 1, OWN, PIX), BF16),
            pltpu.VMEM((NX - 1, OWN, PIX), BF16),
            pltpu.VMEM((2 * CH, HID), BF16),
            pltpu.VMEM((STREAMS, 192, HID), BF16),
            pltpu.VMEM((STREAMS, 128, HID), BF16),
            pltpu.VMEM((STREAMS, 256, HID), BF16),
            pltpu.VMEM((STREAMS, 128, HID), BF16),
            pltpu.VMEM((STREAMS, 112, HID), BF16),
            pltpu.VMEM((STREAMS, 128, HID), BF16),
            pltpu.VMEM((GK_PAD, LANES), BF16),
            pltpu.VMEM((NY - 1, GK_PAD, LANES), BF16),
            pltpu.VMEM((GK_PAD, LANES), BF16),
            pltpu.VMEM((per * (NZ - 1), LANES), BF16),
            pltpu.VMEM((GK_PAD, LANES), BF16),
            pltpu.SemaphoreType.DMA((2 + STREAMS,)),
            pltpu.SemaphoreType.DMA((4,)),
            pltpu.SemaphoreType.DMA((4,)),
            pltpu.SemaphoreType.DMA((2, 2, 7)),
            pltpu.SemaphoreType.DMA((2, 2, 7)),
            pltpu.SemaphoreType.DMA((2, 7)),
            pltpu.SemaphoreType.DMA((2, 7)),
            pltpu.SemaphoreType.DMA((STREAMS, 7)),
            pltpu.SemaphoreType.DMA((STREAMS, 7)),
            pltpu.SemaphoreType.DMA((3,)),
            pltpu.SemaphoreType.DMA((3,)),
        ],
        compiler_params=pltpu.CompilerParams(
            collective_id=0, has_side_effects=True, vmem_limit_bytes=60 << 20
        ),
    )(turned(feature_map), conv_kernel, weight_in, weight_out, turned(cotangent))
    steps = ROWS
    halves = pl.BlockSpec((HID // steps, HID), lambda i: (i, 0))
    row = pl.BlockSpec((1, OWN, COLS), lambda i: (i, 0, 0))
    taps = pl.BlockSpec((9, GROUP, OWN), lambda i: (0, 0, 0))
    grad_in, grad_out, block_out, grad_features, grad_conv = pl.pallas_call(
        lambda *refs: finish(scale, *refs),
        grid=(steps,),
        out_shape=[
            jax.ShapeDtypeStruct((CH, HID), F32),
            jax.ShapeDtypeStruct((HID, CH), F32),
            jax.ShapeDtypeStruct((ROWS, OWN, COLS), BF16),
            jax.ShapeDtypeStruct((ROWS, OWN, COLS), BF16),
            jax.ShapeDtypeStruct((9, GROUP, OWN), F32),
        ],
        in_specs=[
            pl.BlockSpec((CH // steps, HID), lambda i: (steps + i, 0)),
            halves,
            pl.BlockSpec((HID // steps, HID), lambda i: (steps + i, 0)),
            row, row, taps,
        ],
        out_specs=[
            pl.BlockSpec((CH // steps, HID), lambda i: (i, 0)),
            pl.BlockSpec((HID // steps, CH), lambda i: (i, 0)),
            row, row, taps,
        ],
        compiler_params=pltpu.CompilerParams(vmem_limit_bytes=60 << 20),
    )(grads, grads, grads, block_out, grad_features, grad_conv)
    return turned(block_out), turned(grad_features), grad_conv, grad_in, grad_out


def solution(mesh):
    return jax.shard_map(
        body,
        mesh=mesh,
        in_specs=(
            P("space", None, "chan"),
            P(None, None, "chan"),
            P(None, "chan"),
            P("chan", None),
            P("space", None, "chan"),
        ),
        out_specs=(
            P("space", None, "chan"),
            P("space", None, "chan"),
            P(None, None, "chan"),
            P(None, "chan"),
            P("chan", None),
        ),
        check_vma=False,
    )
```

```python
import math

import jax
import jax.numpy as jnp
from jax import lax
from jax.experimental import pallas as pl
from jax.experimental.pallas import tpu as pltpu
from jax.sharding import PartitionSpec as P

MESH = pl.DeviceIdType.MESH
F32 = jnp.float32
BF16 = jnp.bfloat16

NZ, NY, NX = 8, 4, 4
ROWS, COLS, OWN, GROUP = 4, 224, 160, 32
PIX = ROWS * COLS
CH, HID = 1280, 640
LANES = 256
CHUNKS = ((0, 512), (512, 384))
TILES = ((0, 256), (256, 256), (512, 256), (768, 128))
HALVES = ((0, 256), (256, 256), (512, 128))
STREAMS = 5
SROWS = 512
ZFIRST = (True, False, False, False, False)
GK_ROWS = 9 * GROUP
GK_PAD = 384


def dot(a, b, dims):
    return lax.dot_general(a, b, ((dims[:1], dims[1:]), ((), ())), preferred_element_type=F32)


def gelu_slope(values):
    return 0.5 * (1.0 + lax.erf(values * (1.0 / math.sqrt(2.0)))) + values * jnp.exp(
        -0.5 * values * values
    ) * (1.0 / math.sqrt(2.0 * math.pi))


def kernel(
    scale,
    x_ref, ck_ref, wi_hbm, wo_hbm, cot_ref,
    bo_ref, gf_ref, gk_ref, g_hbm,
    xp, hx, dmp, dcat, dense, mixp, wi, wo, wit, wot, cott, mixt, dht, pret, hidt, dpret,
    pb, po, rdb, rdo, psb, pso, rxb, rxo,
    gp, far_r, relay_s, big_r, mid_s, mid_r, fin_s, gks, gkr_y, gk1, gkr_z, gk2,
    lsem, hs, hr, ags, agr, rss, rsr, ars, arr, gss, gsr,
):
    s = lax.axis_index("space")
    c = lax.axis_index("chan")
    z, y, x, k = s // NY, s % NY, c // 2, c % 2
    partner = {"space": s, "chan": 2 * x + 1 - k}
    above = {"space": (s + 31) % 32, "chan": c}
    below = {"space": (s + 1) % 32, "chan": c}

    def xpeer(d):
        return {"space": s, "chan": 2 * ((x + d) % NX) + k}

    def ypeer(d):
        return {"space": z * NY + (y + d) % NY, "chan": c}

    def zpeer(d):
        return {"space": ((z + d) % NZ) * NY + y, "chan": c}

    def send(src, dst, ssem, rsem, dev):
        copy = pltpu.make_async_remote_copy(
            src_ref=src, dst_ref=dst, send_sem=ssem, recv_sem=rsem, device_id=dev, device_id_type=MESH
        )
        copy.start()

    def await_bytes(ref, sem):
        pltpu.make_async_copy(ref, ref, sem).wait()

    def rows(block):
        return pl.ds(pl.multiple_of(block * OWN, 32), OWN)

    load_wi = pltpu.make_async_copy(wi_hbm, wi, lsem.at[0])
    load_wo = pltpu.make_async_copy(wo_hbm, wo, lsem.at[1])
    load_wi.start()
    load_wo.start()
    barrier = pltpu.get_barrier_semaphore()
    peers = [partner, above, below]
    peers += [xpeer(d) for d in range(1, NX)]
    peers += [ypeer(d) for d in range(1, NY)]
    peers += [zpeer(d) for d in range(1, NZ)]
    for dev in peers:
        pl.semaphore_signal(barrier, inc=1, device_id=dev, device_id_type=MESH)

    own_cot = jnp.concatenate([cot_ref[h].astype(F32) for h in range(ROWS)], axis=1)
    cott[rows(c), :] = own_cot.astype(BF16)
    pl.semaphore_wait(barrier, len(peers))

    send(x_ref.at[ROWS - 1], hx.at[0], hs.at[0], hr.at[0], below)
    send(x_ref.at[0], hx.at[1], hs.at[1], hr.at[1], above)

    def gather_send(buf, which, part):
        lanes = pl.ds(CHUNKS[part][0], CHUNKS[part][1])
        own = buf.at[rows(c), lanes]
        for d in (1, 3) if part == 0 else (3, 1):
            send(own, own, ags.at[which, part, d - 1], agr.at[which, part, d - 1], xpeer(d))
        send(own, own, ags.at[which, part, 3], agr.at[which, part, 3], partner)

    def gather_block(buf, which, part, d):
        lanes = pl.ds(CHUNKS[part][0], CHUNKS[part][1])
        got = buf.at[rows(2 * ((x + NX - d) % NX) + k), lanes]
        await_bytes(got, agr.at[which, part, d - 1])
        return got

    def gather_relay(buf, which):
        for part, d in ((0, 1), (1, 3)):
            got = gather_block(buf, which, part, d)
            send(got, got, ags.at[which, part, 1], agr.at[which, part, 1], xpeer(d))
            send(got, got, ags.at[which, part, 3 + d], agr.at[which, part, 3 + d], partner)

    def gather_forward(buf, which, pairs):
        for part, d in pairs:
            got = gather_block(buf, which, part, d)
            send(got, got, ags.at[which, part, 3 + d], agr.at[which, part, 3 + d], partner)

    def gather_wait(buf, which, part):
        lanes = pl.ds(CHUNKS[part][0], CHUNKS[part][1])
        for d in (0, 1, 3, 2):
            got = buf.at[rows(2 * ((x + NX - d) % NX) + 1 - k), lanes]
            await_bytes(got, agr.at[which, part, 3 + d])

    def gather_done(buf, which):
        for part in range(2):
            lanes = pl.ds(CHUNKS[part][0], CHUNKS[part][1])
            for i in range(7):
                await_bytes(buf.at[pl.ds(0, OWN), lanes], ags.at[which, part, i])

    gather_send(cott, 0, 0)
    gather_send(cott, 0, 1)

    xp[:, OWN:LANES] = jnp.zeros((COLS * (ROWS + 2), LANES - OWN), BF16)
    for h in range(ROWS):
        xp[COLS * (h + 1) : COLS * (h + 2), 0:OWN] = x_ref[h].astype(F32).T.astype(BF16)

    row_group = lax.broadcasted_iota(jnp.int32, (OWN, OWN), 0) // GROUP
    col_group = lax.broadcasted_iota(jnp.int32, (OWN, OWN), 1) // GROUP
    same = row_group == col_group
    dense[...] = jnp.zeros_like(dense)
    for t in range(9):
        tap = ck_ref[t].astype(F32)
        full = jnp.where(same, jnp.concatenate([tap] * (OWN // GROUP), axis=0), 0.0)
        dense[t // 3, 0:OWN, LANES * (t % 3) : LANES * (t % 3) + OWN] = full.astype(BF16)

    column = lax.broadcasted_iota(jnp.int32, (COLS, LANES), 0)

    def later(v):
        return jnp.where(column == 0, 0.0, pltpu.roll(v, 1, 0))

    def earlier(v):
        return jnp.where(column == COLS - 1, 0.0, pltpu.roll(v, COLS - 1, 0))

    last = NZ * NY - 1
    await_bytes(hx.at[0], hr.at[0])
    xp[0:COLS, 0:OWN] = jnp.where(s > 0, hx[0].astype(F32).T, 0.0).astype(BF16)
    await_bytes(hx.at[1], hr.at[1])
    below_row = jnp.where(s < last, hx[1].astype(F32).T, 0.0)
    xp[COLS * (ROWS + 1) : COLS * (ROWS + 2), 0:OWN] = below_row.astype(BF16)

    gather_relay(cott, 0)

    def conv_row(h, carry):
        base = pl.multiple_of(h * COLS, COLS)
        total = dot(xp[pl.ds(base, COLS)], dense[0], (1, 0))
        total += dot(xp[pl.ds(base + COLS, COLS)], dense[1], (1, 0))
        total += dot(xp[pl.ds(base + 2 * COLS, COLS)], dense[2], (1, 0))
        out = later(total[:, 0:LANES]) + total[:, LANES : 2 * LANES] + earlier(total[:, 2 * LANES :])
        mixp[pl.ds(base, COLS)] = (xp[pl.ds(base + COLS, COLS)].astype(F32) + out).astype(BF16)
        return carry

    lax.fori_loop(0, ROWS, conv_row, 0)
    for p in range(PIX // 128):
        block = mixp[128 * p : 128 * p + 128].astype(F32).T
        mixt[rows(c), 128 * p : 128 * p + 128] = block[0:OWN].astype(BF16)
        if p == 3:
            gather_send(mixt, 1, 0)
    gather_send(mixt, 1, 1)

    load_wi.wait()
    load_wo.wait()

    def turn_in(i, carry):
        r = pl.multiple_of(i * 128, 128)
        wit[:, pl.ds(r, 128)] = wi[pl.ds(r, 128), :].astype(F32).T.astype(BF16)
        return carry

    def turn_out(i, carry):
        r = pl.multiple_of(i * 128, 128)
        wot[:, pl.ds(r, 128)] = wo[pl.ds(r, 128), :].astype(F32).T.astype(BF16)
        return carry

    lax.fori_loop(0, CH // 128, turn_in, 0)
    gather_forward(cott, 0, ((0, 3), (1, 1)))
    lax.fori_loop(0, HID // 128, turn_out, 0)
    gather_forward(cott, 0, ((0, 2), (1, 2)))
    gather_relay(mixt, 1)
    gather_wait(cott, 0, 0)
    gather_wait(cott, 0, 1)
    for n, w in TILES:
        dht[:, n : n + w] = dot(wo[...], cott[:, n : n + w], (1, 0))

    gather_forward(mixt, 1, ((0, 3), (1, 1), (0, 2)))
    for part in range(2):
        if part == 1:
            gather_forward(mixt, 1, ((1, 2),))
        gather_wait(mixt, 1, part)
        first, width = CHUNKS[part]
        for n, w in TILES:
            if first <= n < first + width:
                pret[:, n : n + w] = dot(wit[...], mixt[:, n : n + w], (1, 0))

        def unit(i, carry, first=first, width=width):
            r = pl.ds(pl.multiple_of(i * 16, 16), 16)
            pre = pret[r, first : first + width]
            upper = 0.5 * (1.0 + lax.erf(pre * (1.0 / math.sqrt(2.0))))
            bell = jnp.exp(-0.5 * pre * pre) * (1.0 / math.sqrt(2.0 * math.pi))
            hidt[r, first : first + width] = (pre * upper).astype(BF16)
            slope = upper + pre * bell
            dpret[r, first : first + width] = (dht[r, first : first + width] * slope).astype(BF16)
            return carry

        lax.fori_loop(0, HID // 16, unit, 0)

    def pair_send(buf, got, which):
        for d in (1, 2, 3, 0):
            block = 2 * ((x + d) % NX) + 1 - k
            send(buf.at[rows(block)], got.at[d], rss.at[which, d], rsr.at[which, d], partner)

    def pair_sum(buf, got, out, landed, which):
        for d in (2, 1, 3, 0):
            await_bytes(got.at[d], rsr.at[which, d])
            if d:
                block = 2 * ((x + d) % NX) + k
                out[d - 1] = (buf[rows(block)].astype(F32) + got[d].astype(F32)).astype(BF16)
                send(out.at[d - 1], landed.at[d - 1], rss.at[which, 3 + d], rsr.at[which, 3 + d], xpeer(d))

    def chan_wait(landed, which):
        for d in range(1, NX):
            await_bytes(landed.at[d - 1], rsr.at[which, 3 + d])

    def chan_sum(buf, got, landed, lanes):
        total = buf[rows(c), lanes].astype(F32) + got[0, :, lanes].astype(F32)
        for d in range(1, NX):
            total = total + landed[d - 1, :, lanes].astype(F32)
        return total

    def pair_done(got, which):
        for i in range(7):
            await_bytes(got.at[0], rss.at[which, i])

    def start(i):
        base = SROWS * i
        if ZFIRST[i]:
            n, per, peer, me = NZ, SROWS // NZ, zpeer, z
        else:
            n, per, peer, me = NY, SROWS // NY, ypeer, y
        return base, n, per, peer, me

    def span(i, q, off=0, size=None):
        base, n, per, peer, me = start(i)
        place = base + per * ((me + q + n) % n) + off
        return pl.ds(pl.multiple_of(place, 32), per if size is None else size)

    def hop_table(i):
        if ZFIRST[i]:
            half = SROWS // NZ // 2
            full = 2 * half
            far = [(-3, 0, full, -1), (-4, 0, half, -2), (3, 0, full, 1), (4, half, half, 2)]
            near = [(-1, 0, full, -1, 0), (1, 0, full, 1, full)]
            relay = [(-2, 0, full, -2, 2 * full), (2, 0, full, 2, 3 * full)]
            return full, half, far, near, relay
        half = SROWS // NY // 2
        full = 2 * half
        far = [(2, 0, half, 1), (2, half, half, -1)]
        near = [(1, half, half, 1, half), (-1, 0, half, -1, full)]
        relay = [(1, 0, half, 1, 0), (-1, half, half, -1, full + half)]
        return full, half, far, near, relay

    def stream_rs1(i):
        base, n, per, peer, me = start(i)
        full, half, far, near, relay = hop_table(i)
        at = 0
        for q, off, size, to in far:
            send(gp.at[span(i, q, off, size)], far_r.at[i, pl.ds(at, size)], ars.at[i, 0], arr.at[i, 0], peer(to % n))
            at += size
        for q, off, size, to, place in near:
            send(
                gp.at[span(i, q, off, size)], big_r.at[i, pl.ds(place, size)],
                ars.at[i, 4], arr.at[i, 4], peer(to % n),
            )

    def far_rows(i):
        return far_r.at[i, pl.ds(0, 192 if ZFIRST[i] else 128)]

    def big_rows(i):
        return big_r.at[i, pl.ds(0, 256)]

    def stream_rs1b(i):
        base, n, per, peer, me = start(i)
        full, half, far, near, relay = hop_table(i)
        await_bytes(far_rows(i), arr.at[i, 0])
        if ZFIRST[i]:
            low = gp[span(i, -2)].astype(F32) + far_r[i, 0:full].astype(F32)
            relay_s[i, 0:half] = (low[0:half] + far_r[i, full : full + half].astype(F32)).astype(BF16)
            relay_s[i, half:full] = low[half:].astype(BF16)
            high = gp[span(i, 2)].astype(F32) + far_r[i, full + half : 2 * full + half].astype(F32)
            relay_s[i, full : full + half] = high[0:half].astype(BF16)
            relay_s[i, full + half : 2 * full] = (
                high[half:] + far_r[i, 2 * full + half : 3 * full].astype(F32)
            ).astype(BF16)
        else:
            up = gp[span(i, 1, 0, half)].astype(F32) + far_r[i, 0:half].astype(F32)
            relay_s[i, 0:half] = up.astype(BF16)
            down = gp[span(i, -1, half, half)].astype(F32) + far_r[i, half:full].astype(F32)
            relay_s[i, half:full] = down.astype(BF16)
        at = 0
        for q, off, size, to, place in relay:
            send(
                relay_s.at[i, pl.ds(at, size)], big_r.at[i, pl.ds(place, size)],
                ars.at[i, 5], arr.at[i, 4], peer(to % n),
            )
            at += size

    def second(i):
        if ZFIRST[i]:
            return NY, ypeer, y
        return NZ, zpeer, z

    def stream_rs2(i):
        base, n, per, peer, me = start(i)
        await_bytes(big_rows(i), arr.at[i, 4])
        total = gp[span(i, 0)].astype(F32)
        for d in range(256 // per):
            total = total + big_r[i, per * d : per * (d + 1)].astype(F32)
        mid_s[i, 0:per] = total.astype(BF16)
        n2, peer2, me2 = second(i)
        for d in range(1, n2):
            there = pl.multiple_of(16 * ((me2 + d) % n2), 16)
            send(
                mid_s.at[i, pl.ds(there, 16)], mid_r.at[i, pl.ds(16 * (d - 1), 16)],
                ars.at[i, 1], arr.at[i, 1], peer2(d),
            )

    def stream_ag1(i):
        n2, peer2, me2 = second(i)
        await_bytes(mid_r.at[i, pl.ds(0, 16 * (n2 - 1))], arr.at[i, 1])
        mine = pl.ds(pl.multiple_of(16 * me2, 16), 16)
        total = mid_s[i, mine].astype(F32)
        for d in range(1, n2):
            total = total + mid_r[i, 16 * (d - 1) : 16 * d].astype(F32)
        fin_s[i, mine] = total.astype(BF16)
        for d in range(1, n2):
            send(fin_s.at[i, mine], fin_s.at[i, mine], ars.at[i, 2], arr.at[i, 2], peer2(d))

    def stream_ag2(i):
        base, n, per, peer, me = start(i)
        n2, peer2, me2 = second(i)
        await_bytes(fin_s.at[i, pl.ds(0, 16 * (n2 - 1))], arr.at[i, 2])
        half = per // 2
        for off, to in spread(i):
            send(
                fin_s.at[i, pl.ds(off, half)], g_hbm.at[span(i, 0, off, half)],
                ars.at[i, 3], arr.at[i, 3] if relayed(i, off, to) else arr.at[i, 5], peer(to % n),
            )
        pltpu.make_async_copy(fin_s.at[i, pl.ds(0, per)], g_hbm.at[span(i, 0)], lsem.at[2 + i]).start()

    def spread(i):
        half = SROWS // NZ // 2 if ZFIRST[i] else SROWS // NY // 2
        if ZFIRST[i]:
            return [(off, to) for to in (2, -2, 1, -1) for off in (0, half)]
        return [(0, 1), (half, -1), (half, 1), (0, -1)]

    def relayed(i, off, to):
        return abs(to) == 2 if ZFIRST[i] else (off == 0) == (to == 1)

    def stream_ag2b(i):
        base, n, per, peer, me = start(i)
        half = per // 2
        await_bytes(fin_s.at[i, pl.ds(0, 128)], arr.at[i, 3])
        if ZFIRST[i]:
            onward = [(-2, 0, per, 1), (2, 0, per, -1), (-2, 0, half, 2), (2, half, half, -2)]
        else:
            onward = [(-1, 0, half, 1), (1, half, half, -1)]
        for q, off, size, to in onward:
            block = g_hbm.at[span(i, q, off, size)]
            send(block, block, ars.at[i, 6], arr.at[i, 6], peer(to % n))

    def stream_end(i):
        base, n, per, peer, me = start(i)
        n2, peer2, me2 = second(i)
        small = mid_r.at[i, pl.ds(0, 16 * (n2 - 1))]
        onward = far_rows(i)
        await_bytes(g_hbm.at[pl.ds(base, 128)], arr.at[i, 5])
        await_bytes(g_hbm.at[pl.ds(base, 192 if ZFIRST[i] else 128)], arr.at[i, 6])
        await_bytes(onward, ars.at[i, 0])
        await_bytes(relay_s.at[i, pl.ds(0, 128)], ars.at[i, 4])
        await_bytes(relay_s.at[i, pl.ds(0, 128)], ars.at[i, 5])
        await_bytes(small, ars.at[i, 1])
        await_bytes(small, ars.at[i, 2])
        await_bytes(big_rows(i), ars.at[i, 3])
        await_bytes(onward, ars.at[i, 6])
        await_bytes(fin_s.at[i, pl.ds(0, per)], lsem.at[2 + i])

    for half in range(2):
        for n, w in HALVES:
            cot_tile = cott[HID * half + n : HID * half + n + w]
            gp[HID * half : HID * half + HID, n : n + w] = dot(hidt[...], cot_tile, (1, 1)).astype(BF16)
    stream_rs1(1)
    stream_rs1(0)
    for n, w in TILES:
        pb[:, n : n + w] = dot(wi[...], dpret[:, n : n + w], (1, 0)).astype(BF16)
    pair_send(pb, rdb, 0)
    for n, w in HALVES:
        gp[CH : 2 * CH, n : n + w] = dot(mixt[...], dpret[n : n + w], (1, 1)).astype(BF16)
    stream_rs1(2)
    stream_rs1b(1)
    for n, w in TILES:
        po[:, n : n + w] = dot(wot[...], hidt[:, n : n + w], (1, 0)).astype(BF16)
    pair_send(po, rdo, 1)
    pair_sum(pb, rdb, psb, rxb, 0)
    stream_rs1(3)
    stream_rs1b(2)
    stream_rs1b(0)
    stream_rs2(1)
    stream_rs1(4)
    stream_rs1b(3)
    stream_rs2(2)
    pair_sum(po, rdo, pso, rxo, 1)
    stream_rs2(0)
    stream_ag1(1)
    stream_rs1b(4)
    stream_rs2(3)
    stream_ag1(2)
    stream_ag2(1)

    chan_wait(rxb, 0)
    dmp[COLS : COLS * (ROWS + 1), OWN:LANES] = jnp.zeros((PIX, LANES - OWN), BF16)
    for p in range(PIX // 128):
        lanes = slice(128 * p, 128 * p + 128)
        total = cott[rows(c), lanes].astype(F32) + chan_sum(pb, rdb, rxb, lanes)
        dmp[COLS + 128 * p : COLS + 128 * p + 128, 0:OWN] = total.T.astype(BF16)
    send(dmp.at[pl.ds(COLS * ROWS, COLS)], dmp.at[pl.ds(0, COLS)], hs.at[2], hr.at[2], below)
    send(dmp.at[pl.ds(COLS, COLS)], dmp.at[pl.ds(COLS * (ROWS + 1), COLS)], hs.at[3], hr.at[3], above)

    for h in range(ROWS):
        v = dmp[COLS * (h + 1) : COLS * (h + 2)].astype(F32)
        dcat[COLS * h : COLS * (h + 1), 0:LANES] = earlier(v).astype(BF16)
        dcat[COLS * h : COLS * (h + 1), LANES : 2 * LANES] = dmp[COLS * (h + 1) : COLS * (h + 2)]
        dcat[COLS * h : COLS * (h + 1), 2 * LANES :] = later(v).astype(BF16)
    lane_group = lax.broadcasted_iota(jnp.int32, (GROUP, LANES), 1) // GROUP
    gks[GK_ROWS:GK_PAD] = jnp.zeros((GK_PAD - GK_ROWS, LANES), BF16)
    for a in range(3):
        full = dot(xp[COLS * a : COLS * a + PIX], dcat[...], (0, 0))
        for b in range(3):
            part = jnp.zeros((GROUP, LANES), F32)
            for g in range(OWN // GROUP):
                piece = full[GROUP * g : GROUP * (g + 1), LANES * b : LANES * (b + 1)]
                part = part + jnp.where(lane_group == g, piece, 0.0)
            gks[GROUP * (3 * a + b) : GROUP * (3 * a + b + 1)] = part.astype(BF16)
    for d in range(1, NY):
        send(gks, gkr_y.at[d - 1], gss.at[0], gsr.at[0], ypeer(d))

    stream_rs2(4)
    stream_ag1(3)
    stream_ag1(0)
    stream_ag2(2)
    stream_ag2b(1)

    await_bytes(dmp.at[pl.ds(0, COLS)], hr.at[2])
    await_bytes(dmp.at[pl.ds(0, COLS)], hr.at[3])
    top = dmp[0:COLS].astype(F32)
    dmp[0:COLS] = jnp.where(s > 0, top, 0.0).astype(BF16)
    end = dmp[COLS * (ROWS + 1) : COLS * (ROWS + 2)].astype(F32)
    dmp[COLS * (ROWS + 1) : COLS * (ROWS + 2)] = jnp.where(s < last, end, 0.0).astype(BF16)

    def back_row(h, carry):
        base = pl.multiple_of(h * COLS, COLS)
        sums = []
        for b in range(3):
            total = None
            for a in range(3):
                u = dmp[pl.ds(base + (2 - a) * COLS, COLS)]
                term = dot(u, dense[a, :, LANES * b : LANES * (b + 1)], (1, 1))
                total = term if total is None else total + term
            sums.append(total)
        out = earlier(sums[0]) + sums[1] + later(sums[2])
        out = out + dmp[pl.ds(base + COLS, COLS)].astype(F32)
        gf_ref[h] = out.T[0:OWN].astype(BF16)
        return carry

    lax.fori_loop(0, ROWS, back_row, 0)

    await_bytes(gkr_y, gsr.at[0])
    total = gks[...].astype(F32)
    for d in range(1, NY):
        total = total + gkr_y[d - 1].astype(F32)
    gk1[...] = total.astype(BF16)
    per = GK_PAD // NZ
    for d in range(1, NZ):
        there = pl.multiple_of(per * ((z + d) % NZ), 16)
        send(gk1.at[pl.ds(there, per)], gkr_z.at[pl.ds(per * (d - 1), per)], gss.at[1], gsr.at[1], zpeer(d))

    stream_ag1(4)
    stream_ag2(3)
    stream_ag2(0)
    stream_ag2b(2)

    stream_ag2(4)
    await_bytes(gkr_z, gsr.at[1])
    mine = pl.ds(pl.multiple_of(per * z, 16), per)
    total = gk1[mine].astype(F32)
    for d in range(1, NZ):
        total = total + gkr_z[per * (d - 1) : per * d].astype(F32)
    gk2[mine] = total.astype(BF16)
    for d in range(1, NZ):
        send(gk2.at[mine], gk2.at[mine], gss.at[2], gsr.at[2], zpeer(d))
    stream_ag2b(3)
    stream_ag2b(0)

    chan_wait(rxo, 1)
    total = chan_sum(po, rdo, rxo, slice(0, PIX)) + mixt[rows(c), :].astype(F32)
    for h in range(ROWS):
        bo_ref[h] = total[:, COLS * h : COLS * (h + 1)].astype(BF16)

    stream_ag2b(4)

    await_bytes(gk2.at[pl.ds(0, per * (NZ - 1))], gsr.at[2])
    for t in range(9):
        gk_ref[t] = gk2[GROUP * t : GROUP * (t + 1), 0:OWN].astype(F32) * scale

    for i in range(STREAMS):
        stream_end(i)
    gather_done(cott, 0)
    gather_done(mixt, 1)
    pair_done(rdb, 0)
    pair_done(rdo, 1)
    for i in range(2):
        await_bytes(hx.at[i], hs.at[i])
        await_bytes(dmp.at[pl.ds(0, COLS)], hs.at[2 + i])
    await_bytes(gkr_y, gss.at[0])
    await_bytes(gkr_z, gss.at[1])
    await_bytes(gkr_z, gss.at[2])


def finish(
    scale, in_ref, left_ref, right_ref, bo_ref, gf_ref, gk_ref,
    grad_in_ref, grad_out_ref, block_out_ref, features_ref, taps_ref,
):
    block_out_ref[...] = bo_ref[...]
    features_ref[...] = gf_ref[...]
    taps_ref[...] = gk_ref[...]
    grad_in_ref[...] = in_ref[...].astype(F32) * scale
    grad_out_ref[:, 0:HID] = left_ref[...].astype(F32) * scale
    grad_out_ref[:, HID:CH] = right_ref[...].astype(F32) * scale


def turned(cells):
    return jnp.transpose(cells, (0, 2, 1))


def body(feature_map, conv_kernel, weight_in, weight_out, cotangent):
    scale = 1.0 / math.sqrt(ROWS * NZ * NY * COLS)
    vmem = pl.BlockSpec(memory_space=pltpu.VMEM)
    hbm = pl.BlockSpec(memory_space=pl.ANY)

    def run(*refs):
        kernel(scale, *refs)

    per = GK_PAD // NZ
    block_out, grad_features, grad_conv, grads = pl.pallas_call(
        run,
        out_shape=[
            jax.ShapeDtypeStruct((ROWS, OWN, COLS), BF16),
            jax.ShapeDtypeStruct((ROWS, OWN, COLS), BF16),
            jax.ShapeDtypeStruct((9, GROUP, OWN), F32),
            jax.ShapeDtypeStruct((2 * CH, HID), BF16),
        ],
        in_specs=[vmem, vmem, hbm, hbm, vmem],
        out_specs=[vmem, vmem, vmem, hbm],
        scratch_shapes=[
            pltpu.VMEM((COLS * (ROWS + 2), LANES), BF16),
            pltpu.VMEM((2, OWN, COLS), BF16),
            pltpu.VMEM((COLS * (ROWS + 2), LANES), BF16),
            pltpu.VMEM((PIX, 3 * LANES), BF16),
            pltpu.VMEM((3, LANES, 3 * LANES), BF16),
            pltpu.VMEM((PIX, LANES), BF16),
            pltpu.VMEM((CH, HID), BF16),
            pltpu.VMEM((HID, CH), BF16),
            pltpu.VMEM((HID, CH), BF16),
            pltpu.VMEM((CH, HID), BF16),
            pltpu.VMEM((CH, PIX), BF16),
            pltpu.VMEM((CH, PIX), BF16),
            pltpu.VMEM((HID, PIX), F32),
            pltpu.VMEM((HID, PIX), F32),
            pltpu.VMEM((HID, PIX), BF16),
            pltpu.VMEM((HID, PIX), BF16),
            pltpu.VMEM((CH, PIX), BF16),
            pltpu.VMEM((CH, PIX), BF16),
            pltpu.VMEM((NX, OWN, PIX), BF16),
            pltpu.VMEM((NX, OWN, PIX), BF16),
            pltpu.VMEM((NX - 1, OWN, PIX), BF16),
            pltpu.VMEM((NX - 1, OWN, PIX), BF16),
            pltpu.VMEM((NX - 1, OWN, PIX), BF16),
            pltpu.VMEM((NX - 1, OWN, PIX), BF16),
            pltpu.VMEM((2 * CH, HID), BF16),
            pltpu.VMEM((STREAMS, 192, HID), BF16),
            pltpu.VMEM((STREAMS, 128, HID), BF16),
            pltpu.VMEM((STREAMS, 256, HID), BF16),
            pltpu.VMEM((STREAMS, 128, HID), BF16),
            pltpu.VMEM((STREAMS, 112, HID), BF16),
            pltpu.VMEM((STREAMS, 128, HID), BF16),
            pltpu.VMEM((GK_PAD, LANES), BF16),
            pltpu.VMEM((NY - 1, GK_PAD, LANES), BF16),
            pltpu.VMEM((GK_PAD, LANES), BF16),
            pltpu.VMEM((per * (NZ - 1), LANES), BF16),
            pltpu.VMEM((GK_PAD, LANES), BF16),
            pltpu.SemaphoreType.DMA((2 + STREAMS,)),
            pltpu.SemaphoreType.DMA((4,)),
            pltpu.SemaphoreType.DMA((4,)),
            pltpu.SemaphoreType.DMA((2, 2, 7)),
            pltpu.SemaphoreType.DMA((2, 2, 7)),
            pltpu.SemaphoreType.DMA((2, 7)),
            pltpu.SemaphoreType.DMA((2, 7)),
            pltpu.SemaphoreType.DMA((STREAMS, 7)),
            pltpu.SemaphoreType.DMA((STREAMS, 7)),
            pltpu.SemaphoreType.DMA((3,)),
            pltpu.SemaphoreType.DMA((3,)),
        ],
        compiler_params=pltpu.CompilerParams(
            collective_id=0, has_side_effects=True, vmem_limit_bytes=60 << 20
        ),
    )(turned(feature_map), conv_kernel, weight_in, weight_out, turned(cotangent))
    steps = 2 * ROWS
    halves = pl.BlockSpec((HID // steps, HID), lambda i: (i, 0))
    row = pl.BlockSpec((1, OWN // 2, COLS), lambda i: (i // 2, i % 2, 0))
    taps = pl.BlockSpec((9, GROUP, OWN), lambda i: (0, 0, 0))
    grad_in, grad_out, block_out, grad_features, grad_conv = pl.pallas_call(
        lambda *refs: finish(scale, *refs),
        grid=(steps,),
        out_shape=[
            jax.ShapeDtypeStruct((CH, HID), F32),
            jax.ShapeDtypeStruct((HID, CH), F32),
            jax.ShapeDtypeStruct((ROWS, OWN, COLS), BF16),
            jax.ShapeDtypeStruct((ROWS, OWN, COLS), BF16),
            jax.ShapeDtypeStruct((9, GROUP, OWN), F32),
        ],
        in_specs=[
            pl.BlockSpec((CH // steps, HID), lambda i: (steps + i, 0)),
            halves,
            pl.BlockSpec((HID // steps, HID), lambda i: (steps + i, 0)),
            row, row, taps,
        ],
        out_specs=[
            pl.BlockSpec((CH // steps, HID), lambda i: (i, 0)),
            pl.BlockSpec((HID // steps, CH), lambda i: (i, 0)),
            row, row, taps,
        ],
        compiler_params=pltpu.CompilerParams(vmem_limit_bytes=60 << 20),
    )(grads, grads, grads, block_out, grad_features, grad_conv)
    return turned(block_out), turned(grad_features), grad_conv, grad_in, grad_out


def solution(mesh):
    return jax.shard_map(
        body,
        mesh=mesh,
        in_specs=(
            P("space", None, "chan"),
            P(None, None, "chan"),
            P(None, "chan"),
            P("chan", None),
            P("space", None, "chan"),
        ),
        out_specs=(
            P("space", None, "chan"),
            P("space", None, "chan"),
            P(None, None, "chan"),
            P(None, "chan"),
            P("chan", None),
        ),
        check_vma=False,
    )
```

```python
import math

import jax
import jax.numpy as jnp
from jax import lax
from jax.experimental import pallas as pl
from jax.experimental.pallas import tpu as pltpu
from jax.sharding import PartitionSpec as P

MESH = pl.DeviceIdType.MESH
F32 = jnp.float32
BF16 = jnp.bfloat16

NZ, NY, NX = 8, 4, 4
ROWS, COLS, OWN, GROUP = 4, 224, 160, 32
PIX = ROWS * COLS
CH, HID = 1280, 640
LANES = 256
CHUNKS = ((0, 512), (512, 384))
TILES = ((0, 256), (256, 256), (512, 256), (768, 128))
HALVES = ((0, 256), (256, 256), (512, 128))
STREAMS = 5
SROWS = 512
ZFIRST = (True, False, False, False, False)
GK_ROWS = 9 * GROUP
GK_PAD = 384


def dot(a, b, dims):
    return lax.dot_general(a, b, ((dims[:1], dims[1:]), ((), ())), preferred_element_type=F32)


def gelu_slope(values):
    return 0.5 * (1.0 + lax.erf(values * (1.0 / math.sqrt(2.0)))) + values * jnp.exp(
        -0.5 * values * values
    ) * (1.0 / math.sqrt(2.0 * math.pi))


def kernel(
    scale,
    x_ref, ck_ref, wi_hbm, wo_hbm, cot_ref,
    bo_ref, gf_ref, gk_ref, g_hbm,
    xp, hx, dmp, dcat, dense, mixp, wi, wo, wit, wot, cott, mixt, dht, pret, hidt, dpret,
    pb, po, rdb, rdo, psb, pso, rxb, rxo,
    gp, far_r, relay_s, big_r, mid_s, mid_r, fin_s, gks, gkr_y, gk1, gkr_z, gk2,
    lsem, hs, hr, ags, agr, rss, rsr, ars, arr, gss, gsr,
):
    s = lax.axis_index("space")
    c = lax.axis_index("chan")
    z, y, x, k = s // NY, s % NY, c // 2, c % 2
    partner = {"space": s, "chan": 2 * x + 1 - k}
    above = {"space": (s + 31) % 32, "chan": c}
    below = {"space": (s + 1) % 32, "chan": c}

    def xpeer(d):
        return {"space": s, "chan": 2 * ((x + d) % NX) + k}

    def ypeer(d):
        return {"space": z * NY + (y + d) % NY, "chan": c}

    def zpeer(d):
        return {"space": ((z + d) % NZ) * NY + y, "chan": c}

    def send(src, dst, ssem, rsem, dev):
        copy = pltpu.make_async_remote_copy(
            src_ref=src, dst_ref=dst, send_sem=ssem, recv_sem=rsem, device_id=dev, device_id_type=MESH
        )
        copy.start()

    def await_bytes(ref, sem):
        pltpu.make_async_copy(ref, ref, sem).wait()

    def rows(block):
        return pl.ds(pl.multiple_of(block * OWN, 32), OWN)

    load_wi = pltpu.make_async_copy(wi_hbm, wi, lsem.at[0])
    load_wo = pltpu.make_async_copy(wo_hbm, wo, lsem.at[1])
    load_wi.start()
    load_wo.start()
    barrier = pltpu.get_barrier_semaphore()
    peers = [partner, above, below]
    peers += [xpeer(d) for d in range(1, NX)]
    peers += [ypeer(d) for d in range(1, NY)]
    peers += [zpeer(d) for d in range(1, NZ)]
    for dev in peers:
        pl.semaphore_signal(barrier, inc=1, device_id=dev, device_id_type=MESH)

    own_cot = jnp.concatenate([cot_ref[h].astype(F32) for h in range(ROWS)], axis=1)
    cott[rows(c), :] = own_cot.astype(BF16)
    pl.semaphore_wait(barrier, len(peers))

    send(x_ref.at[ROWS - 1], hx.at[0], hs.at[0], hr.at[0], below)
    send(x_ref.at[0], hx.at[1], hs.at[1], hr.at[1], above)

    def gather_send(buf, which, part):
        lanes = pl.ds(CHUNKS[part][0], CHUNKS[part][1])
        own = buf.at[rows(c), lanes]
        for d in (1, 3) if part == 0 else (3, 1):
            send(own, own, ags.at[which, part, d - 1], agr.at[which, part, d - 1], xpeer(d))
        send(own, own, ags.at[which, part, 3], agr.at[which, part, 3], partner)

    def gather_block(buf, which, part, d):
        lanes = pl.ds(CHUNKS[part][0], CHUNKS[part][1])
        got = buf.at[rows(2 * ((x + NX - d) % NX) + k), lanes]
        await_bytes(got, agr.at[which, part, d - 1])
        return got

    def gather_relay(buf, which):
        for part, d in ((0, 1), (1, 3)):
            got = gather_block(buf, which, part, d)
            send(got, got, ags.at[which, part, 1], agr.at[which, part, 1], xpeer(d))
            send(got, got, ags.at[which, part, 3 + d], agr.at[which, part, 3 + d], partner)

    def gather_forward(buf, which, pairs):
        for part, d in pairs:
            got = gather_block(buf, which, part, d)
            send(got, got, ags.at[which, part, 3 + d], agr.at[which, part, 3 + d], partner)

    def gather_wait(buf, which, part):
        lanes = pl.ds(CHUNKS[part][0], CHUNKS[part][1])
        for d in (0, 1, 3, 2):
            got = buf.at[rows(2 * ((x + NX - d) % NX) + 1 - k), lanes]
            await_bytes(got, agr.at[which, part, 3 + d])

    def gather_done(buf, which):
        for part in range(2):
            lanes = pl.ds(CHUNKS[part][0], CHUNKS[part][1])
            for i in range(7):
                await_bytes(buf.at[pl.ds(0, OWN), lanes], ags.at[which, part, i])

    gather_send(cott, 0, 0)
    gather_send(cott, 0, 1)

    xp[:, OWN:LANES] = jnp.zeros((COLS * (ROWS + 2), LANES - OWN), BF16)
    for h in range(ROWS):
        xp[COLS * (h + 1) : COLS * (h + 2), 0:OWN] = x_ref[h].astype(F32).T.astype(BF16)

    row_group = lax.broadcasted_iota(jnp.int32, (OWN, OWN), 0) // GROUP
    col_group = lax.broadcasted_iota(jnp.int32, (OWN, OWN), 1) // GROUP
    same = row_group == col_group
    dense[...] = jnp.zeros_like(dense)
    for t in range(9):
        tap = ck_ref[t].astype(F32)
        full = jnp.where(same, jnp.concatenate([tap] * (OWN // GROUP), axis=0), 0.0)
        dense[t // 3, 0:OWN, LANES * (t % 3) : LANES * (t % 3) + OWN] = full.astype(BF16)

    column = lax.broadcasted_iota(jnp.int32, (COLS, LANES), 0)

    def later(v):
        return jnp.where(column == 0, 0.0, pltpu.roll(v, 1, 0))

    def earlier(v):
        return jnp.where(column == COLS - 1, 0.0, pltpu.roll(v, COLS - 1, 0))

    last = NZ * NY - 1
    await_bytes(hx.at[0], hr.at[0])
    xp[0:COLS, 0:OWN] = jnp.where(s > 0, hx[0].astype(F32).T, 0.0).astype(BF16)
    await_bytes(hx.at[1], hr.at[1])
    below_row = jnp.where(s < last, hx[1].astype(F32).T, 0.0)
    xp[COLS * (ROWS + 1) : COLS * (ROWS + 2), 0:OWN] = below_row.astype(BF16)

    gather_relay(cott, 0)

    def conv_row(h, carry):
        base = pl.multiple_of(h * COLS, COLS)
        total = dot(xp[pl.ds(base, COLS)], dense[0], (1, 0))
        total += dot(xp[pl.ds(base + COLS, COLS)], dense[1], (1, 0))
        total += dot(xp[pl.ds(base + 2 * COLS, COLS)], dense[2], (1, 0))
        out = later(total[:, 0:LANES]) + total[:, LANES : 2 * LANES] + earlier(total[:, 2 * LANES :])
        mixp[pl.ds(base, COLS)] = (xp[pl.ds(base + COLS, COLS)].astype(F32) + out).astype(BF16)
        return carry

    lax.fori_loop(0, ROWS, conv_row, 0)
    for p in range(PIX // 128):
        block = mixp[128 * p : 128 * p + 128].astype(F32).T
        mixt[rows(c), 128 * p : 128 * p + 128] = block[0:OWN].astype(BF16)
        if p == 3:
            gather_send(mixt, 1, 0)
    gather_send(mixt, 1, 1)

    load_wi.wait()
    load_wo.wait()

    def turn_in(i, carry):
        r = pl.multiple_of(i * 128, 128)
        wit[:, pl.ds(r, 128)] = wi[pl.ds(r, 128), :].astype(F32).T.astype(BF16)
        return carry

    def turn_out(i, carry):
        r = pl.multiple_of(i * 128, 128)
        wot[:, pl.ds(r, 128)] = wo[pl.ds(r, 128), :].astype(F32).T.astype(BF16)
        return carry

    lax.fori_loop(0, CH // 128, turn_in, 0)
    gather_forward(cott, 0, ((0, 3), (1, 1)))
    lax.fori_loop(0, HID // 128, turn_out, 0)
    gather_forward(cott, 0, ((0, 2), (1, 2)))
    gather_relay(mixt, 1)
    gather_wait(cott, 0, 0)
    gather_wait(cott, 0, 1)
    for n, w in TILES:
        dht[:, n : n + w] = dot(wo[...], cott[:, n : n + w], (1, 0))

    gather_forward(mixt, 1, ((0, 3), (1, 1), (0, 2)))
    for part in range(2):
        if part == 1:
            gather_forward(mixt, 1, ((1, 2),))
        gather_wait(mixt, 1, part)
        first, width = CHUNKS[part]
        for n, w in TILES:
            if first <= n < first + width:
                pret[:, n : n + w] = dot(wit[...], mixt[:, n : n + w], (1, 0))

        def unit(i, carry, first=first, width=width):
            r = pl.ds(pl.multiple_of(i * 16, 16), 16)
            pre = pret[r, first : first + width]
            upper = 0.5 * (1.0 + lax.erf(pre * (1.0 / math.sqrt(2.0))))
            bell = jnp.exp(-0.5 * pre * pre) * (1.0 / math.sqrt(2.0 * math.pi))
            hidt[r, first : first + width] = (pre * upper).astype(BF16)
            slope = upper + pre * bell
            dpret[r, first : first + width] = (dht[r, first : first + width] * slope).astype(BF16)
            return carry

        lax.fori_loop(0, HID // 16, unit, 0)

    def pair_send(buf, got, which):
        for d in (1, 2, 3, 0):
            block = 2 * ((x + d) % NX) + 1 - k
            send(buf.at[rows(block)], got.at[d], rss.at[which, d], rsr.at[which, d], partner)

    def pair_sum(buf, got, out, landed, which):
        for d in (2, 1, 3, 0):
            await_bytes(got.at[d], rsr.at[which, d])
            if d:
                block = 2 * ((x + d) % NX) + k
                out[d - 1] = (buf[rows(block)].astype(F32) + got[d].astype(F32)).astype(BF16)
                send(out.at[d - 1], landed.at[d - 1], rss.at[which, 3 + d], rsr.at[which, 3 + d], xpeer(d))

    def chan_wait(landed, which):
        for d in range(1, NX):
            await_bytes(landed.at[d - 1], rsr.at[which, 3 + d])

    def chan_sum(buf, got, landed, lanes):
        total = buf[rows(c), lanes].astype(F32) + got[0, :, lanes].astype(F32)
        for d in range(1, NX):
            total = total + landed[d - 1, :, lanes].astype(F32)
        return total

    def pair_done(got, which):
        for i in range(7):
            await_bytes(got.at[0], rss.at[which, i])

    def start(i):
        base = SROWS * i
        if ZFIRST[i]:
            n, per, peer, me = NZ, SROWS // NZ, zpeer, z
        else:
            n, per, peer, me = NY, SROWS // NY, ypeer, y
        return base, n, per, peer, me

    def span(i, q, off=0, size=None):
        base, n, per, peer, me = start(i)
        place = base + per * ((me + q + n) % n) + off
        return pl.ds(pl.multiple_of(place, 32), per if size is None else size)

    def hop_table(i):
        if ZFIRST[i]:
            half = SROWS // NZ // 2
            full = 2 * half
            far = [(-3, 0, full, -1), (-4, 0, half, -2), (3, 0, full, 1), (4, half, half, 2)]
            near = [(-1, 0, full, -1, 0), (1, 0, full, 1, full)]
            relay = [(-2, 0, full, -2, 2 * full), (2, 0, full, 2, 3 * full)]
            return full, half, far, near, relay
        half = SROWS // NY // 2
        full = 2 * half
        far = [(2, 0, half, 1), (2, half, half, -1)]
        near = [(1, half, half, 1, half), (-1, 0, half, -1, full)]
        relay = [(1, 0, half, 1, 0), (-1, half, half, -1, full + half)]
        return full, half, far, near, relay

    def stream_rs1(i):
        base, n, per, peer, me = start(i)
        full, half, far, near, relay = hop_table(i)
        at = 0
        for q, off, size, to in far:
            send(gp.at[span(i, q, off, size)], far_r.at[i, pl.ds(at, size)], ars.at[i, 0], arr.at[i, 0], peer(to % n))
            at += size
        for q, off, size, to, place in near:
            send(
                gp.at[span(i, q, off, size)], big_r.at[i, pl.ds(place, size)],
                ars.at[i, 4], arr.at[i, 4], peer(to % n),
            )

    def far_rows(i):
        return far_r.at[i, pl.ds(0, 192 if ZFIRST[i] else 128)]

    def big_rows(i):
        return big_r.at[i, pl.ds(0, 256)]

    def stream_rs1b(i):
        base, n, per, peer, me = start(i)
        full, half, far, near, relay = hop_table(i)
        await_bytes(far_rows(i), arr.at[i, 0])
        if ZFIRST[i]:
            low = gp[span(i, -2)].astype(F32) + far_r[i, 0:full].astype(F32)
            relay_s[i, 0:half] = (low[0:half] + far_r[i, full : full + half].astype(F32)).astype(BF16)
            relay_s[i, half:full] = low[half:].astype(BF16)
            high = gp[span(i, 2)].astype(F32) + far_r[i, full + half : 2 * full + half].astype(F32)
            relay_s[i, full : full + half] = high[0:half].astype(BF16)
            relay_s[i, full + half : 2 * full] = (
                high[half:] + far_r[i, 2 * full + half : 3 * full].astype(F32)
            ).astype(BF16)
        else:
            up = gp[span(i, 1, 0, half)].astype(F32) + far_r[i, 0:half].astype(F32)
            relay_s[i, 0:half] = up.astype(BF16)
            down = gp[span(i, -1, half, half)].astype(F32) + far_r[i, half:full].astype(F32)
            relay_s[i, half:full] = down.astype(BF16)
        at = 0
        for q, off, size, to, place in relay:
            send(
                relay_s.at[i, pl.ds(at, size)], big_r.at[i, pl.ds(place, size)],
                ars.at[i, 5], arr.at[i, 4], peer(to % n),
            )
            at += size

    def second(i):
        if ZFIRST[i]:
            return NY, ypeer, y
        return NZ, zpeer, z

    def stream_rs2(i):
        base, n, per, peer, me = start(i)
        await_bytes(big_rows(i), arr.at[i, 4])
        total = gp[span(i, 0)].astype(F32)
        for d in range(256 // per):
            total = total + big_r[i, per * d : per * (d + 1)].astype(F32)
        mid_s[i, 0:per] = total.astype(BF16)
        n2, peer2, me2 = second(i)
        for d in range(1, n2):
            there = pl.multiple_of(16 * ((me2 + d) % n2), 16)
            send(
                mid_s.at[i, pl.ds(there, 16)], mid_r.at[i, pl.ds(16 * (d - 1), 16)],
                ars.at[i, 1], arr.at[i, 1], peer2(d),
            )

    def stream_ag1(i):
        n2, peer2, me2 = second(i)
        await_bytes(mid_r.at[i, pl.ds(0, 16 * (n2 - 1))], arr.at[i, 1])
        mine = pl.ds(pl.multiple_of(16 * me2, 16), 16)
        total = mid_s[i, mine].astype(F32)
        for d in range(1, n2):
            total = total + mid_r[i, 16 * (d - 1) : 16 * d].astype(F32)
        fin_s[i, mine] = total.astype(BF16)
        for d in range(1, n2):
            send(fin_s.at[i, mine], fin_s.at[i, mine], ars.at[i, 2], arr.at[i, 2], peer2(d))

    def stream_ag2(i):
        base, n, per, peer, me = start(i)
        n2, peer2, me2 = second(i)
        await_bytes(fin_s.at[i, pl.ds(0, 16 * (n2 - 1))], arr.at[i, 2])
        half = per // 2
        for off, to in spread(i):
            send(
                fin_s.at[i, pl.ds(off, half)], g_hbm.at[span(i, 0, off, half)],
                ars.at[i, 3], arr.at[i, 3] if relayed(i, off, to) else arr.at[i, 5], peer(to % n),
            )
        pltpu.make_async_copy(fin_s.at[i, pl.ds(0, per)], g_hbm.at[span(i, 0)], lsem.at[2 + i]).start()

    def spread(i):
        half = SROWS // NZ // 2 if ZFIRST[i] else SROWS // NY // 2
        if ZFIRST[i]:
            return [(off, to) for to in (2, -2, 1, -1) for off in (0, half)]
        return [(0, 1), (half, -1), (half, 1), (0, -1)]

    def relayed(i, off, to):
        return abs(to) == 2 if ZFIRST[i] else (off == 0) == (to == 1)

    def stream_ag2b(i):
        base, n, per, peer, me = start(i)
        half = per // 2
        await_bytes(fin_s.at[i, pl.ds(0, 128)], arr.at[i, 3])
        if ZFIRST[i]:
            onward = [(-2, 0, per, 1), (2, 0, per, -1), (-2, 0, half, 2), (2, half, half, -2)]
        else:
            onward = [(-1, 0, half, 1), (1, half, half, -1)]
        for q, off, size, to in onward:
            block = g_hbm.at[span(i, q, off, size)]
            send(block, block, ars.at[i, 6], arr.at[i, 6], peer(to % n))

    def stream_end(i):
        base, n, per, peer, me = start(i)
        n2, peer2, me2 = second(i)
        small = mid_r.at[i, pl.ds(0, 16 * (n2 - 1))]
        onward = far_rows(i)
        await_bytes(g_hbm.at[pl.ds(base, 128)], arr.at[i, 5])
        await_bytes(g_hbm.at[pl.ds(base, 192 if ZFIRST[i] else 128)], arr.at[i, 6])
        await_bytes(onward, ars.at[i, 0])
        await_bytes(relay_s.at[i, pl.ds(0, 128)], ars.at[i, 4])
        await_bytes(relay_s.at[i, pl.ds(0, 128)], ars.at[i, 5])
        await_bytes(small, ars.at[i, 1])
        await_bytes(small, ars.at[i, 2])
        await_bytes(big_rows(i), ars.at[i, 3])
        await_bytes(onward, ars.at[i, 6])
        await_bytes(fin_s.at[i, pl.ds(0, per)], lsem.at[2 + i])

    for half in range(2):
        for n, w in HALVES:
            cot_tile = cott[HID * half + n : HID * half + n + w]
            gp[HID * half : HID * half + HID, n : n + w] = dot(hidt[...], cot_tile, (1, 1)).astype(BF16)
    stream_rs1(1)
    stream_rs1(0)
    for n, w in TILES:
        pb[:, n : n + w] = dot(wi[...], dpret[:, n : n + w], (1, 0)).astype(BF16)
    pair_send(pb, rdb, 0)
    for n, w in HALVES:
        gp[CH : 2 * CH, n : n + w] = dot(mixt[...], dpret[n : n + w], (1, 1)).astype(BF16)
    stream_rs1(2)
    stream_rs1b(1)
    for n, w in TILES:
        po[:, n : n + w] = dot(wot[...], hidt[:, n : n + w], (1, 0)).astype(BF16)
    pair_send(po, rdo, 1)
    pair_sum(pb, rdb, psb, rxb, 0)
    stream_rs1(3)
    stream_rs1b(2)
    stream_rs1b(0)
    stream_rs2(1)
    stream_rs1(4)
    stream_rs1b(3)
    stream_rs2(2)
    pair_sum(po, rdo, pso, rxo, 1)
    stream_rs2(0)
    stream_ag1(1)
    stream_rs1b(4)
    stream_rs2(3)
    stream_ag1(2)
    stream_ag2(1)

    chan_wait(rxb, 0)
    dmp[COLS : COLS * (ROWS + 1), OWN:LANES] = jnp.zeros((PIX, LANES - OWN), BF16)
    for p in range(PIX // 128):
        lanes = slice(128 * p, 128 * p + 128)
        total = cott[rows(c), lanes].astype(F32) + chan_sum(pb, rdb, rxb, lanes)
        dmp[COLS + 128 * p : COLS + 128 * p + 128, 0:OWN] = total.T.astype(BF16)
    send(dmp.at[pl.ds(COLS * ROWS, COLS)], dmp.at[pl.ds(0, COLS)], hs.at[2], hr.at[2], below)
    send(dmp.at[pl.ds(COLS, COLS)], dmp.at[pl.ds(COLS * (ROWS + 1), COLS)], hs.at[3], hr.at[3], above)

    stream_rs2(4)
    stream_ag1(3)

    for h in range(ROWS):
        v = dmp[COLS * (h + 1) : COLS * (h + 2)].astype(F32)
        dcat[COLS * h : COLS * (h + 1), 0:LANES] = earlier(v).astype(BF16)
        dcat[COLS * h : COLS * (h + 1), LANES : 2 * LANES] = dmp[COLS * (h + 1) : COLS * (h + 2)]
        dcat[COLS * h : COLS * (h + 1), 2 * LANES :] = later(v).astype(BF16)
    lane_group = lax.broadcasted_iota(jnp.int32, (GROUP, LANES), 1) // GROUP
    gks[GK_ROWS:GK_PAD] = jnp.zeros((GK_PAD - GK_ROWS, LANES), BF16)
    for a in range(3):
        full = dot(xp[COLS * a : COLS * a + PIX], dcat[...], (0, 0))
        for b in range(3):
            part = jnp.zeros((GROUP, LANES), F32)
            for g in range(OWN // GROUP):
                piece = full[GROUP * g : GROUP * (g + 1), LANES * b : LANES * (b + 1)]
                part = part + jnp.where(lane_group == g, piece, 0.0)
            gks[GROUP * (3 * a + b) : GROUP * (3 * a + b + 1)] = part.astype(BF16)
    for d in range(1, NY):
        send(gks, gkr_y.at[d - 1], gss.at[0], gsr.at[0], ypeer(d))

    stream_ag1(0)
    stream_ag2(2)
    stream_ag2b(1)

    await_bytes(dmp.at[pl.ds(0, COLS)], hr.at[2])
    await_bytes(dmp.at[pl.ds(0, COLS)], hr.at[3])
    top = dmp[0:COLS].astype(F32)
    dmp[0:COLS] = jnp.where(s > 0, top, 0.0).astype(BF16)
    end = dmp[COLS * (ROWS + 1) : COLS * (ROWS + 2)].astype(F32)
    dmp[COLS * (ROWS + 1) : COLS * (ROWS + 2)] = jnp.where(s < last, end, 0.0).astype(BF16)

    def back_row(h, carry):
        base = pl.multiple_of(h * COLS, COLS)
        sums = []
        for b in range(3):
            total = None
            for a in range(3):
                u = dmp[pl.ds(base + (2 - a) * COLS, COLS)]
                term = dot(u, dense[a, :, LANES * b : LANES * (b + 1)], (1, 1))
                total = term if total is None else total + term
            sums.append(total)
        out = earlier(sums[0]) + sums[1] + later(sums[2])
        out = out + dmp[pl.ds(base + COLS, COLS)].astype(F32)
        gf_ref[h] = out.T[0:OWN].astype(BF16)
        return carry

    lax.fori_loop(0, ROWS, back_row, 0)

    await_bytes(gkr_y, gsr.at[0])
    total = gks[...].astype(F32)
    for d in range(1, NY):
        total = total + gkr_y[d - 1].astype(F32)
    gk1[...] = total.astype(BF16)
    per = GK_PAD // NZ
    for d in range(1, NZ):
        there = pl.multiple_of(per * ((z + d) % NZ), 16)
        send(gk1.at[pl.ds(there, per)], gkr_z.at[pl.ds(per * (d - 1), per)], gss.at[1], gsr.at[1], zpeer(d))

    stream_ag1(4)
    stream_ag2(3)
    stream_ag2(0)
    stream_ag2b(2)

    stream_ag2(4)
    await_bytes(gkr_z, gsr.at[1])
    mine = pl.ds(pl.multiple_of(per * z, 16), per)
    total = gk1[mine].astype(F32)
    for d in range(1, NZ):
        total = total + gkr_z[per * (d - 1) : per * d].astype(F32)
    gk2[mine] = total.astype(BF16)
    for d in range(1, NZ):
        send(gk2.at[mine], gk2.at[mine], gss.at[2], gsr.at[2], zpeer(d))
    stream_ag2b(3)
    stream_ag2b(0)

    chan_wait(rxo, 1)
    total = chan_sum(po, rdo, rxo, slice(0, PIX)) + mixt[rows(c), :].astype(F32)
    for h in range(ROWS):
        bo_ref[h] = total[:, COLS * h : COLS * (h + 1)].astype(BF16)

    stream_ag2b(4)

    await_bytes(gk2.at[pl.ds(0, per * (NZ - 1))], gsr.at[2])
    for t in range(9):
        gk_ref[t] = gk2[GROUP * t : GROUP * (t + 1), 0:OWN].astype(F32) * scale

    for i in range(STREAMS):
        stream_end(i)
    gather_done(cott, 0)
    gather_done(mixt, 1)
    pair_done(rdb, 0)
    pair_done(rdo, 1)
    for i in range(2):
        await_bytes(hx.at[i], hs.at[i])
        await_bytes(dmp.at[pl.ds(0, COLS)], hs.at[2 + i])
    await_bytes(gkr_y, gss.at[0])
    await_bytes(gkr_z, gss.at[1])
    await_bytes(gkr_z, gss.at[2])


def finish(
    scale, in_ref, left_ref, right_ref, bo_ref, gf_ref, gk_ref,
    grad_in_ref, grad_out_ref, block_out_ref, features_ref, taps_ref,
):
    block_out_ref[...] = bo_ref[...]
    features_ref[...] = gf_ref[...]
    taps_ref[...] = gk_ref[...]
    grad_in_ref[...] = in_ref[...].astype(F32) * scale
    grad_out_ref[:, 0:HID] = left_ref[...].astype(F32) * scale
    grad_out_ref[:, HID:CH] = right_ref[...].astype(F32) * scale


def turned(cells):
    return jnp.transpose(cells, (0, 2, 1))


def body(feature_map, conv_kernel, weight_in, weight_out, cotangent):
    scale = 1.0 / math.sqrt(ROWS * NZ * NY * COLS)
    vmem = pl.BlockSpec(memory_space=pltpu.VMEM)
    hbm = pl.BlockSpec(memory_space=pl.ANY)

    def run(*refs):
        kernel(scale, *refs)

    per = GK_PAD // NZ
    block_out, grad_features, grad_conv, grads = pl.pallas_call(
        run,
        out_shape=[
            jax.ShapeDtypeStruct((ROWS, OWN, COLS), BF16),
            jax.ShapeDtypeStruct((ROWS, OWN, COLS), BF16),
            jax.ShapeDtypeStruct((9, GROUP, OWN), F32),
            jax.ShapeDtypeStruct((2 * CH, HID), BF16),
        ],
        in_specs=[vmem, vmem, hbm, hbm, vmem],
        out_specs=[vmem, vmem, vmem, hbm],
        scratch_shapes=[
            pltpu.VMEM((COLS * (ROWS + 2), LANES), BF16),
            pltpu.VMEM((2, OWN, COLS), BF16),
            pltpu.VMEM((COLS * (ROWS + 2), LANES), BF16),
            pltpu.VMEM((PIX, 3 * LANES), BF16),
            pltpu.VMEM((3, LANES, 3 * LANES), BF16),
            pltpu.VMEM((PIX, LANES), BF16),
            pltpu.VMEM((CH, HID), BF16),
            pltpu.VMEM((HID, CH), BF16),
            pltpu.VMEM((HID, CH), BF16),
            pltpu.VMEM((CH, HID), BF16),
            pltpu.VMEM((CH, PIX), BF16),
            pltpu.VMEM((CH, PIX), BF16),
            pltpu.VMEM((HID, PIX), F32),
            pltpu.VMEM((HID, PIX), F32),
            pltpu.VMEM((HID, PIX), BF16),
            pltpu.VMEM((HID, PIX), BF16),
            pltpu.VMEM((CH, PIX), BF16),
            pltpu.VMEM((CH, PIX), BF16),
            pltpu.VMEM((NX, OWN, PIX), BF16),
            pltpu.VMEM((NX, OWN, PIX), BF16),
            pltpu.VMEM((NX - 1, OWN, PIX), BF16),
            pltpu.VMEM((NX - 1, OWN, PIX), BF16),
            pltpu.VMEM((NX - 1, OWN, PIX), BF16),
            pltpu.VMEM((NX - 1, OWN, PIX), BF16),
            pltpu.VMEM((2 * CH, HID), BF16),
            pltpu.VMEM((STREAMS, 192, HID), BF16),
            pltpu.VMEM((STREAMS, 128, HID), BF16),
            pltpu.VMEM((STREAMS, 256, HID), BF16),
            pltpu.VMEM((STREAMS, 128, HID), BF16),
            pltpu.VMEM((STREAMS, 112, HID), BF16),
            pltpu.VMEM((STREAMS, 128, HID), BF16),
            pltpu.VMEM((GK_PAD, LANES), BF16),
            pltpu.VMEM((NY - 1, GK_PAD, LANES), BF16),
            pltpu.VMEM((GK_PAD, LANES), BF16),
            pltpu.VMEM((per * (NZ - 1), LANES), BF16),
            pltpu.VMEM((GK_PAD, LANES), BF16),
            pltpu.SemaphoreType.DMA((2 + STREAMS,)),
            pltpu.SemaphoreType.DMA((4,)),
            pltpu.SemaphoreType.DMA((4,)),
            pltpu.SemaphoreType.DMA((2, 2, 7)),
            pltpu.SemaphoreType.DMA((2, 2, 7)),
            pltpu.SemaphoreType.DMA((2, 7)),
            pltpu.SemaphoreType.DMA((2, 7)),
            pltpu.SemaphoreType.DMA((STREAMS, 7)),
            pltpu.SemaphoreType.DMA((STREAMS, 7)),
            pltpu.SemaphoreType.DMA((3,)),
            pltpu.SemaphoreType.DMA((3,)),
        ],
        compiler_params=pltpu.CompilerParams(
            collective_id=0, has_side_effects=True, vmem_limit_bytes=60 << 20
        ),
    )(turned(feature_map), conv_kernel, weight_in, weight_out, turned(cotangent))
    steps = 2 * ROWS
    halves = pl.BlockSpec((HID // steps, HID), lambda i: (i, 0))
    row = pl.BlockSpec((1, OWN // 2, COLS), lambda i: (i // 2, i % 2, 0))
    taps = pl.BlockSpec((9, GROUP, OWN), lambda i: (0, 0, 0))
    grad_in, grad_out, block_out, grad_features, grad_conv = pl.pallas_call(
        lambda *refs: finish(scale, *refs),
        grid=(steps,),
        out_shape=[
            jax.ShapeDtypeStruct((CH, HID), F32),
            jax.ShapeDtypeStruct((HID, CH), F32),
            jax.ShapeDtypeStruct((ROWS, OWN, COLS), BF16),
            jax.ShapeDtypeStruct((ROWS, OWN, COLS), BF16),
            jax.ShapeDtypeStruct((9, GROUP, OWN), F32),
        ],
        in_specs=[
            pl.BlockSpec((CH // steps, HID), lambda i: (steps + i, 0)),
            halves,
            pl.BlockSpec((HID // steps, HID), lambda i: (steps + i, 0)),
            row, row, taps,
        ],
        out_specs=[
            pl.BlockSpec((CH // steps, HID), lambda i: (i, 0)),
            pl.BlockSpec((HID // steps, CH), lambda i: (i, 0)),
            row, row, taps,
        ],
        compiler_params=pltpu.CompilerParams(vmem_limit_bytes=60 << 20),
    )(grads, grads, grads, block_out, grad_features, grad_conv)
    return turned(block_out), turned(grad_features), grad_conv, grad_in, grad_out


def solution(mesh):
    return jax.shard_map(
        body,
        mesh=mesh,
        in_specs=(
            P("space", None, "chan"),
            P(None, None, "chan"),
            P(None, "chan"),
            P("chan", None),
            P("space", None, "chan"),
        ),
        out_specs=(
            P("space", None, "chan"),
            P("space", None, "chan"),
            P(None, None, "chan"),
            P(None, "chan"),
            P("chan", None),
        ),
        check_vma=False,
    )
```
